32 devices in a mesh: group: 4 (over x, core), inner: 8 (over z, y).
Axes of the slice: x: 2, y: 2, z: 4, core: 2. Of those that a mesh axis runs over, the one named last changes fastest.
Arguments:
- out_grad: bfloat16 [64, 3584], P(('group', 'inner')), may hold values from -6 to 6
- routing_weight: bfloat16 [64, 4], P(('group', 'inner')), may hold values from 0.099609375 to 1
- expert_ids: int32 [64, 4], P(('group', 'inner')), may hold values from 0 to 15, as said below
- slot_index: int32 [64, 4], P(('group', 'inner')), may hold values from 0 to 5, as said below
- w_gate: bfloat16 [3584, 4096], P(None, ('group', 'inner')), may hold values from -0.09375 to 0.09375
- w_up: bfloat16 [3584, 4096], P(None, ('group', 'inner')), may hold values from -0.09375 to 0.09375
- w_down: bfloat16 [4096, 3584], P(('group', 'inner')), may hold values from -0.375 to 0.375
- pre_act: bfloat16 [2, 24, 4096], P(None, None, ('group', 'inner')), may hold values from -5 to 5
Outputs:
- grad_tokens: bfloat16 [64, 3584], P(('group', 'inner'))
- grad_routing: float32 [64, 4], P(('group', 'inner'))
The draws below stay inside these ranges and needn't reach their ends.
Inputs may be any that keep to these rules, and one draw needn't show every extreme that they name: `expert_ids`: each token names 4 different experts, two in each of 2 different node groups (expert e lies in group e // 4). Among the 16 tokens of one index of group, every node group is named by exactly half of the tokens, and in every node group half of the experts are named by exactly 6 of these tokens and the other half by 2. slot_index[t, k] is the number of tokens before t, among the 16 tokens of the same index of group, that name expert expert_ids[t, k].
All inputs are finite; a program needn't handle non-finite values.
Results may differ from the reference program's by a relative error of at most 0.0075.
Values may be sent and summed in bfloat16 or wider, within the bound.
No kernel may reach another device: no remote copies, remote signals or barrier semaphores. Data moves between devices by JAX's collectives and lax.ppermute only.
A program may use at most 64 MiB of HBM per device.

```python
import math
import jax
import jax.numpy as jnp
from jax import lax

D = 3584
HID_DEV = 128
SPLIT = 2
FF = 256
EXP_GROUP = 4
EXPERTS = 16
TOPG = 2
TOPK = 4
BLOCK = 16
CAP = 6
TOKENS = 64
N_GROUP = 4


def block_route(key):
    key_pos, key_group, key_order = jax.random.split(key, 3)
    position = jax.random.permutation(key_pos, BLOCK).astype(jnp.int32)
    relabel = jax.random.permutation(key_group, N_GROUP).astype(jnp.int32)
    offsets = jnp.arange(TOPG, dtype=jnp.int32)
    chosen = relabel[(position[:, None] + offsets[None, :]) % N_GROUP]
    member = jnp.any(chosen[:, :, None] == jnp.arange(N_GROUP, dtype=jnp.int32)[None, None, :], axis=1).astype(jnp.int32)
    ranking = jnp.cumsum(member, axis=0) - member
    order_keys = jax.random.split(key_order, N_GROUP)
    orders = jax.vmap(lambda one_key: jax.random.permutation(one_key, EXP_GROUP).astype(jnp.int32))(order_keys)
    loads = jnp.where(jnp.arange(EXP_GROUP) < EXP_GROUP // 2, CAP, CAP // 3).astype(jnp.int32)
    listing = jax.vmap(lambda order_row: jnp.repeat(order_row, loads, total_repeat_length=BLOCK))(orders)
    rank_sel = jnp.take_along_axis(ranking, chosen, axis=1)
    first_pick = listing[chosen, rank_sel]
    second_pick = listing[chosen, rank_sel + BLOCK // 2]
    local_ids = jnp.stack([first_pick, second_pick], axis=-1).reshape(BLOCK, TOPK)
    group_ids = jnp.repeat(chosen, 2, axis=1)
    expert_table = (group_ids * EXP_GROUP + local_ids).astype(jnp.int32)
    hits = jnp.any(expert_table[:, :, None] == jnp.arange(EXPERTS, dtype=jnp.int32)[None, None, :], axis=1).astype(jnp.int32)
    before = jnp.cumsum(hits, axis=0) - hits
    slot_table = jnp.take_along_axis(before, expert_table, axis=1).astype(jnp.int32)
    return (expert_table, slot_table)


def routing_tables(key):
    block_keys = jax.random.split(key, N_GROUP)
    expert_table, slot_table = jax.vmap(block_route)(block_keys)
    return (expert_table.reshape(TOKENS, TOPK), slot_table.reshape(TOKENS, TOPK))


def draw_expert_ids(key, part):
    shared = routing_tables(key)
    return shared[0]


def draw_slot_index(key, part):
    shared = routing_tables(key)
    return shared[1]


def levels(rng, dims, cuts, smallest, high):
    gain, own = 1.0, jax.random.fold_in(rng, 6)
    for axis_at, parts in cuts:
        draws = jnp.exp(jax.random.uniform(jax.random.fold_in(own, axis_at), (parts,), jnp.float32, smallest / len(cuts), high / len(cuts)))
        gain = gain * jnp.repeat(draws, dims[axis_at] // parts).reshape([-1 if axis == axis_at else 1 for axis in range(len(dims))])
    return gain


def scatter_about(key, dims, spread, limit, cuts=(), kind=jnp.bfloat16):
    array = jax.random.normal(key, dims, jnp.float32) * spread
    if len(cuts) > 0:
        array = levels(key, dims, cuts, -0.22, 0.18) * array
    return jnp.clip(array, min=-limit, max=limit).astype(kind)


def setup_inputs(seed: int = 0) -> dict:
    streams_of = jax.random.split(jax.random.key(seed), 9)
    out_grad = scatter_about(streams_of[0], (TOKENS, D), 1.0, 6.0, ((0, 32),))
    routing_weight = jnp.clip(jnp.exp(math.log(1.0) - 2.306499 * jax.random.uniform(streams_of[1], (TOKENS, TOPK), jnp.float32) ** levels(streams_of[1], (TOKENS, TOPK), ((0, 32),), -0.2, 0.2)), 0.099609375, 1.0).astype(jnp.bfloat16)
    expert_ids = draw_expert_ids(jax.random.fold_in(streams_of[8], 71), 0)
    slot_index = draw_slot_index(jax.random.fold_in(streams_of[8], 71), 0)
    w_gate = scatter_about(streams_of[4], (D, EXPERTS * FF), D ** -0.5, 0.09375, ((1, 32),))
    w_up = scatter_about(streams_of[5], (D, EXPERTS * FF), D ** -0.5, 0.09375, ((1, 32),))
    w_down = scatter_about(streams_of[6], (EXPERTS * FF, D), FF ** -0.5, 0.375, ((0, 32),))
    pre_act = scatter_about(streams_of[7], (2, N_GROUP * CAP, EXPERTS * FF), 1.0, 5.0, ((2, 32),))
    return dict(out_grad=out_grad, routing_weight=routing_weight, expert_ids=expert_ids, slot_index=slot_index, w_gate=w_gate, w_up=w_up, w_down=w_down, pre_act=pre_act)


def expert_backward(token_rows, weight, gate_weight, up_weight, down_weight, saved_pre):
    highest = lax.Precision.HIGHEST
    slot_rows = token_rows.shape[0]
    back_proj = jnp.dot(token_rows, down_weight.T, preferred_element_type=jnp.float32)
    pre_gate = saved_pre[0].astype(jnp.float32)
    pre_up = saved_pre[1].astype(jnp.float32)
    gate_sig = jax.nn.sigmoid(pre_gate)
    swish_gate = pre_gate * gate_sig
    hidden = swish_gate * pre_up
    gate_blocks = jnp.sum((hidden * back_proj).reshape(slot_rows, SPLIT, HID_DEV), axis=2).astype(jnp.bfloat16)
    gate_blocks = lax.optimization_barrier(gate_blocks)
    gate_term = jnp.sum(gate_blocks.astype(jnp.float32), axis=1)
    scaled = weight[:, None] * back_proj
    grad_up = (scaled * swish_gate).astype(jnp.bfloat16)
    grad_gate = (scaled * pre_up * gate_sig * (1.0 + pre_gate * (1.0 - gate_sig))).astype(jnp.bfloat16)
    gate_split = grad_gate.astype(jnp.float32).reshape(slot_rows, SPLIT, HID_DEV)
    up_split = grad_up.astype(jnp.float32).reshape(slot_rows, SPLIT, HID_DEV)
    gate_w_split = gate_weight.astype(jnp.float32).reshape(D, SPLIT, HID_DEV)
    up_w_split = up_weight.astype(jnp.float32).reshape(D, SPLIT, HID_DEV)
    pieces = jnp.einsum("sjh,djh->jsd", gate_split, gate_w_split, precision=highest)
    pieces = pieces + jnp.einsum("sjh,djh->jsd", up_split, up_w_split, precision=highest)
    pieces = lax.optimization_barrier(pieces.astype(jnp.bfloat16))
    partial_value = jnp.sum(pieces.astype(jnp.float32), axis=0)
    return partial_value, gate_term


def reference(out_grad, routing_weight, expert_ids, slot_index, w_gate, w_up, w_down, pre_act):
    slots_per = N_GROUP * CAP
    slot_total = EXPERTS * slots_per
    source = (jnp.arange(TOKENS, dtype=jnp.int32) // BLOCK)[:, None]
    position = expert_ids * slots_per + source * CAP + slot_index
    flat_pos = position.reshape(-1)
    repeated = jnp.repeat(out_grad, TOPK, axis=0)
    buffer_rows = jnp.zeros((slot_total, D), jnp.bfloat16).at[flat_pos].set(repeated)
    buffer_weight = jnp.zeros((slot_total,), jnp.float32).at[flat_pos].set(routing_weight.reshape(-1).astype(jnp.float32))

    def one_expert(expert):
        first_row = expert * slots_per
        token_rows = lax.dynamic_slice_in_dim(buffer_rows, first_row, slots_per, 0)
        weight = lax.dynamic_slice_in_dim(buffer_weight, first_row, slots_per, 0)
        column = expert * FF
        gate_weight = lax.dynamic_slice_in_dim(w_gate, column, FF, 1)
        up_weight = lax.dynamic_slice_in_dim(w_up, column, FF, 1)
        down_weight = lax.dynamic_slice_in_dim(w_down, column, FF, 0)
        saved_pre = lax.dynamic_slice_in_dim(pre_act, column, FF, 2)
        return expert_backward(token_rows, weight, gate_weight, up_weight, down_weight, saved_pre)

    partials, gate_terms = lax.map(one_expert, jnp.arange(EXPERTS, dtype=jnp.int32))
    partials = partials.reshape(slot_total, D)
    gate_terms = gate_terms.reshape(slot_total)
    grad_rows = jnp.sum(partials[position], axis=1)
    grad_gate = gate_terms[position]
    return grad_rows.astype(jnp.bfloat16), grad_gate
```

```python
import jax
import jax.numpy as jnp
from jax import lax
from jax.sharding import PartitionSpec as P

LANES = 128
AXES = ("group", "inner")


def exchange(array, axis):
    return lax.all_to_all(array, axis, split_axis=0, concat_axis=0, tiled=True)


def pack(rows, *small):
    width = sum(s.shape[-1] for s in small)
    pad = -width % LANES
    parts = [rows] + [s.astype(rows.dtype) for s in small]
    if pad:
        parts.append(jnp.zeros(rows.shape[:-1] + (pad,), rows.dtype))
    return jnp.concatenate(parts, axis=-1)


def gradients(back_proj, weight, pre_gate, pre_up):
    gate_sig = jax.nn.sigmoid(pre_gate)
    swish_gate = pre_gate * gate_sig
    gate_piece = jnp.sum(swish_gate * pre_up * back_proj, axis=1, keepdims=True)
    scaled = weight * back_proj
    grad_up = (scaled * swish_gate).astype(jnp.bfloat16)
    grad_gate = (scaled * pre_up * gate_sig * (1.0 + pre_gate * (1.0 - gate_sig))).astype(
        jnp.bfloat16
    )
    return grad_gate, grad_up, gate_piece


def across(a, b):
    return lax.dot_general(a, b, (((1,), (1,)), ((), ())), preferred_element_type=jnp.float32)


def flat(out_grad, routing_weight, expert_ids, slot_index, w_gate, w_up, w_down, pre_act):
    group_count = lax.axis_size("group")
    inner_count = lax.axis_size("inner")
    devices = group_count * inner_count
    own, width = out_grad.shape
    topk = expert_ids.shape[1]
    split_count = min(8, inner_count // 4)
    experts_here = inner_count // split_count
    tokens = devices * own
    slots = pre_act.shape[1]
    capacity = slots // group_count
    expert = lax.axis_index("group") * experts_here + lax.axis_index("inner") // split_count

    payload = pack(out_grad, expert_ids, slot_index, routing_weight)
    sent = jnp.broadcast_to(payload[None], (devices,) + payload.shape)
    arrived = exchange(sent, AXES).reshape(tokens, payload.shape[1])
    rows = arrived[:, :width]
    small = arrived[:, width : width + 3 * topk].astype(jnp.float32)
    mine = (small[:, :topk] == expert.astype(jnp.float32)).astype(jnp.float32)
    slot = jnp.sum(mine * small[:, topk : 2 * topk], axis=1)
    weight = jnp.sum(mine * small[:, 2 * topk :], axis=1, keepdims=True)
    chosen = jnp.sum(mine, axis=1)
    source = jnp.arange(tokens, dtype=jnp.int32) // (inner_count * own)
    place = source * capacity + slot.astype(jnp.int32)
    one_hot = jnp.logical_and(
        place[:, None] == jnp.arange(slots, dtype=jnp.int32)[None, :], chosen[:, None] > 0.5
    ).astype(jnp.bfloat16)
    pre_gate = jnp.dot(one_hot, pre_act[0], preferred_element_type=jnp.float32)
    pre_up = jnp.dot(one_hot, pre_act[1], preferred_element_type=jnp.float32)
    back_proj = across(rows, w_down)
    grad_gate, grad_up, gate_piece = gradients(back_proj, weight, pre_gate, pre_up)
    pieces = (across(grad_gate, w_gate) + across(grad_up, w_up)).astype(jnp.bfloat16)
    back = pack(pieces, mine * gate_piece).reshape(devices, own, -1)
    total = jnp.sum(exchange(back, AXES).astype(jnp.float32), axis=0)
    return total[:, :width].astype(jnp.bfloat16), total[:, width : width + topk]


def staged(out_grad, routing_weight, expert_ids, slot_index, w_gate, w_up, w_down, pre_act):
    group_count = lax.axis_size("group")
    inner_count = lax.axis_size("inner")
    own, width = out_grad.shape
    topk = expert_ids.shape[1]
    split_count = min(8, inner_count // 4)
    experts_here = inner_count // split_count
    local_expert = lax.axis_index("inner") // split_count
    block = inner_count * own
    slots = pre_act.shape[1]
    capacity = slots // group_count
    high = -(-(capacity + 1) // 8) * 8

    payload = pack(out_grad, expert_ids, slot_index, routing_weight)
    sent = jnp.broadcast_to(payload[None], (inner_count,) + payload.shape)
    arrived = exchange(sent, "inner").reshape(block, payload.shape[1])
    rows = arrived[:, :width]
    small = arrived[:, width : width + 3 * topk].astype(jnp.float32)
    ids = small[:, :topk].astype(jnp.int32)
    slot = small[:, topk : 2 * topk].astype(jnp.int32)
    weight = small[:, 2 * topk :]
    selected = ids % experts_here == local_expert
    column = ids // experts_here * high + slot
    one_hot = jnp.logical_and(
        column[:, :, None] == jnp.arange(group_count * high, dtype=jnp.int32), selected[:, :, None]
    ).astype(jnp.float32)
    placement = jnp.sum(one_hot, axis=1).astype(jnp.bfloat16)
    send_weight = jnp.sum(one_hot * weight[:, :, None], axis=(0, 1)).reshape(group_count, 1, high)
    send_rows = lax.dot_general(
        placement, rows, (((0,), (0,)), ((), ())), preferred_element_type=jnp.float32
    ).reshape(group_count, high, width)
    last = jnp.arange(high) == high - 1
    weight_row = jnp.pad(send_weight, ((0, 0), (0, 0), (0, width - high)))
    send = jnp.where(last[None, :, None], weight_row, send_rows).astype(jnp.bfloat16)
    buffer = exchange(send, "group")

    buffer_weight = buffer[:, high - 1, :capacity].astype(jnp.float32).reshape(slots, 1)
    buffer_rows = buffer[:, :capacity].reshape(slots, width)
    back_proj = across(buffer_rows, w_down)
    grad_gate, grad_up, gate_piece = gradients(
        back_proj, buffer_weight, pre_act[0].astype(jnp.float32), pre_act[1].astype(jnp.float32)
    )
    pieces = (across(grad_gate, w_gate) + across(grad_up, w_up)).reshape(group_count, capacity, width)
    gate_row = jnp.pad(
        gate_piece.reshape(group_count, 1, capacity), ((0, 0), (0, 0), (0, width - capacity))
    )
    pieces = jnp.pad(pieces, ((0, 0), (0, high - capacity), (0, 0)))
    back = exchange(jnp.where(last[None, :, None], gate_row, pieces).astype(jnp.bfloat16), "group")

    owned = jnp.dot(
        placement, back.reshape(group_count * high, width), preferred_element_type=jnp.float32
    ).astype(jnp.bfloat16)
    gates = back[:, high - 1, :high].reshape(group_count * high).astype(jnp.float32)
    gate_rows = jnp.sum(one_hot * gates, axis=2)
    final = exchange(pack(owned, gate_rows).reshape(inner_count, own, -1), "inner")
    total = jnp.sum(final.astype(jnp.float32), axis=0)
    return total[:, :width].astype(jnp.bfloat16), total[:, width : width + topk]


def solution(mesh):
    in_specs = (
        P(AXES, None),
        P(AXES, None),
        P(AXES, None),
        P(AXES, None),
        P(None, AXES),
        P(None, AXES),
        P(AXES, None),
        P(None, None, AXES),
    )
    out_specs = (P(AXES, None), P(AXES, None))
    on_device = flat if mesh.size <= 64 else staged
    return jax.shard_map(
        on_device, mesh=mesh, in_specs=in_specs, out_specs=out_specs, check_vma=False
    )
```

```python
import jax
import jax.numpy as jnp
from jax import lax
from jax.sharding import PartitionSpec as P

LANES = 128
AXES = ("group", "inner")


def exchange(array, axis):
    return lax.all_to_all(array, axis, split_axis=0, concat_axis=0, tiled=True)


def pack(rows, *small):
    width = sum(s.shape[-1] for s in small)
    pad = -width % LANES
    parts = [rows] + [s.astype(rows.dtype) for s in small]
    if pad:
        parts.append(jnp.zeros(rows.shape[:-1] + (pad,), rows.dtype))
    return jnp.concatenate(parts, axis=-1)


def gradients(back_proj, weight, pre_gate, pre_up):
    gate_sig = jax.nn.sigmoid(pre_gate)
    swish_gate = pre_gate * gate_sig
    gate_piece = jnp.sum(swish_gate * pre_up * back_proj, axis=1, keepdims=True)
    scaled = weight * back_proj
    grad_up = (scaled * swish_gate).astype(jnp.bfloat16)
    grad_gate = (scaled * pre_up * gate_sig * (1.0 + pre_gate * (1.0 - gate_sig))).astype(
        jnp.bfloat16
    )
    return grad_gate, grad_up, gate_piece


def across(a, b):
    return lax.dot_general(a, b, (((1,), (1,)), ((), ())), preferred_element_type=jnp.float32)


def staged(out_grad, routing_weight, expert_ids, slot_index, w_gate, w_up, w_down, pre_act):
    group_count = lax.axis_size("group")
    inner_count = lax.axis_size("inner")
    own, width = out_grad.shape
    topk = expert_ids.shape[1]
    split_count = min(8, inner_count // 4)
    experts_here = inner_count // split_count
    local_expert = lax.axis_index("inner") // split_count
    block = inner_count * own
    slots = pre_act.shape[1]
    capacity = slots // group_count
    high = -(-(capacity + 1) // 8) * 8

    payload = pack(out_grad, expert_ids, slot_index, routing_weight)
    sent = jnp.broadcast_to(payload[None], (inner_count,) + payload.shape)
    arrived = exchange(sent, "inner").reshape(block, payload.shape[1])
    rows = arrived[:, :width]
    small = arrived[:, width : width + 3 * topk].astype(jnp.float32)
    ids = small[:, :topk].astype(jnp.int32)
    slot = small[:, topk : 2 * topk].astype(jnp.int32)
    weight = small[:, 2 * topk :]
    selected = ids % experts_here == local_expert
    column = ids // experts_here * high + slot
    one_hot = jnp.logical_and(
        column[:, :, None] == jnp.arange(group_count * high, dtype=jnp.int32), selected[:, :, None]
    ).astype(jnp.float32)
    placement = jnp.sum(one_hot, axis=1).astype(jnp.bfloat16)
    send_weight = jnp.sum(one_hot * weight[:, :, None], axis=(0, 1)).reshape(group_count, 1, high)
    send_rows = lax.dot_general(
        placement, rows, (((0,), (0,)), ((), ())), preferred_element_type=jnp.float32
    ).reshape(group_count, high, width)
    last = jnp.arange(high) == high - 1
    weight_row = jnp.pad(send_weight, ((0, 0), (0, 0), (0, width - high)))
    send = jnp.where(last[None, :, None], weight_row, send_rows).astype(jnp.bfloat16)
    buffer = exchange(send, "group")

    buffer_weight = buffer[:, high - 1, :capacity].astype(jnp.float32).reshape(slots, 1)
    buffer_rows = buffer[:, :capacity].reshape(slots, width)
    back_proj = across(buffer_rows, w_down)
    grad_gate, grad_up, gate_piece = gradients(
        back_proj, buffer_weight, pre_act[0].astype(jnp.float32), pre_act[1].astype(jnp.float32)
    )
    pieces = (across(grad_gate, w_gate) + across(grad_up, w_up)).reshape(group_count, capacity, width)
    gate_row = jnp.pad(
        gate_piece.reshape(group_count, 1, capacity), ((0, 0), (0, 0), (0, width - capacity))
    )
    pieces = jnp.pad(pieces, ((0, 0), (0, high - capacity), (0, 0)))
    back = exchange(jnp.where(last[None, :, None], gate_row, pieces).astype(jnp.bfloat16), "group")

    owned = jnp.dot(
        placement, back.reshape(group_count * high, width), preferred_element_type=jnp.float32
    ).astype(jnp.bfloat16)
    gates = back[:, high - 1, :high].reshape(group_count * high).astype(jnp.float32)
    gate_rows = jnp.sum(one_hot * gates, axis=2)
    final = exchange(pack(owned, gate_rows).reshape(inner_count, own, -1), "inner")
    total = jnp.sum(final.astype(jnp.float32), axis=0)
    return total[:, :width].astype(jnp.bfloat16), total[:, width : width + topk]


def solution(mesh):
    in_specs = (
        P(AXES, None),
        P(AXES, None),
        P(AXES, None),
        P(AXES, None),
        P(None, AXES),
        P(None, AXES),
        P(AXES, None),
        P(None, None, AXES),
    )
    out_specs = (P(AXES, None), P(AXES, None))
    on_device = staged
    return jax.shard_map(
        on_device, mesh=mesh, in_specs=in_specs, out_specs=out_specs, check_vma=False
    )
```

```python
import jax
import jax.numpy as jnp
from jax import lax
from jax.sharding import PartitionSpec as P

LANES = 128
AXES = ("group", "inner")


def pairwise(axis):
    count = lax.axis_size(axis)
    return count <= 8 and count & (count - 1) == 0


def place(axis, index):
    return index ^ lax.axis_index(axis) if pairwise(axis) else index


def exchange(array, axis):
    if not pairwise(axis):
        return lax.all_to_all(array, axis, split_axis=0, concat_axis=0, tiled=True)
    count = lax.axis_size(axis)
    arrived = [array[0]] + [
        lax.ppermute(array[r], axis, [(i, i ^ r) for i in range(count)]) for r in range(1, count)
    ]
    return jnp.stack(arrived)


def pack(rows, *small):
    width = sum(s.shape[-1] for s in small)
    pad = -width % LANES
    parts = [rows] + [s.astype(rows.dtype) for s in small]
    if pad:
        parts.append(jnp.zeros(rows.shape[:-1] + (pad,), rows.dtype))
    return jnp.concatenate(parts, axis=-1)


def gradients(back_proj, weight, pre_gate, pre_up):
    gate_sig = jax.nn.sigmoid(pre_gate)
    swish_gate = pre_gate * gate_sig
    gate_piece = jnp.sum(swish_gate * pre_up * back_proj, axis=1, keepdims=True)
    scaled = weight * back_proj
    grad_up = (scaled * swish_gate).astype(jnp.bfloat16)
    grad_gate = (scaled * pre_up * gate_sig * (1.0 + pre_gate * (1.0 - gate_sig))).astype(
        jnp.bfloat16
    )
    return grad_gate, grad_up, gate_piece


def across(a, b):
    return lax.dot_general(a, b, (((1,), (1,)), ((), ())), preferred_element_type=jnp.float32)


def on_device(out_grad, routing_weight, expert_ids, slot_index, w_gate, w_up, w_down, pre_act):
    group_count = lax.axis_size("group")
    inner_count = lax.axis_size("inner")
    own, width = out_grad.shape
    topk = expert_ids.shape[1]
    split_count = min(8, inner_count // 4)
    experts_here = inner_count // split_count
    local_expert = lax.axis_index("inner") // split_count
    slots = pre_act.shape[1]
    capacity = slots // group_count
    high = -(-(capacity + 1) // 8) * 8
    partners = place("group", jnp.arange(group_count, dtype=jnp.int32))

    saved = pre_act.reshape(2, group_count, capacity, -1)
    saved = jnp.take(saved, partners, axis=1).reshape(2, slots, -1).astype(jnp.float32)

    payload = pack(out_grad, expert_ids, slot_index, routing_weight)
    arrived = exchange(jnp.broadcast_to(payload[None], (inner_count,) + payload.shape), "inner")
    arrived = arrived.reshape(inner_count * own, -1)
    rows = arrived[:, :width]
    small = arrived[:, width : width + 3 * topk].astype(jnp.float32)
    ids = small[:, :topk].astype(jnp.int32)
    slot = small[:, topk : 2 * topk].astype(jnp.int32)
    weight = small[:, 2 * topk :]
    selected = ids % experts_here == local_expert
    column = place("group", ids // experts_here) * high + slot
    one_hot = jnp.logical_and(
        column[:, :, None] == jnp.arange(group_count * high, dtype=jnp.int32), selected[:, :, None]
    ).astype(jnp.float32)
    placement = jnp.sum(one_hot, axis=1).astype(jnp.bfloat16)
    send_weight = jnp.sum(one_hot * weight[:, :, None], axis=(0, 1)).reshape(group_count, 1, high)
    send_rows = lax.dot_general(
        placement, rows, (((0,), (0,)), ((), ())), preferred_element_type=jnp.float32
    ).reshape(group_count, high, width)
    last = jnp.arange(high) == high - 1
    weight_row = jnp.pad(send_weight, ((0, 0), (0, 0), (0, width - high)))
    send = jnp.where(last[None, :, None], weight_row, send_rows).astype(jnp.bfloat16)
    buffer = exchange(send, "group")

    buffer_weight = buffer[:, high - 1, :capacity].astype(jnp.float32).reshape(slots, 1)
    buffer_rows = buffer[:, :capacity].reshape(slots, width)
    back_proj = across(buffer_rows, w_down)
    grad_gate, grad_up, gate_piece = gradients(back_proj, buffer_weight, saved[0], saved[1])
    pieces = (across(grad_gate, w_gate) + across(grad_up, w_up)).reshape(group_count, capacity, width)
    gate_row = jnp.pad(
        gate_piece.reshape(group_count, 1, capacity), ((0, 0), (0, 0), (0, width - capacity))
    )
    pieces = jnp.pad(pieces, ((0, 0), (0, high - capacity), (0, 0)))
    pieces = jnp.where(last[None, :, None], gate_row, pieces).astype(jnp.bfloat16)
    back = exchange(pieces, "group")

    owned = jnp.dot(
        placement, back.reshape(group_count * high, width), preferred_element_type=jnp.float32
    ).astype(jnp.bfloat16)
    gates = back[:, high - 1, :high].reshape(group_count * high).astype(jnp.float32)
    gate_rows = jnp.sum(one_hot * gates, axis=2)
    final = pack(owned, gate_rows).reshape(inner_count, own, -1)
    total = jnp.sum(exchange(final, "inner").astype(jnp.float32), axis=0)
    return total[:, :width].astype(jnp.bfloat16), total[:, width : width + topk]


def solution(mesh):
    in_specs = (
        P(AXES, None),
        P(AXES, None),
        P(AXES, None),
        P(AXES, None),
        P(None, AXES),
        P(None, AXES),
        P(AXES, None),
        P(None, None, AXES),
    )
    out_specs = (P(AXES, None), P(AXES, None))
    return jax.shard_map(
        on_device, mesh=mesh, in_specs=in_specs, out_specs=out_specs, check_vma=False
    )
```

```python
import jax
import jax.numpy as jnp
from jax import lax
from jax.sharding import Mesh, PartitionSpec as P

LANES = 128
CORES = 2


def exchange(array, axis):
    return lax.all_to_all(array, axis, split_axis=0, concat_axis=0, tiled=True)


def pack(rows, *small):
    width = sum(s.shape[-1] for s in small)
    pad = -width % LANES
    parts = [rows] + [s.astype(rows.dtype) for s in small]
    if pad:
        parts.append(jnp.zeros(rows.shape[:-1] + (pad,), rows.dtype))
    return jnp.concatenate(parts, axis=-1)


def gradients(back_proj, weight, pre_gate, pre_up):
    gate_sig = jax.nn.sigmoid(pre_gate)
    swish_gate = pre_gate * gate_sig
    gate_piece = jnp.sum(swish_gate * pre_up * back_proj, axis=1, keepdims=True)
    scaled = weight * back_proj
    grad_up = (scaled * swish_gate).astype(jnp.bfloat16)
    grad_gate = (scaled * pre_up * gate_sig * (1.0 + pre_gate * (1.0 - gate_sig))).astype(
        jnp.bfloat16
    )
    return grad_gate, grad_up, gate_piece


def across(a, b):
    return lax.dot_general(a, b, (((1,), (1,)), ((), ())), preferred_element_type=jnp.float32)


def sizes(group_count, inner_count):
    split_count = min(8, inner_count // 4)
    return split_count, inner_count // split_count


def flat(out_grad, routing_weight, expert_ids, slot_index, w_gate, w_up, w_down, pre_act):
    row_count = lax.axis_size("row")
    inner_count = lax.axis_size("inner")
    group_count = row_count * CORES
    core = lax.axis_index("core")
    split_count, experts_here = sizes(group_count, inner_count)
    own, width = out_grad.shape
    topk = expert_ids.shape[1]
    peers = row_count * inner_count
    half = peers * own
    slots = pre_act.shape[1]
    capacity = slots // group_count
    expert = (lax.axis_index("row") * CORES + core) * experts_here
    expert = expert + lax.axis_index("inner") // split_count
    other_core = [(0, 1), (1, 0)]

    payload = pack(out_grad, expert_ids, slot_index, routing_weight)
    sent = jnp.broadcast_to(payload[None], (peers,) + payload.shape)
    near = exchange(sent, ("row", "inner")).reshape(half, -1)
    arrived = jnp.concatenate([near, lax.ppermute(near, "core", other_core)], axis=0)
    rows = arrived[:, :width]
    small = arrived[:, width : width + 3 * topk].astype(jnp.float32)
    mine = (small[:, :topk] == expert.astype(jnp.float32)).astype(jnp.float32)
    slot = jnp.sum(mine * small[:, topk : 2 * topk], axis=1)
    weight = jnp.sum(mine * small[:, 2 * topk :], axis=1, keepdims=True)
    chosen = jnp.sum(mine, axis=1)
    index = jnp.arange(CORES * half, dtype=jnp.int32)
    source = index % half // (inner_count * own) * CORES + (index // half ^ core)
    place = source * capacity + slot.astype(jnp.int32)
    one_hot = jnp.logical_and(
        place[:, None] == jnp.arange(slots, dtype=jnp.int32)[None, :], chosen[:, None] > 0.5
    ).astype(jnp.bfloat16)
    pre_gate = jnp.dot(one_hot, pre_act[0], preferred_element_type=jnp.float32)
    pre_up = jnp.dot(one_hot, pre_act[1], preferred_element_type=jnp.float32)
    back_proj = across(rows, w_down)
    grad_gate, grad_up, gate_piece = gradients(back_proj, weight, pre_gate, pre_up)
    pieces = (across(grad_gate, w_gate) + across(grad_up, w_up)).astype(jnp.bfloat16)
    back = pack(pieces, mine * gate_piece)
    added = lax.ppermute(back[half:], "core", other_core).astype(jnp.float32)
    added = (back[:half].astype(jnp.float32) + added).astype(jnp.bfloat16)
    total = exchange(added.reshape(peers, own, -1), ("row", "inner"))
    total = jnp.sum(total.astype(jnp.float32), axis=0)
    return total[:, :width].astype(jnp.bfloat16), total[:, width : width + topk]


def staged(out_grad, routing_weight, expert_ids, slot_index, w_gate, w_up, w_down, pre_act):
    group_count = lax.axis_size("group")
    inner_count = lax.axis_size("inner")
    own, width = out_grad.shape
    topk = expert_ids.shape[1]
    split_count, experts_here = sizes(group_count, inner_count)
    local_expert = lax.axis_index("inner") // split_count
    block = inner_count * own
    slots = pre_act.shape[1]
    capacity = slots // group_count
    high = -(-(capacity + 1) // 8) * 8

    payload = pack(out_grad, expert_ids, slot_index, routing_weight)
    sent = jnp.broadcast_to(payload[None], (inner_count,) + payload.shape)
    arrived = exchange(sent, "inner").reshape(block, payload.shape[1])
    rows = arrived[:, :width]
    small = arrived[:, width : width + 3 * topk].astype(jnp.float32)
    ids = small[:, :topk].astype(jnp.int32)
    slot = small[:, topk : 2 * topk].astype(jnp.int32)
    weight = small[:, 2 * topk :]
    selected = ids % experts_here == local_expert
    column = ids // experts_here * high + slot
    one_hot = jnp.logical_and(
        column[:, :, None] == jnp.arange(group_count * high, dtype=jnp.int32), selected[:, :, None]
    ).astype(jnp.float32)
    placement = jnp.sum(one_hot, axis=1).astype(jnp.bfloat16)
    send_weight = jnp.sum(one_hot * weight[:, :, None], axis=(0, 1)).reshape(group_count, 1, high)
    send_rows = lax.dot_general(
        placement, rows, (((0,), (0,)), ((), ())), preferred_element_type=jnp.float32
    ).reshape(group_count, high, width)
    last = jnp.arange(high) == high - 1
    weight_row = jnp.pad(send_weight, ((0, 0), (0, 0), (0, width - high)))
    send = jnp.where(last[None, :, None], weight_row, send_rows).astype(jnp.bfloat16)
    buffer = exchange(send, "group")

    buffer_weight = buffer[:, high - 1, :capacity].astype(jnp.float32).reshape(slots, 1)
    buffer_rows = buffer[:, :capacity].reshape(slots, width)
    back_proj = across(buffer_rows, w_down)
    grad_gate, grad_up, gate_piece = gradients(
        back_proj, buffer_weight, pre_act[0].astype(jnp.float32), pre_act[1].astype(jnp.float32)
    )
    pieces = (across(grad_gate, w_gate) + across(grad_up, w_up)).reshape(group_count, capacity, width)
    gate_row = jnp.pad(
        gate_piece.reshape(group_count, 1, capacity), ((0, 0), (0, 0), (0, width - capacity))
    )
    pieces = jnp.pad(pieces, ((0, 0), (0, high - capacity), (0, 0)))
    back = exchange(jnp.where(last[None, :, None], gate_row, pieces).astype(jnp.bfloat16), "group")

    owned = jnp.dot(
        placement, back.reshape(group_count * high, width), preferred_element_type=jnp.float32
    ).astype(jnp.bfloat16)
    gates = back[:, high - 1, :high].reshape(group_count * high).astype(jnp.float32)
    gate_rows = jnp.sum(one_hot * gates, axis=2)
    final = exchange(pack(owned, gate_rows).reshape(inner_count, own, -1), "inner")
    total = jnp.sum(final.astype(jnp.float32), axis=0)
    return total[:, :width].astype(jnp.bfloat16), total[:, width : width + topk]


def solution(mesh):
    if mesh.size <= 64:
        group_count, inner_count = mesh.devices.shape
        devices = mesh.devices.reshape(group_count // CORES, CORES, inner_count)
        mesh, axes, on_device = Mesh(devices, ("row", "core", "inner")), ("row", "core", "inner"), flat
    else:
        axes, on_device = ("group", "inner"), staged
    token, hidden = P(axes, None), P(None, axes)
    return jax.shard_map(
        on_device,
        mesh=mesh,
        in_specs=(token, token, token, token, hidden, hidden, token, P(None, None, axes)),
        out_specs=(token, token),
        check_vma=False,
    )
```

```python
import functools

import jax
import jax.numpy as jnp
from jax import lax
from jax.experimental import pallas as pl
from jax.experimental.pallas import tpu as pltpu
from jax.sharding import Mesh, PartitionSpec as P

LANES = 128
CORES = 2


def exchange(array, axis):
    return lax.all_to_all(array, axis, split_axis=0, concat_axis=0, tiled=True)


def pack(rows, *small):
    width = sum(s.shape[-1] for s in small)
    pad = -width % LANES
    parts = [rows] + [s.astype(rows.dtype) for s in small]
    if pad:
        parts.append(jnp.zeros(rows.shape[:-1] + (pad,), rows.dtype))
    return jnp.concatenate(parts, axis=-1)


def gradients(back_proj, weight, pre_gate, pre_up):
    gate_sig = jax.nn.sigmoid(pre_gate)
    swish_gate = pre_gate * gate_sig
    gate_piece = jnp.sum(swish_gate * pre_up * back_proj, axis=1, keepdims=True)
    scaled = weight * back_proj
    grad_up = (scaled * swish_gate).astype(jnp.bfloat16)
    grad_gate = (scaled * pre_up * gate_sig * (1.0 + pre_gate * (1.0 - gate_sig))).astype(
        jnp.bfloat16
    )
    return grad_gate, grad_up, gate_piece


def across(a, b):
    return lax.dot_general(a, b, (((1,), (1,)), ((), ())), preferred_element_type=jnp.float32)


def sizes(group_count, inner_count):
    split_count = min(8, inner_count // 4)
    return split_count, inner_count // split_count


def pack_kernel(out_grad, ids, slots, weights, sent, rows, words, reals, small, sems):
    width = out_grad.shape[1]
    topk = ids.shape[1]
    copies = [
        pltpu.make_async_copy(source, target, sems.at[at])
        for at, (source, target) in enumerate(
            ((ids, words.at[0]), (slots, words.at[1]), (weights, reals), (out_grad, rows))
        )
    ]
    for copy in copies:
        copy.start()
    small[...] = jnp.zeros_like(small)
    for copy in copies:
        copy.wait()
    for at, part in enumerate((words[0], words[1], reals[...])):
        small[:, at * topk : (at + 1) * topk] = part.astype(jnp.float32)
    tail = small[...].astype(sent.dtype)
    own_rows = rows[...]
    for peer in range(sent.shape[0]):
        sent[peer, :, :width] = own_rows
        sent[peer, :, width:] = tail


def load_kernel(count, *refs):
    sources, targets, sems = refs[:count], refs[count : 2 * count], refs[2 * count]
    copies = [
        pltpu.make_async_copy(source, target, sems.at[at])
        for at, (source, target) in enumerate(zip(sources, targets))
    ]
    for copy in copies:
        copy.start()
    for copy in copies:
        copy.wait()


def expert_kernel(topk, capacity, is_far, arrived, w_gate, w_up, w_down, pre_act, out):
    half, packed = arrived.shape
    width = w_gate.shape[0]
    slots = pre_act.shape[1]
    row_count = lax.axis_size("row")
    split_count, experts_here = sizes(row_count * CORES, lax.axis_size("inner"))
    core = lax.axis_index("core")
    expert = (lax.axis_index("row") * CORES + core) * experts_here
    expert = expert + lax.axis_index("inner") // split_count
    small = arrived[:, width:].astype(jnp.float32)
    lane = lax.broadcasted_iota(jnp.int32, small.shape, 1)
    mine = jnp.where(
        jnp.logical_and(small == expert.astype(jnp.float32), lane < topk), 1.0, 0.0
    )
    slot = jnp.sum(pltpu.roll(mine, topk, 1) * small, axis=1, keepdims=True)
    weight = jnp.sum(pltpu.roll(mine, 2 * topk, 1) * small, axis=1, keepdims=True)
    chosen = jnp.sum(mine, axis=1, keepdims=True)
    row = lax.broadcasted_iota(jnp.int32, (half, slots), 0) // (half // row_count)
    source = row * CORES + (1 - core if is_far else core)
    place = source * capacity + slot.astype(jnp.int32)
    column = lax.broadcasted_iota(jnp.int32, (half, slots), 1)
    one_hot = jnp.where(jnp.logical_and(place == column, chosen > 0.5), 1.0, 0.0)
    one_hot = one_hot.astype(jnp.bfloat16)
    pre_gate = jnp.dot(one_hot, pre_act[0], preferred_element_type=jnp.float32)
    pre_up = jnp.dot(one_hot, pre_act[1], preferred_element_type=jnp.float32)
    back_proj = across(arrived[:, :width], w_down[...])
    grad_gate, grad_up, gate_piece = gradients(back_proj, weight, pre_gate, pre_up)
    step = 512 if width % 512 == 0 else LANES
    for at in range(0, width, step):
        cols = slice(at, at + step)
        pieces = across(grad_gate, w_gate[cols]) + across(grad_up, w_up[cols])
        out[:, cols] = pieces.astype(out.dtype)
    out[:, width:] = (mine * gate_piece).astype(out.dtype)


def final_kernel(pieces, grad_rows, grad_gate):
    total = pieces[0].astype(jnp.float32)
    for peer in range(1, pieces.shape[0]):
        total = total + pieces[peer].astype(jnp.float32)
    width, topk = grad_rows.shape[1], grad_gate.shape[1]
    grad_rows[...] = total[:, :width].astype(grad_rows.dtype)
    grad_gate[...] = total[:, width : width + topk]


def stay_in_hbm(*arrays):
    return [pltpu.with_memory_space_constraint(a, pltpu.HBM) for a in arrays]


def flat(out_grad, routing_weight, expert_ids, slot_index, w_gate, w_up, w_down, pre_act):
    row_count = lax.axis_size("row")
    inner_count = lax.axis_size("inner")
    own, width = out_grad.shape
    topk = expert_ids.shape[1]
    peers = row_count * inner_count
    half = peers * own
    capacity = pre_act.shape[1] // (row_count * CORES)
    packed = width + LANES
    other_core = [(0, 1), (1, 0)]
    in_vmem = pl.BlockSpec(memory_space=pltpu.VMEM)
    in_hbm = pl.BlockSpec(memory_space=pltpu.HBM)

    sent = pl.pallas_call(
        pack_kernel,
        out_shape=jax.ShapeDtypeStruct((peers, own, packed), out_grad.dtype),
        in_specs=[in_hbm] * 4,
        out_specs=in_vmem,
        scratch_shapes=[
            pltpu.VMEM((own, width), out_grad.dtype),
            pltpu.VMEM((2, own, topk), expert_ids.dtype),
            pltpu.VMEM((own, topk), routing_weight.dtype),
            pltpu.VMEM((own, LANES), jnp.float32),
            pltpu.SemaphoreType.DMA((4,)),
        ],
        name="pack_rows",
    )(*stay_in_hbm(out_grad, expert_ids, slot_index, routing_weight))
    tensors = (w_gate, w_up, w_down, pre_act)
    loaded = pl.pallas_call(
        functools.partial(load_kernel, len(tensors)),
        out_shape=[pltpu.VMEM(t.shape, t.dtype) for t in tensors],
        in_specs=[in_hbm] * len(tensors),
        out_specs=[in_vmem] * len(tensors),
        scratch_shapes=[pltpu.SemaphoreType.DMA((len(tensors),))],
        cost_estimate=pl.CostEstimate(
            flops=0, bytes_accessed=2 * sum(t.nbytes for t in tensors), transcendentals=0
        ),
        name="load_weights",
    )(*stay_in_hbm(*tensors))

    def pieces(is_far, arrived):
        return pl.pallas_call(
            functools.partial(expert_kernel, topk, capacity, is_far),
            out_shape=jax.ShapeDtypeStruct((half, packed), out_grad.dtype),
            in_specs=[in_vmem] * 5,
            out_specs=in_vmem,
            compiler_params=pltpu.CompilerParams(vmem_limit_bytes=16 * 2**20),
            cost_estimate=pl.CostEstimate(
                flops=6 * half * w_gate.size,
                bytes_accessed=sum(t.nbytes for t in tensors) + 2 * arrived.nbytes,
                transcendentals=half * w_gate.shape[1],
            ),
            name="far_pieces" if is_far else "near_pieces",
        )(arrived, *loaded)

    near = exchange(sent, ("row", "inner")).reshape(half, packed)
    far = lax.ppermute(near, "core", other_core)
    near_pieces = pieces(False, near)
    added = lax.ppermute(pieces(True, far), "core", other_core).astype(jnp.float32)
    added = (near_pieces.astype(jnp.float32) + added).astype(out_grad.dtype)
    returned = exchange(added.reshape(peers, own, packed), ("row", "inner"))
    return pl.pallas_call(
        final_kernel,
        out_shape=[
            jax.ShapeDtypeStruct((own, width), out_grad.dtype),
            jax.ShapeDtypeStruct((own, topk), jnp.float32),
        ],
        in_specs=[in_vmem],
        out_specs=[in_vmem] * 2,
        name="sum_pieces",
    )(returned)


def staged(out_grad, routing_weight, expert_ids, slot_index, w_gate, w_up, w_down, pre_act):
    group_count = lax.axis_size("group")
    inner_count = lax.axis_size("inner")
    own, width = out_grad.shape
    topk = expert_ids.shape[1]
    split_count, experts_here = sizes(group_count, inner_count)
    local_expert = lax.axis_index("inner") // split_count
    block = inner_count * own
    slots = pre_act.shape[1]
    capacity = slots // group_count
    high = -(-(capacity + 1) // 8) * 8

    payload = pack(out_grad, expert_ids, slot_index, routing_weight)
    sent = jnp.broadcast_to(payload[None], (inner_count,) + payload.shape)
    arrived = exchange(sent, "inner").reshape(block, payload.shape[1])
    rows = arrived[:, :width]
    small = arrived[:, width : width + 3 * topk].astype(jnp.float32)
    ids = small[:, :topk].astype(jnp.int32)
    slot = small[:, topk : 2 * topk].astype(jnp.int32)
    weight = small[:, 2 * topk :]
    selected = ids % experts_here == local_expert
    column = ids // experts_here * high + slot
    one_hot = jnp.logical_and(
        column[:, :, None] == jnp.arange(group_count * high, dtype=jnp.int32), selected[:, :, None]
    ).astype(jnp.float32)
    placement = jnp.sum(one_hot, axis=1).astype(jnp.bfloat16)
    send_weight = jnp.sum(one_hot * weight[:, :, None], axis=(0, 1)).reshape(group_count, 1, high)
    send_rows = lax.dot_general(
        placement, rows, (((0,), (0,)), ((), ())), preferred_element_type=jnp.float32
    ).reshape(group_count, high, width)
    last = jnp.arange(high) == high - 1
    weight_row = jnp.pad(send_weight, ((0, 0), (0, 0), (0, width - high)))
    send = jnp.where(last[None, :, None], weight_row, send_rows).astype(jnp.bfloat16)
    buffer = exchange(send, "group")

    buffer_weight = buffer[:, high - 1, :capacity].astype(jnp.float32).reshape(slots, 1)
    buffer_rows = buffer[:, :capacity].reshape(slots, width)
    back_proj = across(buffer_rows, w_down)
    grad_gate, grad_up, gate_piece = gradients(
        back_proj, buffer_weight, pre_act[0].astype(jnp.float32), pre_act[1].astype(jnp.float32)
    )
    pieces = (across(grad_gate, w_gate) + across(grad_up, w_up)).reshape(group_count, capacity, width)
    gate_row = jnp.pad(
        gate_piece.reshape(group_count, 1, capacity), ((0, 0), (0, 0), (0, width - capacity))
    )
    pieces = jnp.pad(pieces, ((0, 0), (0, high - capacity), (0, 0)))
    back = exchange(jnp.where(last[None, :, None], gate_row, pieces).astype(jnp.bfloat16), "group")

    owned = jnp.dot(
        placement, back.reshape(group_count * high, width), preferred_element_type=jnp.float32
    ).astype(jnp.bfloat16)
    gates = back[:, high - 1, :high].reshape(group_count * high).astype(jnp.float32)
    gate_rows = jnp.sum(one_hot * gates, axis=2)
    final = exchange(pack(owned, gate_rows).reshape(inner_count, own, -1), "inner")
    total = jnp.sum(final.astype(jnp.float32), axis=0)
    return total[:, :width].astype(jnp.bfloat16), total[:, width : width + topk]


def solution(mesh):
    if mesh.size <= 64:
        group_count, inner_count = mesh.devices.shape
        devices = mesh.devices.reshape(group_count // CORES, CORES, inner_count)
        mesh, axes, on_device = Mesh(devices, ("row", "core", "inner")), ("row", "core", "inner"), flat
    else:
        axes, on_device = ("group", "inner"), staged
    token, hidden = P(axes, None), P(None, axes)
    return jax.shard_map(
        on_device,
        mesh=mesh,
        in_specs=(token, token, token, token, hidden, hidden, token, P(None, None, axes)),
        out_specs=(token, token),
        check_vma=False,
    )
```

```python
import functools

import jax
import jax.numpy as jnp
from jax import lax
from jax.experimental import pallas as pl
from jax.experimental.pallas import tpu as pltpu
from jax.sharding import Mesh, PartitionSpec as P

LANES = 128
CORES = 2
PLANE = ((0, 0), (1, 0), (0, 1), (1, 1))


def exchange(array, axis):
    return lax.all_to_all(array, axis, split_axis=0, concat_axis=0, tiled=True)


def pack(rows, *small):
    width = sum(s.shape[-1] for s in small)
    pad = -width % LANES
    parts = [rows] + [s.astype(rows.dtype) for s in small]
    if pad:
        parts.append(jnp.zeros(rows.shape[:-1] + (pad,), rows.dtype))
    return jnp.concatenate(parts, axis=-1)


def gradients(back_proj, weight, pre_gate, pre_up):
    gate_sig = jax.nn.sigmoid(pre_gate)
    swish_gate = pre_gate * gate_sig
    gate_piece = jnp.sum(swish_gate * pre_up * back_proj, axis=1, keepdims=True)
    scaled = weight * back_proj
    grad_up = (scaled * swish_gate).astype(jnp.bfloat16)
    grad_gate = (scaled * pre_up * gate_sig * (1.0 + pre_gate * (1.0 - gate_sig))).astype(
        jnp.bfloat16
    )
    return grad_gate, grad_up, gate_piece


def across(a, b):
    return lax.dot_general(a, b, (((1,), (1,)), ((), ())), preferred_element_type=jnp.float32)


def sizes(group_count, inner_count):
    split_count = min(8, inner_count // 4)
    return split_count, inner_count // split_count


def pack_kernel(out_grad, ids, slots, weights, sent, words, reals, small, sems):
    width = out_grad.shape[1]
    topk = ids.shape[1]
    copies = [
        pltpu.make_async_copy(source, target, sems.at[at])
        for at, (source, target) in enumerate(
            ((ids, words.at[0]), (slots, words.at[1]), (weights, reals))
        )
    ]
    copies.append(pltpu.make_async_copy(out_grad, sent.at[:, :width], sems.at[3]))
    for copy in copies:
        copy.start()
    small[...] = jnp.zeros_like(small)
    for copy in copies:
        copy.wait()
    for at, part in enumerate((words[0], words[1], reals[...])):
        small[:, at * topk : (at + 1) * topk] = part.astype(jnp.float32)
    sent[:, width:] = small[...].astype(sent.dtype)


def load_kernel(count, *refs):
    sources, targets, sems = refs[:count], refs[count : 2 * count], refs[2 * count]
    copies = [
        pltpu.make_async_copy(source, target, sems.at[at])
        for at, (source, target) in enumerate(zip(sources, targets))
    ]
    for copy in copies:
        copy.start()
    for copy in copies:
        copy.wait()


def expert_kernel(topk, capacity, is_far, arrived, w_gate, w_up, w_down, pre_act, out):
    half, packed = arrived.shape
    width = w_gate.shape[0]
    slots = pre_act.shape[1]
    x, core = lax.axis_index("x"), lax.axis_index("core")
    expert = (x * CORES + core) * lax.axis_size("z") + lax.axis_index("z")
    small = arrived[:, width:].astype(jnp.float32)
    lane = lax.broadcasted_iota(jnp.int32, small.shape, 1)
    mine = jnp.where(
        jnp.logical_and(small == expert.astype(jnp.float32), lane < topk), 1.0, 0.0
    )
    slot = jnp.sum(pltpu.roll(mine, topk, 1) * small, axis=1, keepdims=True)
    weight = jnp.sum(pltpu.roll(mine, 2 * topk, 1) * small, axis=1, keepdims=True)
    chosen = jnp.sum(mine, axis=1, keepdims=True)
    partner = lax.broadcasted_iota(jnp.int32, (half, slots), 0) // (half // len(PLANE))
    column = lax.broadcasted_iota(jnp.int32, (half, slots), 1)
    source = (x ^ (partner & 1)) * CORES + (1 - core if is_far else core)
    place = source * capacity + slot.astype(jnp.int32)
    one_hot = jnp.where(jnp.logical_and(place == column, chosen > 0.5), 1.0, 0.0)
    one_hot = one_hot.astype(jnp.bfloat16)
    pre_gate = jnp.dot(one_hot, pre_act[0], preferred_element_type=jnp.float32)
    pre_up = jnp.dot(one_hot, pre_act[1], preferred_element_type=jnp.float32)
    back_proj = across(arrived[:, :width], w_down[...])
    grad_gate, grad_up, gate_piece = gradients(back_proj, weight, pre_gate, pre_up)
    step = 512 if width % 512 == 0 else LANES
    for at in range(0, width, step):
        cols = slice(at, at + step)
        pieces = across(grad_gate, w_gate[cols]) + across(grad_up, w_up[cols])
        out[:, cols] = pieces.astype(out.dtype)
    gates = mine * gate_piece
    gates = jnp.where(lax.axis_index("y") == 0, gates, pltpu.roll(gates, topk, 1))
    out[:, width:] = gates.astype(out.dtype)


def plane_sum_kernel(own, *refs):
    arrived, outs = refs[: len(PLANE) - 1], refs[len(PLANE) - 1 :]
    total = own[...].astype(jnp.float32)
    for part in arrived:
        total = total + part[...].astype(jnp.float32)
    total = total.astype(own.dtype)
    rows = outs[0].shape[0]
    for at, out in enumerate(outs):
        out[...] = total[at * rows : (at + 1) * rows]


def final_kernel(*refs):
    arrived, (grad_rows, grad_gate) = refs[:-2], refs[-2:]
    total = arrived[0][...].astype(jnp.float32)
    for part in arrived[1:]:
        total = total + part[...].astype(jnp.float32)
    width, topk = grad_rows.shape[1], grad_gate.shape[1]
    grad_rows[...] = total[:, :width].astype(grad_rows.dtype)
    gates = total[:, width:]
    grad_gate[...] = gates[:, :topk] + gates[:, topk : 2 * topk]


def stay_in_hbm(*arrays):
    return [pltpu.with_memory_space_constraint(a, pltpu.HBM) for a in arrays]


def swap_z(parts):
    count = lax.axis_size("z")
    return [parts[0]] + [
        lax.ppermute(parts[r], "z", [(i, i ^ r) for i in range(count)]) for r in range(1, count)
    ]


def swap_plane(parts):
    arrived = [parts[0]]
    for part, (dx, dy) in zip(parts[1:], PLANE[1:]):
        pairs = [(2 * x + y, 2 * (x ^ dx) + (y ^ dy)) for x in range(2) for y in range(2)]
        arrived.append(lax.ppermute(part, ("x", "y"), pairs))
    return arrived


def swap_core(array):
    return lax.ppermute(array, "core", [(0, 1), (1, 0)])


def flat(out_grad, routing_weight, expert_ids, slot_index, w_gate, w_up, w_down, pre_act):
    own, width = out_grad.shape
    topk = expert_ids.shape[1]
    z_count = lax.axis_size("z")
    quarter = z_count * own
    half = len(PLANE) * quarter
    capacity = pre_act.shape[1] // (lax.axis_size("x") * CORES)
    packed = width + LANES
    in_vmem = pl.BlockSpec(memory_space=pltpu.VMEM)
    in_hbm = pl.BlockSpec(memory_space=pltpu.HBM)

    sent = pl.pallas_call(
        pack_kernel,
        out_shape=jax.ShapeDtypeStruct((own, packed), out_grad.dtype),
        in_specs=[in_hbm] * 4,
        out_specs=in_vmem,
        scratch_shapes=[
            pltpu.VMEM((2, own, topk), expert_ids.dtype),
            pltpu.VMEM((own, topk), routing_weight.dtype),
            pltpu.VMEM((own, LANES), jnp.float32),
            pltpu.SemaphoreType.DMA((4,)),
        ],
        name="pack_rows",
    )(*stay_in_hbm(out_grad, expert_ids, slot_index, routing_weight))
    tensors = (w_gate, w_up, w_down, pre_act)
    loaded = pl.pallas_call(
        functools.partial(load_kernel, len(tensors)),
        out_shape=[pltpu.VMEM(t.shape, t.dtype) for t in tensors],
        in_specs=[in_hbm] * len(tensors),
        out_specs=[in_vmem] * len(tensors),
        scratch_shapes=[pltpu.SemaphoreType.DMA((len(tensors),))],
        cost_estimate=pl.CostEstimate(
            flops=0, bytes_accessed=2 * sum(t.nbytes for t in tensors), transcendentals=0
        ),
        name="load_weights",
    )(*stay_in_hbm(*tensors))

    def pieces(is_far, arrived):
        return pl.pallas_call(
            functools.partial(expert_kernel, topk, capacity, is_far),
            out_shape=jax.ShapeDtypeStruct((half, packed), out_grad.dtype),
            in_specs=[in_vmem] * 5,
            out_specs=in_vmem,
            compiler_params=pltpu.CompilerParams(vmem_limit_bytes=16 * 2**20),
            cost_estimate=pl.CostEstimate(
                flops=6 * half * w_gate.size,
                bytes_accessed=sum(t.nbytes for t in tensors) + 2 * arrived.nbytes,
                transcendentals=half * w_gate.shape[1],
            ),
            name="far_pieces" if is_far else "near_pieces",
        )(arrived, *loaded)

    column = jnp.concatenate(swap_z([sent] * z_count), axis=0)
    near = jnp.concatenate(swap_plane([column] * len(PLANE)), axis=0)
    far = swap_core(near)
    near_pieces = pieces(False, near)
    added = swap_core(pieces(True, far)).astype(jnp.float32)
    added = (near_pieces.astype(jnp.float32) + added).astype(out_grad.dtype)
    quarters = [added[at * quarter : (at + 1) * quarter] for at in range(len(PLANE))]
    parts = pl.pallas_call(
        plane_sum_kernel,
        out_shape=[jax.ShapeDtypeStruct((own, packed), out_grad.dtype)] * z_count,
        in_specs=[in_vmem] * len(PLANE),
        out_specs=[in_vmem] * z_count,
        name="plane_sum",
    )(*swap_plane(quarters))
    return pl.pallas_call(
        final_kernel,
        out_shape=[
            jax.ShapeDtypeStruct((own, width), out_grad.dtype),
            jax.ShapeDtypeStruct((own, topk), jnp.float32),
        ],
        in_specs=[in_vmem] * z_count,
        out_specs=[in_vmem] * 2,
        name="final_sum",
    )(*swap_z(parts))


def staged(out_grad, routing_weight, expert_ids, slot_index, w_gate, w_up, w_down, pre_act):
    group_count = lax.axis_size("group")
    inner_count = lax.axis_size("inner")
    own, width = out_grad.shape
    topk = expert_ids.shape[1]
    split_count, experts_here = sizes(group_count, inner_count)
    local_expert = lax.axis_index("inner") // split_count
    block = inner_count * own
    slots = pre_act.shape[1]
    capacity = slots // group_count
    high = -(-(capacity + 1) // 8) * 8

    payload = pack(out_grad, expert_ids, slot_index, routing_weight)
    sent = jnp.broadcast_to(payload[None], (inner_count,) + payload.shape)
    arrived = exchange(sent, "inner").reshape(block, payload.shape[1])
    rows = arrived[:, :width]
    small = arrived[:, width : width + 3 * topk].astype(jnp.float32)
    ids = small[:, :topk].astype(jnp.int32)
    slot = small[:, topk : 2 * topk].astype(jnp.int32)
    weight = small[:, 2 * topk :]
    selected = ids % experts_here == local_expert
    column = ids // experts_here * high + slot
    one_hot = jnp.logical_and(
        column[:, :, None] == jnp.arange(group_count * high, dtype=jnp.int32), selected[:, :, None]
    ).astype(jnp.float32)
    placement = jnp.sum(one_hot, axis=1).astype(jnp.bfloat16)
    send_weight = jnp.sum(one_hot * weight[:, :, None], axis=(0, 1)).reshape(group_count, 1, high)
    send_rows = lax.dot_general(
        placement, rows, (((0,), (0,)), ((), ())), preferred_element_type=jnp.float32
    ).reshape(group_count, high, width)
    last = jnp.arange(high) == high - 1
    weight_row = jnp.pad(send_weight, ((0, 0), (0, 0), (0, width - high)))
    send = jnp.where(last[None, :, None], weight_row, send_rows).astype(jnp.bfloat16)
    buffer = exchange(send, "group")

    buffer_weight = buffer[:, high - 1, :capacity].astype(jnp.float32).reshape(slots, 1)
    buffer_rows = buffer[:, :capacity].reshape(slots, width)
    back_proj = across(buffer_rows, w_down)
    grad_gate, grad_up, gate_piece = gradients(
        back_proj, buffer_weight, pre_act[0].astype(jnp.float32), pre_act[1].astype(jnp.float32)
    )
    pieces = (across(grad_gate, w_gate) + across(grad_up, w_up)).reshape(group_count, capacity, width)
    gate_row = jnp.pad(
        gate_piece.reshape(group_count, 1, capacity), ((0, 0), (0, 0), (0, width - capacity))
    )
    pieces = jnp.pad(pieces, ((0, 0), (0, high - capacity), (0, 0)))
    back = exchange(jnp.where(last[None, :, None], gate_row, pieces).astype(jnp.bfloat16), "group")

    owned = jnp.dot(
        placement, back.reshape(group_count * high, width), preferred_element_type=jnp.float32
    ).astype(jnp.bfloat16)
    gates = back[:, high - 1, :high].reshape(group_count * high).astype(jnp.float32)
    gate_rows = jnp.sum(one_hot * gates, axis=2)
    final = exchange(pack(owned, gate_rows).reshape(inner_count, own, -1), "inner")
    total = jnp.sum(final.astype(jnp.float32), axis=0)
    return total[:, :width].astype(jnp.bfloat16), total[:, width : width + topk]


def solution(mesh):
    if mesh.devices.shape == (4, 8):
        axes, on_device = ("x", "core", "z", "y"), flat
        mesh = Mesh(mesh.devices.reshape(2, CORES, 4, 2), axes)
    else:
        axes, on_device = ("group", "inner"), staged
    token, hidden = P(axes, None), P(None, axes)
    return jax.shard_map(
        on_device,
        mesh=mesh,
        in_specs=(token, token, token, token, hidden, hidden, token, P(None, None, axes)),
        out_specs=(token, token),
        check_vma=False,
    )
```

```python
import functools

import jax
import jax.numpy as jnp
from jax import lax
from jax.experimental import pallas as pl
from jax.experimental.pallas import tpu as pltpu
from jax.sharding import Mesh, PartitionSpec as P

LANES = 128
CORES = 2


def exchange(array, axis):
    return lax.all_to_all(array, axis, split_axis=0, concat_axis=0, tiled=True)


def pack(rows, *small):
    width = rows.shape[1]
    behind = sum(s.shape[1] for s in small)
    total = width + behind + -behind % LANES
    packed, at = jnp.pad(rows, ((0, 0), (0, total - width))).astype(jnp.float32), width
    for part in small:
        end = at + part.shape[1]
        wide = jnp.pad(part, ((0, 0), (at, total - end)))
        packed = packed + wide.astype(jnp.float32)
        at = end
    return packed.astype(rows.dtype)


def gradients(back_proj, weight, pre_gate, pre_up):
    gate_sig = jax.nn.sigmoid(pre_gate)
    swish_gate = pre_gate * gate_sig
    gate_piece = jnp.sum(swish_gate * pre_up * back_proj, axis=1, keepdims=True)
    scaled = weight * back_proj
    grad_up = (scaled * swish_gate).astype(jnp.bfloat16)
    grad_gate = (scaled * pre_up * gate_sig * (1.0 + pre_gate * (1.0 - gate_sig))).astype(
        jnp.bfloat16
    )
    return grad_gate, grad_up, gate_piece


def across(a, b):
    return lax.dot_general(a, b, (((1,), (1,)), ((), ())), preferred_element_type=jnp.float32)


def sizes(group_count, inner_count):
    split_count = min(8, inner_count // 4)
    return split_count, inner_count // split_count


def load_kernel(w_gate, w_up, w_down, pre_act, w_both, down, saved, sems):
    hidden = w_gate.shape[1]
    copies = [
        pltpu.make_async_copy(source, target, sems.at[at])
        for at, (source, target) in enumerate(
            (
                (w_down, down),
                (pre_act, saved),
                (w_gate, w_both.at[:, :hidden]),
                (w_up, w_both.at[:, hidden:]),
            )
        )
    ]
    for copy in copies:
        copy.start()
    for copy in copies:
        copy.wait()


def expert_kernel(topk, capacity, is_far, arrived, w_both, w_down, pre_act, out):
    half, packed = arrived.shape
    width = w_both.shape[0]
    slots = pre_act.shape[1]
    row_count = lax.axis_size("row")
    split_count, experts_here = sizes(row_count * CORES, lax.axis_size("inner"))
    core = lax.axis_index("core")
    expert = (lax.axis_index("row") * CORES + core) * experts_here
    expert = expert + lax.axis_index("inner") // split_count
    small = arrived[:, width:].astype(jnp.float32)
    lane = lax.broadcasted_iota(jnp.int32, small.shape, 1)
    mine = jnp.where(
        jnp.logical_and(small == expert.astype(jnp.float32), lane < topk), 1.0, 0.0
    )
    slot = jnp.sum(pltpu.roll(mine, topk, 1) * small, axis=1, keepdims=True)
    weight = jnp.sum(pltpu.roll(mine, 2 * topk, 1) * small, axis=1, keepdims=True)
    chosen = jnp.sum(mine, axis=1, keepdims=True)
    row = lax.broadcasted_iota(jnp.int32, (half, slots), 0) // (half // row_count)
    source = row * CORES + (1 - core if is_far else core)
    place = source * capacity + slot.astype(jnp.int32)
    column = lax.broadcasted_iota(jnp.int32, (half, slots), 1)
    one_hot = jnp.where(jnp.logical_and(place == column, chosen > 0.5), 1.0, 0.0)
    one_hot = one_hot.astype(jnp.bfloat16)
    pre_gate = jnp.dot(one_hot, pre_act[0], preferred_element_type=jnp.float32)
    pre_up = jnp.dot(one_hot, pre_act[1], preferred_element_type=jnp.float32)
    back_proj = across(arrived[:, :width], w_down[...])
    grad_gate, grad_up, gate_piece = gradients(back_proj, weight, pre_gate, pre_up)
    grads = jnp.concatenate([grad_gate, grad_up], axis=1)
    step = 512 if width % 512 == 0 else LANES
    for at in range(0, width, step):
        cols = slice(at, at + step)
        out[:, cols] = across(grads, w_both[cols]).astype(out.dtype)
    out[:, width:] = (mine * gate_piece).astype(out.dtype)


def stay_in_hbm(*arrays):
    return [pltpu.with_memory_space_constraint(a, pltpu.HBM) for a in arrays]


def flat(out_grad, routing_weight, expert_ids, slot_index, w_gate, w_up, w_down, pre_act):
    row_count = lax.axis_size("row")
    inner_count = lax.axis_size("inner")
    own, width = out_grad.shape
    topk = expert_ids.shape[1]
    peers = row_count * inner_count
    half = peers * own
    capacity = pre_act.shape[1] // (row_count * CORES)
    packed = width + LANES
    other_core = [(0, 1), (1, 0)]
    in_vmem = pl.BlockSpec(memory_space=pltpu.VMEM)
    in_hbm = pl.BlockSpec(memory_space=pltpu.HBM)

    sent = jnp.broadcast_to(
        pack(out_grad, expert_ids, slot_index, routing_weight)[None], (peers, own, packed)
    )
    tensors = (w_gate, w_up, w_down, pre_act)
    loaded = pl.pallas_call(
        load_kernel,
        out_shape=[
            pltpu.VMEM((width, 2 * w_gate.shape[1]), w_gate.dtype),
            pltpu.VMEM(w_down.shape, w_down.dtype),
            pltpu.VMEM(pre_act.shape, pre_act.dtype),
        ],
        in_specs=[in_hbm] * 4,
        out_specs=[in_vmem] * 3,
        scratch_shapes=[pltpu.SemaphoreType.DMA((4,))],
        cost_estimate=pl.CostEstimate(
            flops=0, bytes_accessed=2 * sum(t.nbytes for t in tensors), transcendentals=0
        ),
        name="load_weights",
    )(*stay_in_hbm(*tensors))

    def pieces(is_far, arrived):
        return pl.pallas_call(
            functools.partial(expert_kernel, topk, capacity, is_far),
            out_shape=jax.ShapeDtypeStruct((half, packed), out_grad.dtype),
            in_specs=[in_vmem] * 4,
            out_specs=in_vmem,
            compiler_params=pltpu.CompilerParams(vmem_limit_bytes=16 * 2**20),
            cost_estimate=pl.CostEstimate(
                flops=6 * half * w_gate.size,
                bytes_accessed=sum(t.nbytes for t in tensors) + 2 * arrived.nbytes,
                transcendentals=half * w_gate.shape[1],
            ),
            name="far_pieces" if is_far else "near_pieces",
        )(arrived, *loaded)

    near = exchange(sent, ("row", "inner")).reshape(half, packed)
    far = lax.ppermute(near, "core", other_core)
    near_pieces = pieces(False, near)
    added = lax.ppermute(pieces(True, far), "core", other_core).astype(jnp.float32)
    added = (near_pieces.astype(jnp.float32) + added).astype(out_grad.dtype)
    returned = exchange(added.reshape(peers, own, packed), ("row", "inner"))
    rows, gates = returned[:, :, :width], returned[:, :, width : width + topk]
    grad_rows = jnp.sum(rows.astype(jnp.float32), axis=0).astype(out_grad.dtype)
    return grad_rows, jnp.sum(gates.astype(jnp.float32), axis=0)


def staged(out_grad, routing_weight, expert_ids, slot_index, w_gate, w_up, w_down, pre_act):
    group_count = lax.axis_size("group")
    inner_count = lax.axis_size("inner")
    own, width = out_grad.shape
    topk = expert_ids.shape[1]
    split_count, experts_here = sizes(group_count, inner_count)
    local_expert = lax.axis_index("inner") // split_count
    block = inner_count * own
    slots = pre_act.shape[1]
    capacity = slots // group_count
    high = -(-(capacity + 1) // 8) * 8

    payload = pack(out_grad, expert_ids, slot_index, routing_weight)
    sent = jnp.broadcast_to(payload[None], (inner_count,) + payload.shape)
    arrived = exchange(sent, "inner").reshape(block, payload.shape[1])
    rows = arrived[:, :width]
    small = arrived[:, width : width + 3 * topk].astype(jnp.float32)
    ids = small[:, :topk].astype(jnp.int32)
    slot = small[:, topk : 2 * topk].astype(jnp.int32)
    weight = small[:, 2 * topk :]
    selected = ids % experts_here == local_expert
    column = ids // experts_here * high + slot
    one_hot = jnp.logical_and(
        column[:, :, None] == jnp.arange(group_count * high, dtype=jnp.int32), selected[:, :, None]
    ).astype(jnp.float32)
    placement = jnp.sum(one_hot, axis=1).astype(jnp.bfloat16)
    send_weight = jnp.sum(one_hot * weight[:, :, None], axis=(0, 1)).reshape(group_count, 1, high)
    send_rows = lax.dot_general(
        placement, rows, (((0,), (0,)), ((), ())), preferred_element_type=jnp.float32
    ).reshape(group_count, high, width)
    last = jnp.arange(high) == high - 1
    weight_row = jnp.pad(send_weight, ((0, 0), (0, 0), (0, width - high)))
    send = jnp.where(last[None, :, None], weight_row, send_rows).astype(jnp.bfloat16)
    buffer = exchange(send, "group")

    buffer_weight = buffer[:, high - 1, :capacity].astype(jnp.float32).reshape(slots, 1)
    buffer_rows = buffer[:, :capacity].reshape(slots, width)
    back_proj = across(buffer_rows, w_down)
    grad_gate, grad_up, gate_piece = gradients(
        back_proj, buffer_weight, pre_act[0].astype(jnp.float32), pre_act[1].astype(jnp.float32)
    )
    pieces = (across(grad_gate, w_gate) + across(grad_up, w_up)).reshape(group_count, capacity, width)
    gate_row = jnp.pad(
        gate_piece.reshape(group_count, 1, capacity), ((0, 0), (0, 0), (0, width - capacity))
    )
    pieces = jnp.pad(pieces, ((0, 0), (0, high - capacity), (0, 0)))
    back = exchange(jnp.where(last[None, :, None], gate_row, pieces).astype(jnp.bfloat16), "group")

    owned = jnp.dot(
        placement, back.reshape(group_count * high, width), preferred_element_type=jnp.float32
    ).astype(jnp.bfloat16)
    gates = back[:, high - 1, :high].reshape(group_count * high).astype(jnp.float32)
    gate_rows = jnp.sum(one_hot * gates, axis=2)
    final = exchange(pack(owned, gate_rows).reshape(inner_count, own, -1), "inner")
    total = jnp.sum(final.astype(jnp.float32), axis=0)
    return total[:, :width].astype(jnp.bfloat16), total[:, width : width + topk]


def solution(mesh):
    if mesh.size <= 64:
        group_count, inner_count = mesh.devices.shape
        devices = mesh.devices.reshape(group_count // CORES, CORES, inner_count)
        mesh, axes, on_device = Mesh(devices, ("row", "core", "inner")), ("row", "core", "inner"), flat
    else:
        axes, on_device = ("group", "inner"), staged
    token, hidden = P(axes, None), P(None, axes)
    return jax.shard_map(
        on_device,
        mesh=mesh,
        in_specs=(token, token, token, token, hidden, hidden, token, P(None, None, axes)),
        out_specs=(token, token),
        check_vma=False,
    )
```

```python
import functools

import jax
import jax.numpy as jnp
from jax import lax
from jax.experimental import pallas as pl
from jax.experimental.pallas import tpu as pltpu
from jax.sharding import Mesh, PartitionSpec as P

LANES = 128
CORES = 2


def exchange(array, axis):
    return lax.all_to_all(array, axis, split_axis=0, concat_axis=0, tiled=True)


def pack(rows, *small):
    width = rows.shape[1]
    behind = sum(s.shape[1] for s in small)
    total = width + behind + -behind % LANES
    packed, at = jnp.pad(rows, ((0, 0), (0, total - width))).astype(jnp.float32), width
    for part in small:
        end = at + part.shape[1]
        wide = jnp.pad(part, ((0, 0), (at, total - end)))
        packed = packed + wide.astype(jnp.float32)
        at = end
    return packed.astype(rows.dtype)


def gradients(back_proj, weight, pre_gate, pre_up):
    gate_sig = jax.nn.sigmoid(pre_gate)
    swish_gate = pre_gate * gate_sig
    gate_piece = jnp.sum(swish_gate * pre_up * back_proj, axis=1, keepdims=True)
    scaled = weight * back_proj
    grad_up = (scaled * swish_gate).astype(jnp.bfloat16)
    grad_gate = (scaled * pre_up * gate_sig * (1.0 + pre_gate * (1.0 - gate_sig))).astype(
        jnp.bfloat16
    )
    return grad_gate, grad_up, gate_piece


def across(a, b):
    return lax.dot_general(a, b, (((1,), (1,)), ((), ())), preferred_element_type=jnp.float32)


def sizes(group_count, inner_count):
    split_count = min(8, inner_count // 4)
    return split_count, inner_count // split_count


def expert_kernel(
    topk, capacity, arrived, w_gate, w_up, w_down, pre_act, gate2, up2, down2, saved2, out, *scratch
):
    gate1, up1, down1, saved1, sems = scratch
    copies = [
        pltpu.make_async_copy(source, target, sems.at[at])
        for at, (source, target) in enumerate(
            ((w_down, down1), (pre_act, saved1), (w_gate, gate1), (w_up, up1))
        )
    ]
    for copy in copies:
        copy.start()
    half, packed = arrived.shape
    width = w_gate.shape[0]
    slots = pre_act.shape[1]
    row_count = lax.axis_size("row")
    split_count, experts_here = sizes(row_count * CORES, lax.axis_size("inner"))
    core = lax.axis_index("core")
    group_row = lax.axis_index("row") * CORES
    local_expert = lax.axis_index("inner") // split_count
    small = arrived[:, width:].astype(jnp.float32)
    lane = lax.broadcasted_iota(jnp.int32, small.shape, 1)
    source = lax.broadcasted_iota(jnp.int32, (half, slots), 0) // (half // row_count)
    first = (source * CORES + core) * capacity
    column = lax.broadcasted_iota(jnp.int32, (half, slots), 1)

    def routed(group_core):
        expert = (group_row + group_core) * experts_here + local_expert
        mine = jnp.where(
            jnp.logical_and(small == expert.astype(jnp.float32), lane < topk), 1.0, 0.0
        )
        slot = jnp.sum(pltpu.roll(mine, topk, 1) * small, axis=1, keepdims=True)
        weight = jnp.sum(pltpu.roll(mine, 2 * topk, 1) * small, axis=1, keepdims=True)
        chosen = jnp.sum(mine, axis=1, keepdims=True)
        hit = jnp.logical_and(first + slot.astype(jnp.int32) == column, chosen > 0.5)
        return mine, weight, jnp.where(hit, 1.0, 0.0).astype(jnp.bfloat16)

    def backward(routing, back_proj, saved):
        mine, weight, one_hot = routing
        pre_gate = jnp.dot(one_hot, saved[0], preferred_element_type=jnp.float32)
        pre_up = jnp.dot(one_hot, saved[1], preferred_element_type=jnp.float32)
        grad_gate, grad_up, gate_piece = gradients(back_proj, weight, pre_gate, pre_up)
        return grad_gate, grad_up, mine * gate_piece

    rows = arrived[:, :width]
    other, own = routed(1 - core), routed(core)
    grad_gate2, grad_up2, gates2 = backward(other, across(rows, down2[...]), saved2)
    copies[0].wait()
    copies[1].wait()
    grad_gate1, grad_up1, gates1 = backward(own, across(rows, down1[...]), saved1)
    copies[2].wait()
    copies[3].wait()
    grads = jnp.concatenate([grad_gate1, grad_up1, grad_gate2, grad_up2], axis=1)
    step = 512 if width % 512 == 0 else LANES
    for at in range(0, width, step):
        cols = slice(at, at + step)
        both = jnp.concatenate([gate1[cols], up1[cols], gate2[cols], up2[cols]], axis=1)
        out[:, cols] = across(grads, both).astype(out.dtype)
    out[:, width:] = (gates1 + gates2).astype(out.dtype)


def stay_in(space, *arrays):
    return [pltpu.with_memory_space_constraint(a, space) for a in arrays]


def flat(out_grad, routing_weight, expert_ids, slot_index, w_gate, w_up, w_down, pre_act):
    row_count = lax.axis_size("row")
    inner_count = lax.axis_size("inner")
    own, width = out_grad.shape
    topk = expert_ids.shape[1]
    peers = row_count * inner_count
    half = peers * own
    capacity = pre_act.shape[1] // (row_count * CORES)
    packed = width + LANES
    in_vmem = pl.BlockSpec(memory_space=pltpu.VMEM)
    in_hbm = pl.BlockSpec(memory_space=pltpu.HBM)

    tensors = (w_gate, w_up, w_down, pre_act)
    swapped = [lax.ppermute(t, "core", [(0, 1), (1, 0)]) for t in tensors]
    sent = jnp.broadcast_to(
        pack(out_grad, expert_ids, slot_index, routing_weight)[None], (peers, own, packed)
    )
    arrived = exchange(sent, ("row", "inner")).reshape(half, packed)
    pieces = pl.pallas_call(
        functools.partial(expert_kernel, topk, capacity),
        out_shape=jax.ShapeDtypeStruct((half, packed), out_grad.dtype),
        in_specs=[in_vmem] + [in_hbm] * 4 + [in_vmem] * 4,
        out_specs=in_vmem,
        scratch_shapes=[pltpu.VMEM(t.shape, t.dtype) for t in tensors]
        + [pltpu.SemaphoreType.DMA((4,))],
        compiler_params=pltpu.CompilerParams(vmem_limit_bytes=16 * 2**20),
        cost_estimate=pl.CostEstimate(
            flops=12 * half * w_gate.size,
            bytes_accessed=2 * sum(t.nbytes for t in tensors) + 2 * arrived.nbytes,
            transcendentals=2 * half * w_gate.shape[1],
        ),
        name="expert_pieces",
    )(arrived, *stay_in(pltpu.HBM, *tensors), *stay_in(pltpu.VMEM, *swapped))
    returned = exchange(pieces.reshape(peers, own, packed), ("row", "inner"))
    rows, gates = returned[:, :, :width], returned[:, :, width : width + topk]
    grad_rows = jnp.sum(rows.astype(jnp.float32), axis=0).astype(out_grad.dtype)
    return grad_rows, jnp.sum(gates.astype(jnp.float32), axis=0)


def staged(out_grad, routing_weight, expert_ids, slot_index, w_gate, w_up, w_down, pre_act):
    group_count = lax.axis_size("group")
    inner_count = lax.axis_size("inner")
    own, width = out_grad.shape
    topk = expert_ids.shape[1]
    split_count, experts_here = sizes(group_count, inner_count)
    local_expert = lax.axis_index("inner") // split_count
    block = inner_count * own
    slots = pre_act.shape[1]
    capacity = slots // group_count
    high = -(-(capacity + 1) // 8) * 8

    payload = pack(out_grad, expert_ids, slot_index, routing_weight)
    sent = jnp.broadcast_to(payload[None], (inner_count,) + payload.shape)
    arrived = exchange(sent, "inner").reshape(block, payload.shape[1])
    rows = arrived[:, :width]
    small = arrived[:, width : width + 3 * topk].astype(jnp.float32)
    ids = small[:, :topk].astype(jnp.int32)
    slot = small[:, topk : 2 * topk].astype(jnp.int32)
    weight = small[:, 2 * topk :]
    selected = ids % experts_here == local_expert
    column = ids // experts_here * high + slot
    one_hot = jnp.logical_and(
        column[:, :, None] == jnp.arange(group_count * high, dtype=jnp.int32), selected[:, :, None]
    ).astype(jnp.float32)
    placement = jnp.sum(one_hot, axis=1).astype(jnp.bfloat16)
    send_weight = jnp.sum(one_hot * weight[:, :, None], axis=(0, 1)).reshape(group_count, 1, high)
    send_rows = lax.dot_general(
        placement, rows, (((0,), (0,)), ((), ())), preferred_element_type=jnp.float32
    ).reshape(group_count, high, width)
    last = jnp.arange(high) == high - 1
    weight_row = jnp.pad(send_weight, ((0, 0), (0, 0), (0, width - high)))
    send = jnp.where(last[None, :, None], weight_row, send_rows).astype(jnp.bfloat16)
    buffer = exchange(send, "group")

    buffer_weight = buffer[:, high - 1, :capacity].astype(jnp.float32).reshape(slots, 1)
    buffer_rows = buffer[:, :capacity].reshape(slots, width)
    back_proj = across(buffer_rows, w_down)
    grad_gate, grad_up, gate_piece = gradients(
        back_proj, buffer_weight, pre_act[0].astype(jnp.float32), pre_act[1].astype(jnp.float32)
    )
    pieces = (across(grad_gate, w_gate) + across(grad_up, w_up)).reshape(group_count, capacity, width)
    gate_row = jnp.pad(
        gate_piece.reshape(group_count, 1, capacity), ((0, 0), (0, 0), (0, width - capacity))
    )
    pieces = jnp.pad(pieces, ((0, 0), (0, high - capacity), (0, 0)))
    back = exchange(jnp.where(last[None, :, None], gate_row, pieces).astype(jnp.bfloat16), "group")

    owned = jnp.dot(
        placement, back.reshape(group_count * high, width), preferred_element_type=jnp.float32
    ).astype(jnp.bfloat16)
    gates = back[:, high - 1, :high].reshape(group_count * high).astype(jnp.float32)
    gate_rows = jnp.sum(one_hot * gates, axis=2)
    final = exchange(pack(owned, gate_rows).reshape(inner_count, own, -1), "inner")
    total = jnp.sum(final.astype(jnp.float32), axis=0)
    return total[:, :width].astype(jnp.bfloat16), total[:, width : width + topk]


def solution(mesh):
    if mesh.size <= 64:
        group_count, inner_count = mesh.devices.shape
        devices = mesh.devices.reshape(group_count // CORES, CORES, inner_count)
        mesh, axes, on_device = Mesh(devices, ("row", "core", "inner")), ("row", "core", "inner"), flat
    else:
        axes, on_device = ("group", "inner"), staged
    token, hidden = P(axes, None), P(None, axes)
    return jax.shard_map(
        on_device,
        mesh=mesh,
        in_specs=(token, token, token, token, hidden, hidden, token, P(None, None, axes)),
        out_specs=(token, token),
        check_vma=False,
    )
```

```python
import functools

import jax
import jax.numpy as jnp
from jax import lax
from jax.experimental import pallas as pl
from jax.experimental.pallas import tpu as pltpu
from jax.sharding import Mesh, PartitionSpec as P

LANES = 128
CORES = 2


def exchange(array, axis):
    return lax.all_to_all(array, axis, split_axis=0, concat_axis=0, tiled=True)


def pack(rows, *small):
    width = rows.shape[1]
    behind = sum(s.shape[1] for s in small)
    total = width + behind + -behind % LANES
    packed, at = jnp.pad(rows, ((0, 0), (0, total - width))).astype(jnp.float32), width
    for part in small:
        end = at + part.shape[1]
        wide = jnp.pad(part, ((0, 0), (at, total - end)))
        packed = packed + wide.astype(jnp.float32)
        at = end
    return packed.astype(rows.dtype)


def gradients(back_proj, weight, pre_gate, pre_up):
    gate_sig = jax.nn.sigmoid(pre_gate)
    swish_gate = pre_gate * gate_sig
    gate_piece = jnp.sum(swish_gate * pre_up * back_proj, axis=1, keepdims=True)
    scaled = weight * back_proj
    grad_up = (scaled * swish_gate).astype(jnp.bfloat16)
    grad_gate = (scaled * pre_up * gate_sig * (1.0 + pre_gate * (1.0 - gate_sig))).astype(
        jnp.bfloat16
    )
    return grad_gate, grad_up, gate_piece


def across(a, b):
    return lax.dot_general(a, b, (((1,), (1,)), ((), ())), preferred_element_type=jnp.float32)


def sizes(group_count, inner_count):
    split_count = min(8, inner_count // 4)
    return split_count, inner_count // split_count


def load_kernel(count, *refs):
    sources, targets, sems = refs[:count], refs[count : 2 * count], refs[2 * count]
    copies = [
        pltpu.make_async_copy(source, target, sems.at[at])
        for at, (source, target) in enumerate(zip(sources, targets))
    ]
    for copy in copies:
        copy.start()
    for copy in copies:
        copy.wait()


def expert_kernel(
    topk, capacity, arrived, gate1, up1, down1, saved1, gate2, up2, down2, saved2, out
):
    half, packed = arrived.shape
    width, hidden = gate1.shape
    slots = saved1.shape[1]
    row_count = lax.axis_size("row")
    split_count, experts_here = sizes(row_count * CORES, lax.axis_size("inner"))
    core = lax.axis_index("core")
    group_row = lax.axis_index("row") * CORES
    local_expert = lax.axis_index("inner") // split_count
    down = jnp.concatenate([down1[...], down2[...]], axis=0)
    back = across(down, arrived[:, :width]).T
    small = arrived[:, width:].astype(jnp.float32)
    lane = lax.broadcasted_iota(jnp.int32, small.shape, 1)
    source = lax.broadcasted_iota(jnp.int32, (half, slots), 0) // (half // row_count)
    first = (source * CORES + core) * capacity
    column = lax.broadcasted_iota(jnp.int32, (half, slots), 1)

    def backward(group_core, back_proj, saved):
        expert = (group_row + group_core) * experts_here + local_expert
        mine = jnp.where(
            jnp.logical_and(small == expert.astype(jnp.float32), lane < topk), 1.0, 0.0
        )
        slot = jnp.sum(pltpu.roll(mine, topk, 1) * small, axis=1, keepdims=True)
        weight = jnp.sum(pltpu.roll(mine, 2 * topk, 1) * small, axis=1, keepdims=True)
        chosen = jnp.sum(mine, axis=1, keepdims=True)
        hit = jnp.logical_and(first + slot.astype(jnp.int32) == column, chosen > 0.5)
        one_hot = jnp.where(hit, 1.0, 0.0).astype(jnp.bfloat16)
        pre_gate = jnp.dot(one_hot, saved[0], preferred_element_type=jnp.float32)
        pre_up = jnp.dot(one_hot, saved[1], preferred_element_type=jnp.float32)
        grad_gate, grad_up, gate_piece = gradients(back_proj, weight, pre_gate, pre_up)
        return grad_gate, grad_up, mine * gate_piece

    grad_gate1, grad_up1, gates1 = backward(core, back[:, :hidden], saved1)
    grad_gate2, grad_up2, gates2 = backward(1 - core, back[:, hidden:], saved2)
    grads = jnp.concatenate([grad_gate1, grad_up1, grad_gate2, grad_up2], axis=1)
    step = 512 if width % 512 == 0 else LANES
    for at in range(0, width, step):
        cols = slice(at, at + step)
        weights = jnp.concatenate([gate1[cols], up1[cols], gate2[cols], up2[cols]], axis=1)
        out[:, cols] = across(weights, grads).T.astype(out.dtype)
    out[:, width:] = (gates1 + gates2).astype(out.dtype)


def stay_in(space, *arrays):
    return [pltpu.with_memory_space_constraint(a, space) for a in arrays]


def flat(out_grad, routing_weight, expert_ids, slot_index, w_gate, w_up, w_down, pre_act):
    row_count = lax.axis_size("row")
    inner_count = lax.axis_size("inner")
    own, width = out_grad.shape
    topk = expert_ids.shape[1]
    peers = row_count * inner_count
    half = peers * own
    capacity = pre_act.shape[1] // (row_count * CORES)
    packed = width + LANES
    in_vmem = pl.BlockSpec(memory_space=pltpu.VMEM)
    in_hbm = pl.BlockSpec(memory_space=pltpu.HBM)

    tensors = (w_gate, w_up, w_down, pre_act)
    swapped = [lax.ppermute(t, "core", [(0, 1), (1, 0)]) for t in tensors]
    sent = jnp.broadcast_to(
        pack(out_grad, expert_ids, slot_index, routing_weight)[None], (peers, own, packed)
    )
    arrived = exchange(sent, ("row", "inner")).reshape(half, packed)
    loaded = pl.pallas_call(
        functools.partial(load_kernel, len(tensors)),
        out_shape=[pltpu.VMEM(t.shape, t.dtype) for t in tensors],
        in_specs=[in_hbm] * len(tensors),
        out_specs=[in_vmem] * len(tensors),
        scratch_shapes=[pltpu.SemaphoreType.DMA((len(tensors),))],
        cost_estimate=pl.CostEstimate(
            flops=0, bytes_accessed=2 * sum(t.nbytes for t in tensors), transcendentals=0
        ),
        name="load_weights",
    )(*stay_in(pltpu.HBM, *tensors))
    pieces = pl.pallas_call(
        functools.partial(expert_kernel, topk, capacity),
        out_shape=jax.ShapeDtypeStruct((half, packed), out_grad.dtype),
        in_specs=[in_vmem] * 9,
        out_specs=in_vmem,
        compiler_params=pltpu.CompilerParams(vmem_limit_bytes=16 * 2**20),
        cost_estimate=pl.CostEstimate(
            flops=12 * half * w_gate.size,
            bytes_accessed=2 * sum(t.nbytes for t in tensors) + 2 * arrived.nbytes,
            transcendentals=2 * half * w_gate.shape[1],
        ),
        name="expert_pieces",
    )(arrived, *loaded, *stay_in(pltpu.VMEM, *swapped))
    returned = exchange(pieces.reshape(peers, own, packed), ("row", "inner"))
    rows, gates = returned[:, :, :width], returned[:, :, width : width + topk]
    grad_rows = jnp.sum(rows.astype(jnp.float32), axis=0).astype(out_grad.dtype)
    return grad_rows, jnp.sum(gates.astype(jnp.float32), axis=0)


def staged(out_grad, routing_weight, expert_ids, slot_index, w_gate, w_up, w_down, pre_act):
    group_count = lax.axis_size("group")
    inner_count = lax.axis_size("inner")
    own, width = out_grad.shape
    topk = expert_ids.shape[1]
    split_count, experts_here = sizes(group_count, inner_count)
    local_expert = lax.axis_index("inner") // split_count
    block = inner_count * own
    slots = pre_act.shape[1]
    capacity = slots // group_count
    high = -(-(capacity + 1) // 8) * 8

    payload = pack(out_grad, expert_ids, slot_index, routing_weight)
    sent = jnp.broadcast_to(payload[None], (inner_count,) + payload.shape)
    arrived = exchange(sent, "inner").reshape(block, payload.shape[1])
    rows = arrived[:, :width]
    small = arrived[:, width : width + 3 * topk].astype(jnp.float32)
    ids = small[:, :topk].astype(jnp.int32)
    slot = small[:, topk : 2 * topk].astype(jnp.int32)
    weight = small[:, 2 * topk :]
    selected = ids % experts_here == local_expert
    column = ids // experts_here * high + slot
    one_hot = jnp.logical_and(
        column[:, :, None] == jnp.arange(group_count * high, dtype=jnp.int32), selected[:, :, None]
    ).astype(jnp.float32)
    placement = jnp.sum(one_hot, axis=1).astype(jnp.bfloat16)
    send_weight = jnp.sum(one_hot * weight[:, :, None], axis=(0, 1)).reshape(group_count, 1, high)
    send_rows = lax.dot_general(
        placement, rows, (((0,), (0,)), ((), ())), preferred_element_type=jnp.float32
    ).reshape(group_count, high, width)
    last = jnp.arange(high) == high - 1
    weight_row = jnp.pad(send_weight, ((0, 0), (0, 0), (0, width - high)))
    send = jnp.where(last[None, :, None], weight_row, send_rows).astype(jnp.bfloat16)
    buffer = exchange(send, "group")

    buffer_weight = buffer[:, high - 1, :capacity].astype(jnp.float32).reshape(slots, 1)
    buffer_rows = buffer[:, :capacity].reshape(slots, width)
    back_proj = across(buffer_rows, w_down)
    grad_gate, grad_up, gate_piece = gradients(
        back_proj, buffer_weight, pre_act[0].astype(jnp.float32), pre_act[1].astype(jnp.float32)
    )
    pieces = (across(grad_gate, w_gate) + across(grad_up, w_up)).reshape(group_count, capacity, width)
    gate_row = jnp.pad(
        gate_piece.reshape(group_count, 1, capacity), ((0, 0), (0, 0), (0, width - capacity))
    )
    pieces = jnp.pad(pieces, ((0, 0), (0, high - capacity), (0, 0)))
    back = exchange(jnp.where(last[None, :, None], gate_row, pieces).astype(jnp.bfloat16), "group")

    owned = jnp.dot(
        placement, back.reshape(group_count * high, width), preferred_element_type=jnp.float32
    ).astype(jnp.bfloat16)
    gates = back[:, high - 1, :high].reshape(group_count * high).astype(jnp.float32)
    gate_rows = jnp.sum(one_hot * gates, axis=2)
    final = exchange(pack(owned, gate_rows).reshape(inner_count, own, -1), "inner")
    total = jnp.sum(final.astype(jnp.float32), axis=0)
    return total[:, :width].astype(jnp.bfloat16), total[:, width : width + topk]


def solution(mesh):
    if mesh.size <= 64:
        group_count, inner_count = mesh.devices.shape
        devices = mesh.devices.reshape(group_count // CORES, CORES, inner_count)
        mesh, axes, on_device = Mesh(devices, ("row", "core", "inner")), ("row", "core", "inner"), flat
    else:
        axes, on_device = ("group", "inner"), staged
    token, hidden = P(axes, None), P(None, axes)
    return jax.shard_map(
        on_device,
        mesh=mesh,
        in_specs=(token, token, token, token, hidden, hidden, token, P(None, None, axes)),
        out_specs=(token, token),
        check_vma=False,
    )
```

```python
import functools

import jax
import jax.numpy as jnp
from jax import lax
from jax.experimental import pallas as pl
from jax.experimental.pallas import tpu as pltpu
from jax.sharding import Mesh, PartitionSpec as P

LANES = 128
CORES = 2


def exchange(array, axis):
    return lax.all_to_all(array, axis, split_axis=0, concat_axis=0, tiled=True)


def pack(rows, *small):
    width = rows.shape[1]
    behind = sum(s.shape[1] for s in small)
    total = width + behind + -behind % LANES
    packed, at = jnp.pad(rows, ((0, 0), (0, total - width))).astype(jnp.float32), width
    for part in small:
        end = at + part.shape[1]
        wide = jnp.pad(part, ((0, 0), (at, total - end)))
        packed = packed + wide.astype(jnp.float32)
        at = end
    return packed.astype(rows.dtype)


def gradients(back_proj, weight, pre_gate, pre_up):
    gate_sig = jax.nn.sigmoid(pre_gate)
    swish_gate = pre_gate * gate_sig
    gate_piece = jnp.sum(swish_gate * pre_up * back_proj, axis=1, keepdims=True)
    scaled = weight * back_proj
    grad_up = (scaled * swish_gate).astype(jnp.bfloat16)
    grad_gate = (scaled * pre_up * gate_sig * (1.0 + pre_gate * (1.0 - gate_sig))).astype(
        jnp.bfloat16
    )
    return grad_gate, grad_up, gate_piece


def across(a, b):
    return lax.dot_general(a, b, (((1,), (1,)), ((), ())), preferred_element_type=jnp.float32)


def sizes(group_count, inner_count):
    split_count = min(8, inner_count // 4)
    return split_count, inner_count // split_count


def expert_kernel(
    topk, capacity, arrived, w_gate, w_up, w_down, pre_act, gate2, up2, down2, saved2, out, *scratch
):
    gate1, up1, down1, saved1, sems = scratch
    copies = [
        pltpu.make_async_copy(source, target, sems.at[at])
        for at, (source, target) in enumerate(
            ((pre_act, saved1), (w_down, down1), (w_gate, gate1), (w_up, up1))
        )
    ]
    for copy in copies:
        copy.start()
    half, packed = arrived.shape
    width = w_gate.shape[0]
    slots = pre_act.shape[1]
    row_count = lax.axis_size("row")
    split_count, experts_here = sizes(row_count * CORES, lax.axis_size("inner"))
    core = lax.axis_index("core")
    group_row = lax.axis_index("row") * CORES
    local_expert = lax.axis_index("inner") // split_count
    small = arrived[:, width:].astype(jnp.float32)
    lane = lax.broadcasted_iota(jnp.int32, small.shape, 1)
    source = lax.broadcasted_iota(jnp.int32, (half, slots), 0) // (half // row_count)
    first = (source * CORES + core) * capacity
    column = lax.broadcasted_iota(jnp.int32, (half, slots), 1)

    def routed(group_core):
        expert = (group_row + group_core) * experts_here + local_expert
        mine = jnp.where(
            jnp.logical_and(small == expert.astype(jnp.float32), lane < topk), 1.0, 0.0
        )
        slot = jnp.sum(pltpu.roll(mine, topk, 1) * small, axis=1, keepdims=True)
        weight = jnp.sum(pltpu.roll(mine, 2 * topk, 1) * small, axis=1, keepdims=True)
        chosen = jnp.sum(mine, axis=1, keepdims=True)
        hit = jnp.logical_and(first + slot.astype(jnp.int32) == column, chosen > 0.5)
        return mine, weight, jnp.where(hit, 1.0, 0.0).astype(jnp.bfloat16)

    def backward(routing, back_proj, saved):
        mine, weight, one_hot = routing
        pre_gate = jnp.dot(one_hot, saved[0], preferred_element_type=jnp.float32)
        pre_up = jnp.dot(one_hot, saved[1], preferred_element_type=jnp.float32)
        grad_gate, grad_up, gate_piece = gradients(back_proj, weight, pre_gate, pre_up)
        return grad_gate, grad_up, mine * gate_piece

    rows = arrived[:, :width]
    other, own = routed(1 - core), routed(core)
    grad_gate2, grad_up2, gates2 = backward(other, across(rows, down2[...]), saved2)
    copies[0].wait()
    copies[1].wait()
    grad_gate1, grad_up1, gates1 = backward(own, across(rows, down1[...]), saved1)
    copies[2].wait()
    copies[3].wait()
    grads = jnp.concatenate([grad_gate1, grad_up1, grad_gate2, grad_up2], axis=1)
    step = 512 if width % 512 == 0 else LANES
    for at in range(0, width, step):
        cols = slice(at, at + step)
        both = jnp.concatenate([gate1[cols], up1[cols], gate2[cols], up2[cols]], axis=1)
        out[:, cols] = across(grads, both).astype(out.dtype)
    out[:, width:] = (gates1 + gates2).astype(out.dtype)


def stay_in(space, *arrays):
    return [pltpu.with_memory_space_constraint(a, space) for a in arrays]


def flat(out_grad, routing_weight, expert_ids, slot_index, w_gate, w_up, w_down, pre_act):
    row_count = lax.axis_size("row")
    inner_count = lax.axis_size("inner")
    own, width = out_grad.shape
    topk = expert_ids.shape[1]
    peers = row_count * inner_count
    half = peers * own
    capacity = pre_act.shape[1] // (row_count * CORES)
    packed = width + LANES
    in_vmem = pl.BlockSpec(memory_space=pltpu.VMEM)
    in_hbm = pl.BlockSpec(memory_space=pltpu.HBM)

    weights = (w_gate, w_up, w_down)
    saved, *swapped = [
        lax.ppermute(t, "core", [(0, 1), (1, 0)]) for t in (pre_act, *weights)
    ]
    payload = pack(out_grad, expert_ids, slot_index, routing_weight)
    payload, saved = lax.optimization_barrier((payload, saved))
    sent = jnp.broadcast_to(payload[None], (peers, own, packed))
    arrived = exchange(sent, ("row", "inner")).reshape(half, packed)
    pieces = pl.pallas_call(
        functools.partial(expert_kernel, topk, capacity),
        out_shape=jax.ShapeDtypeStruct((half, packed), out_grad.dtype),
        in_specs=[in_vmem] + [in_hbm] * 4 + [in_vmem] * 4,
        out_specs=in_vmem,
        scratch_shapes=[pltpu.VMEM(t.shape, t.dtype) for t in (*weights, pre_act)]
        + [pltpu.SemaphoreType.DMA((4,))],
        compiler_params=pltpu.CompilerParams(vmem_limit_bytes=16 * 2**20),
        cost_estimate=pl.CostEstimate(
            flops=12 * half * w_gate.size,
            bytes_accessed=2 * sum(t.nbytes for t in weights) + 2 * arrived.nbytes,
            transcendentals=2 * half * w_gate.shape[1],
        ),
        name="expert_pieces",
    )(
        arrived,
        *stay_in(pltpu.HBM, *weights, pre_act),
        *stay_in(pltpu.VMEM, *swapped, saved),
    )
    returned = exchange(pieces.reshape(peers, own, packed), ("row", "inner"))
    rows, gates = returned[:, :, :width], returned[:, :, width : width + topk]
    grad_rows = jnp.sum(rows.astype(jnp.float32), axis=0).astype(out_grad.dtype)
    return grad_rows, jnp.sum(gates.astype(jnp.float32), axis=0)


def staged(out_grad, routing_weight, expert_ids, slot_index, w_gate, w_up, w_down, pre_act):
    group_count = lax.axis_size("group")
    inner_count = lax.axis_size("inner")
    own, width = out_grad.shape
    topk = expert_ids.shape[1]
    split_count, experts_here = sizes(group_count, inner_count)
    local_expert = lax.axis_index("inner") // split_count
    block = inner_count * own
    slots = pre_act.shape[1]
    capacity = slots // group_count
    high = -(-(capacity + 1) // 8) * 8

    payload = pack(out_grad, expert_ids, slot_index, routing_weight)
    sent = jnp.broadcast_to(payload[None], (inner_count,) + payload.shape)
    arrived = exchange(sent, "inner").reshape(block, payload.shape[1])
    rows = arrived[:, :width]
    small = arrived[:, width : width + 3 * topk].astype(jnp.float32)
    ids = small[:, :topk].astype(jnp.int32)
    slot = small[:, topk : 2 * topk].astype(jnp.int32)
    weight = small[:, 2 * topk :]
    selected = ids % experts_here == local_expert
    column = ids // experts_here * high + slot
    one_hot = jnp.logical_and(
        column[:, :, None] == jnp.arange(group_count * high, dtype=jnp.int32), selected[:, :, None]
    ).astype(jnp.float32)
    placement = jnp.sum(one_hot, axis=1).astype(jnp.bfloat16)
    send_weight = jnp.sum(one_hot * weight[:, :, None], axis=(0, 1)).reshape(group_count, 1, high)
    send_rows = lax.dot_general(
        placement, rows, (((0,), (0,)), ((), ())), preferred_element_type=jnp.float32
    ).reshape(group_count, high, width)
    last = jnp.arange(high) == high - 1
    weight_row = jnp.pad(send_weight, ((0, 0), (0, 0), (0, width - high)))
    send = jnp.where(last[None, :, None], weight_row, send_rows).astype(jnp.bfloat16)
    buffer = exchange(send, "group")

    buffer_weight = buffer[:, high - 1, :capacity].astype(jnp.float32).reshape(slots, 1)
    buffer_rows = buffer[:, :capacity].reshape(slots, width)
    back_proj = across(buffer_rows, w_down)
    grad_gate, grad_up, gate_piece = gradients(
        back_proj, buffer_weight, pre_act[0].astype(jnp.float32), pre_act[1].astype(jnp.float32)
    )
    pieces = (across(grad_gate, w_gate) + across(grad_up, w_up)).reshape(group_count, capacity, width)
    gate_row = jnp.pad(
        gate_piece.reshape(group_count, 1, capacity), ((0, 0), (0, 0), (0, width - capacity))
    )
    pieces = jnp.pad(pieces, ((0, 0), (0, high - capacity), (0, 0)))
    back = exchange(jnp.where(last[None, :, None], gate_row, pieces).astype(jnp.bfloat16), "group")

    owned = jnp.dot(
        placement, back.reshape(group_count * high, width), preferred_element_type=jnp.float32
    ).astype(jnp.bfloat16)
    gates = back[:, high - 1, :high].reshape(group_count * high).astype(jnp.float32)
    gate_rows = jnp.sum(one_hot * gates, axis=2)
    final = exchange(pack(owned, gate_rows).reshape(inner_count, own, -1), "inner")
    total = jnp.sum(final.astype(jnp.float32), axis=0)
    return total[:, :width].astype(jnp.bfloat16), total[:, width : width + topk]


def solution(mesh):
    if mesh.size <= 64:
        group_count, inner_count = mesh.devices.shape
        devices = mesh.devices.reshape(group_count // CORES, CORES, inner_count)
        mesh, axes, on_device = Mesh(devices, ("row", "core", "inner")), ("row", "core", "inner"), flat
    else:
        axes, on_device = ("group", "inner"), staged
    token, hidden = P(axes, None), P(None, axes)
    return jax.shard_map(
        on_device,
        mesh=mesh,
        in_specs=(token, token, token, token, hidden, hidden, token, P(None, None, axes)),
        out_specs=(token, token),
        check_vma=False,
    )
```

```python
import functools

import jax
import jax.numpy as jnp
from jax import lax
from jax.experimental import pallas as pl
from jax.experimental.pallas import tpu as pltpu
from jax.sharding import Mesh, PartitionSpec as P

LANES = 128
CORES = 2


def exchange(array, axis):
    return lax.all_to_all(array, axis, split_axis=0, concat_axis=0, tiled=True)


def pack(rows, *small):
    width = rows.shape[1]
    behind = sum(s.shape[1] for s in small)
    total = width + behind + -behind % LANES
    packed, at = jnp.pad(rows, ((0, 0), (0, total - width))).astype(jnp.float32), width
    for part in small:
        end = at + part.shape[1]
        wide = jnp.pad(part, ((0, 0), (at, total - end)))
        packed = packed + wide.astype(jnp.float32)
        at = end
    return packed.astype(rows.dtype)


def gradients(back_proj, weight, pre_gate, pre_up):
    gate_sig = jax.nn.sigmoid(pre_gate)
    swish_gate = pre_gate * gate_sig
    gate_piece = jnp.sum(swish_gate * pre_up * back_proj, axis=1, keepdims=True)
    scaled = weight * back_proj
    grad_up = (scaled * swish_gate).astype(jnp.bfloat16)
    grad_gate = (scaled * pre_up * gate_sig * (1.0 + pre_gate * (1.0 - gate_sig))).astype(
        jnp.bfloat16
    )
    return grad_gate, grad_up, gate_piece


def across(a, b):
    return lax.dot_general(a, b, (((1,), (1,)), ((), ())), preferred_element_type=jnp.float32)


def sizes(group_count, inner_count):
    split_count = min(8, inner_count // 4)
    return split_count, inner_count // split_count


def expert_kernel(
    topk, capacity, arrived, w_gate, w_up, w_down, pre_act, gate2, up2, down2, saved2, out, *scratch
):
    gate1, up1, down1, saved1, total, sems = scratch
    copies = [
        pltpu.make_async_copy(source, target, sems.at[at])
        for at, (source, target) in enumerate(
            ((pre_act, saved1), (w_down, down1), (w_gate, gate1), (w_up, up1))
        )
    ]
    for copy in copies:
        copy.start()
    half, packed = arrived.shape
    width = w_gate.shape[0]
    slots = pre_act.shape[1]
    row_count = lax.axis_size("row")
    split_count, experts_here = sizes(row_count * CORES, lax.axis_size("inner"))
    core = lax.axis_index("core")
    group_row = lax.axis_index("row") * CORES
    local_expert = lax.axis_index("inner") // split_count
    small = arrived[:, width:].astype(jnp.float32)
    lane = lax.broadcasted_iota(jnp.int32, small.shape, 1)
    source = lax.broadcasted_iota(jnp.int32, (half, slots), 0) // (half // row_count)
    first = (source * CORES + core) * capacity
    column = lax.broadcasted_iota(jnp.int32, (half, slots), 1)

    def routed(group_core):
        expert = (group_row + group_core) * experts_here + local_expert
        mine = jnp.where(
            jnp.logical_and(small == expert.astype(jnp.float32), lane < topk), 1.0, 0.0
        )
        slot = jnp.sum(pltpu.roll(mine, topk, 1) * small, axis=1, keepdims=True)
        weight = jnp.sum(pltpu.roll(mine, 2 * topk, 1) * small, axis=1, keepdims=True)
        chosen = jnp.sum(mine, axis=1, keepdims=True)
        hit = jnp.logical_and(first + slot.astype(jnp.int32) == column, chosen > 0.5)
        return mine, weight, jnp.where(hit, 1.0, 0.0).astype(jnp.bfloat16)

    def backward(routing, back_proj, saved):
        mine, weight, one_hot = routing
        pre_gate = jnp.dot(one_hot, saved[0], preferred_element_type=jnp.float32)
        pre_up = jnp.dot(one_hot, saved[1], preferred_element_type=jnp.float32)
        grad_gate, grad_up, gate_piece = gradients(back_proj, weight, pre_gate, pre_up)
        return grad_gate, grad_up, mine * gate_piece

    rows = arrived[:, :width]
    other, own = routed(1 - core), routed(core)
    grad_gate, grad_up, gates2 = backward(other, across(rows, down2[...]), saved2)
    grads = jnp.concatenate([grad_gate, grad_up], axis=1)
    step = 512 if width % 512 == 0 else LANES
    spans = [slice(at, at + step) for at in range(0, width, step)]
    for cols in spans:
        both = jnp.concatenate([gate2[cols], up2[cols]], axis=1)
        total[:, cols] = across(grads, both)
    copies[0].wait()
    copies[1].wait()
    grad_gate, grad_up, gates1 = backward(own, across(rows, down1[...]), saved1)
    grads = jnp.concatenate([grad_gate, grad_up], axis=1)
    copies[2].wait()
    copies[3].wait()
    for cols in spans:
        both = jnp.concatenate([gate1[cols], up1[cols]], axis=1)
        out[:, cols] = (total[:, cols] + across(grads, both)).astype(out.dtype)
    out[:, width:] = (gates1 + gates2).astype(out.dtype)


def stay_in(space, *arrays):
    return [pltpu.with_memory_space_constraint(a, space) for a in arrays]


def swap_cores(array):
    return lax.ppermute(array, "core", [(0, 1), (1, 0)])


def flat(out_grad, routing_weight, expert_ids, slot_index, w_gate, w_up, w_down, pre_act):
    row_count = lax.axis_size("row")
    inner_count = lax.axis_size("inner")
    own, width = out_grad.shape
    topk = expert_ids.shape[1]
    peers = row_count * inner_count
    half = peers * own
    capacity = pre_act.shape[1] // (row_count * CORES)
    packed = width + LANES
    in_vmem = pl.BlockSpec(memory_space=pltpu.VMEM)
    in_hbm = pl.BlockSpec(memory_space=pltpu.HBM)

    saved = swap_cores(pre_act)
    payload = pack(out_grad, expert_ids, slot_index, routing_weight)
    payload, *weights = lax.optimization_barrier((payload, w_gate, w_up, w_down))
    swapped = [swap_cores(w) for w in weights]
    payload, saved = lax.optimization_barrier((payload, saved))
    sent = jnp.broadcast_to(payload[None], (peers, own, packed))
    arrived = exchange(sent, ("row", "inner")).reshape(half, packed)
    pieces = pl.pallas_call(
        functools.partial(expert_kernel, topk, capacity),
        out_shape=jax.ShapeDtypeStruct((half, packed), out_grad.dtype),
        in_specs=[in_vmem] + [in_hbm] * 4 + [in_vmem] * 4,
        out_specs=in_vmem,
        scratch_shapes=[pltpu.VMEM(t.shape, t.dtype) for t in (*weights, pre_act)]
        + [pltpu.VMEM((half, width), jnp.float32), pltpu.SemaphoreType.DMA((4,))],
        compiler_params=pltpu.CompilerParams(vmem_limit_bytes=16 * 2**20),
        cost_estimate=pl.CostEstimate(
            flops=12 * half * w_gate.size,
            bytes_accessed=2 * sum(t.nbytes for t in weights) + 2 * arrived.nbytes,
            transcendentals=2 * half * w_gate.shape[1],
        ),
        name="expert_pieces",
    )(
        arrived,
        *stay_in(pltpu.HBM, *weights, pre_act),
        *stay_in(pltpu.VMEM, *swapped, saved),
    )
    returned = exchange(pieces.reshape(peers, own, packed), ("row", "inner"))
    rows, gates = returned[:, :, :width], returned[:, :, width : width + topk]
    grad_rows = jnp.sum(rows.astype(jnp.float32), axis=0).astype(out_grad.dtype)
    return grad_rows, jnp.sum(gates.astype(jnp.float32), axis=0)


def staged(out_grad, routing_weight, expert_ids, slot_index, w_gate, w_up, w_down, pre_act):
    group_count = lax.axis_size("group")
    inner_count = lax.axis_size("inner")
    own, width = out_grad.shape
    topk = expert_ids.shape[1]
    split_count, experts_here = sizes(group_count, inner_count)
    local_expert = lax.axis_index("inner") // split_count
    block = inner_count * own
    slots = pre_act.shape[1]
    capacity = slots // group_count
    high = -(-(capacity + 1) // 8) * 8

    payload = pack(out_grad, expert_ids, slot_index, routing_weight)
    sent = jnp.broadcast_to(payload[None], (inner_count,) + payload.shape)
    arrived = exchange(sent, "inner").reshape(block, payload.shape[1])
    rows = arrived[:, :width]
    small = arrived[:, width : width + 3 * topk].astype(jnp.float32)
    ids = small[:, :topk].astype(jnp.int32)
    slot = small[:, topk : 2 * topk].astype(jnp.int32)
    weight = small[:, 2 * topk :]
    selected = ids % experts_here == local_expert
    column = ids // experts_here * high + slot
    one_hot = jnp.logical_and(
        column[:, :, None] == jnp.arange(group_count * high, dtype=jnp.int32), selected[:, :, None]
    ).astype(jnp.float32)
    placement = jnp.sum(one_hot, axis=1).astype(jnp.bfloat16)
    send_weight = jnp.sum(one_hot * weight[:, :, None], axis=(0, 1)).reshape(group_count, 1, high)
    send_rows = lax.dot_general(
        placement, rows, (((0,), (0,)), ((), ())), preferred_element_type=jnp.float32
    ).reshape(group_count, high, width)
    last = jnp.arange(high) == high - 1
    weight_row = jnp.pad(send_weight, ((0, 0), (0, 0), (0, width - high)))
    send = jnp.where(last[None, :, None], weight_row, send_rows).astype(jnp.bfloat16)
    buffer = exchange(send, "group")

    buffer_weight = buffer[:, high - 1, :capacity].astype(jnp.float32).reshape(slots, 1)
    buffer_rows = buffer[:, :capacity].reshape(slots, width)
    back_proj = across(buffer_rows, w_down)
    grad_gate, grad_up, gate_piece = gradients(
        back_proj, buffer_weight, pre_act[0].astype(jnp.float32), pre_act[1].astype(jnp.float32)
    )
    pieces = (across(grad_gate, w_gate) + across(grad_up, w_up)).reshape(group_count, capacity, width)
    gate_row = jnp.pad(
        gate_piece.reshape(group_count, 1, capacity), ((0, 0), (0, 0), (0, width - capacity))
    )
    pieces = jnp.pad(pieces, ((0, 0), (0, high - capacity), (0, 0)))
    back = exchange(jnp.where(last[None, :, None], gate_row, pieces).astype(jnp.bfloat16), "group")

    owned = jnp.dot(
        placement, back.reshape(group_count * high, width), preferred_element_type=jnp.float32
    ).astype(jnp.bfloat16)
    gates = back[:, high - 1, :high].reshape(group_count * high).astype(jnp.float32)
    gate_rows = jnp.sum(one_hot * gates, axis=2)
    final = exchange(pack(owned, gate_rows).reshape(inner_count, own, -1), "inner")
    total = jnp.sum(final.astype(jnp.float32), axis=0)
    return total[:, :width].astype(jnp.bfloat16), total[:, width : width + topk]


def solution(mesh):
    if mesh.size <= 64:
        group_count, inner_count = mesh.devices.shape
        devices = mesh.devices.reshape(group_count // CORES, CORES, inner_count)
        mesh, axes, on_device = Mesh(devices, ("row", "core", "inner")), ("row", "core", "inner"), flat
    else:
        axes, on_device = ("group", "inner"), staged
    token, hidden = P(axes, None), P(None, axes)
    return jax.shard_map(
        on_device,
        mesh=mesh,
        in_specs=(token, token, token, token, hidden, hidden, token, P(None, None, axes)),
        out_specs=(token, token),
        check_vma=False,
    )
```

```python
import functools

import jax
import jax.numpy as jnp
from jax import lax
from jax.experimental import pallas as pl
from jax.experimental.pallas import tpu as pltpu
from jax.sharding import Mesh, PartitionSpec as P

LANES = 128
CORES = 2
SAVED_ROWS = 32


def exchange(array, axis):
    return lax.all_to_all(array, axis, split_axis=0, concat_axis=0, tiled=True)


def pack(rows, *small):
    width = sum(s.shape[1] for s in small)
    fill = jnp.zeros((rows.shape[0], -width % LANES), rows.dtype)
    return jnp.concatenate([rows, *(s.astype(rows.dtype) for s in small), fill], axis=1)


def gradients(back_proj, weight, pre_gate, pre_up):
    gate_sig = jax.nn.sigmoid(pre_gate)
    swish_gate = pre_gate * gate_sig
    gate_piece = jnp.sum(swish_gate * pre_up * back_proj, axis=1, keepdims=True)
    scaled = weight * back_proj
    grad_up = (scaled * swish_gate).astype(jnp.bfloat16)
    grad_gate = (scaled * pre_up * gate_sig * (1.0 + pre_gate * (1.0 - gate_sig))).astype(
        jnp.bfloat16
    )
    return grad_gate, grad_up, gate_piece


def across(a, b):
    return lax.dot_general(a, b, (((1,), (1,)), ((), ())), preferred_element_type=jnp.float32)


def sizes(group_count, inner_count):
    split_count = min(8, inner_count // 4)
    return split_count, inner_count // split_count


def pack_kernel(
    out_grad, ids, slots, weights, w_gate, w_up, w_down, pre_act,
    sent, both, down, rows, words, reals, saved, small, sems,
):
    width, topk = w_gate.shape[0], ids.shape[1]
    copies = [
        pltpu.make_async_copy(source, target, sems.at[at])
        for at, (source, target) in enumerate(
            (
                (ids, words.at[0]),
                (slots, words.at[1]),
                (weights, reals),
                (out_grad, rows),
                (pre_act, saved),
                (w_gate, both.at[:width]),
                (w_up, both.at[width : 2 * width]),
                (w_down, down),
            )
        )
    ]
    for copy in copies:
        copy.start()
    small[...] = jnp.zeros_like(small)
    both[2 * width :] = jnp.zeros((both.shape[0] - 2 * width, both.shape[1]), both.dtype)
    for copy in copies[:5]:
        copy.wait()
    for at, part in enumerate((words[0], words[1], reals[...])):
        small[:, at * topk : (at + 1) * topk] = part.astype(jnp.float32)
    tail = small[...].astype(sent.dtype)
    own_rows = rows[...]
    for peer in range(sent.shape[0]):
        sent[peer, :, :width] = own_rows
        sent[peer, :, width:] = tail
    for at in range(2):
        first = 2 * width + at * SAVED_ROWS
        both[first : first + saved.shape[1]] = saved[at]
    for copy in copies[5:]:
        copy.wait()


def expert_kernel(topk, slots, arrived, both1, down1, both2, down2, out):
    half, packed = arrived.shape
    width = packed - LANES
    row_count = lax.axis_size("row")
    capacity = slots // (row_count * CORES)
    split_count, experts_here = sizes(row_count * CORES, lax.axis_size("inner"))
    core = lax.axis_index("core")
    group_row = lax.axis_index("row") * CORES
    local_expert = lax.axis_index("inner") // split_count
    small = arrived[:, width:].astype(jnp.float32)
    lane = lax.broadcasted_iota(jnp.int32, small.shape, 1)
    source = lax.broadcasted_iota(jnp.int32, (half, slots), 0) // (half // row_count)
    first = (source * CORES + core) * capacity
    column = lax.broadcasted_iota(jnp.int32, (half, slots), 1)

    def routed(group_core):
        expert = (group_row + group_core) * experts_here + local_expert
        mine = jnp.where(
            jnp.logical_and(small == expert.astype(jnp.float32), lane < topk), 1.0, 0.0
        )
        slot = jnp.sum(pltpu.roll(mine, topk, 1) * small, axis=1, keepdims=True)
        weight = jnp.sum(pltpu.roll(mine, 2 * topk, 1) * small, axis=1, keepdims=True)
        chosen = jnp.sum(mine, axis=1, keepdims=True)
        hit = jnp.logical_and(first + slot.astype(jnp.int32) == column, chosen > 0.5)
        return mine, weight, jnp.where(hit, 1.0, 0.0).astype(jnp.bfloat16)

    def backward(routing, back_proj, both):
        mine, weight, one_hot = routing
        pre_gate, pre_up = [
            jnp.dot(
                one_hot,
                both[2 * width + at * SAVED_ROWS : 2 * width + at * SAVED_ROWS + slots],
                preferred_element_type=jnp.float32,
            )
            for at in range(2)
        ]
        grad_gate, grad_up, gate_piece = gradients(back_proj, weight, pre_gate, pre_up)
        return grad_gate, grad_up, mine * gate_piece

    rows = arrived[:, :width]
    own, other = routed(core), routed(1 - core)
    grad_gate1, grad_up1, gates1 = backward(own, across(rows, down1[...]), both1)
    grad_gate2, grad_up2, gates2 = backward(other, across(rows, down2[...]), both2)
    grads = jnp.concatenate([grad_gate1, grad_up1, grad_gate2, grad_up2], axis=1)
    step = 512 if width % 512 == 0 else LANES
    for at in range(0, width, step):
        weights = [b[first + at : first + at + step] for b in (both1, both2) for first in (0, width)]
        pieces = across(grads, jnp.concatenate(weights, axis=1))
        out[:, at : at + step] = pieces.astype(out.dtype)
    out[:, width:] = (gates1 + gates2).astype(out.dtype)


def stay_in(space, *arrays):
    return [pltpu.with_memory_space_constraint(a, space) for a in arrays]


def swap_cores(array):
    return lax.ppermute(array, "core", [(0, 1), (1, 0)])


def flat(out_grad, routing_weight, expert_ids, slot_index, w_gate, w_up, w_down, pre_act):
    row_count = lax.axis_size("row")
    inner_count = lax.axis_size("inner")
    own, width = out_grad.shape
    topk = expert_ids.shape[1]
    peers = row_count * inner_count
    half = peers * own
    slots, hidden = pre_act.shape[1:]
    packed = width + LANES
    in_vmem = pl.BlockSpec(memory_space=pltpu.VMEM)
    in_hbm = pl.BlockSpec(memory_space=pltpu.HBM)
    bf16 = out_grad.dtype

    sent, both, down = pl.pallas_call(
        pack_kernel,
        out_shape=[
            jax.ShapeDtypeStruct((peers, own, packed), bf16),
            jax.ShapeDtypeStruct((2 * width + 2 * SAVED_ROWS, hidden), bf16),
            jax.ShapeDtypeStruct(w_down.shape, bf16),
        ],
        in_specs=[in_hbm] * 8,
        out_specs=[in_vmem] * 3,
        scratch_shapes=[
            pltpu.VMEM((own, width), bf16),
            pltpu.VMEM((2, own, topk), expert_ids.dtype),
            pltpu.VMEM((own, topk), bf16),
            pltpu.VMEM(pre_act.shape, bf16),
            pltpu.VMEM((own, LANES), jnp.float32),
            pltpu.SemaphoreType.DMA((8,)),
        ],
        name="pack_rows",
    )(
        *stay_in(
            pltpu.HBM,
            *(out_grad, expert_ids, slot_index, routing_weight),
            *(w_gate, w_up, w_down, pre_act),
        )
    )
    both2, down2 = swap_cores(both), swap_cores(down)
    arrived = exchange(sent, ("row", "inner")).reshape(half, packed)
    pieces = pl.pallas_call(
        functools.partial(expert_kernel, topk, slots),
        out_shape=jax.ShapeDtypeStruct((half, packed), bf16),
        in_specs=[in_vmem] * 5,
        out_specs=in_vmem,
        compiler_params=pltpu.CompilerParams(vmem_limit_bytes=16 * 2**20),
        cost_estimate=pl.CostEstimate(
            flops=12 * half * w_down.size,
            bytes_accessed=2 * (both.nbytes + down.nbytes + arrived.nbytes),
            transcendentals=2 * half * hidden,
        ),
        name="expert_pieces",
    )(arrived, both, down, both2, down2)
    returned = exchange(pieces.reshape(peers, own, packed), ("row", "inner"))
    rows, gates = returned[:, :, :width], returned[:, :, width : width + topk]
    grad_rows = jnp.sum(rows.astype(jnp.float32), axis=0).astype(out_grad.dtype)
    return grad_rows, jnp.sum(gates.astype(jnp.float32), axis=0)


def staged(out_grad, routing_weight, expert_ids, slot_index, w_gate, w_up, w_down, pre_act):
    group_count = lax.axis_size("group")
    inner_count = lax.axis_size("inner")
    own, width = out_grad.shape
    topk = expert_ids.shape[1]
    split_count, experts_here = sizes(group_count, inner_count)
    local_expert = lax.axis_index("inner") // split_count
    block = inner_count * own
    slots = pre_act.shape[1]
    capacity = slots // group_count
    high = -(-(capacity + 1) // 8) * 8

    payload = pack(out_grad, expert_ids, slot_index, routing_weight)
    sent = jnp.broadcast_to(payload[None], (inner_count,) + payload.shape)
    arrived = exchange(sent, "inner").reshape(block, payload.shape[1])
    rows = arrived[:, :width]
    small = arrived[:, width : width + 3 * topk].astype(jnp.float32)
    ids = small[:, :topk].astype(jnp.int32)
    slot = small[:, topk : 2 * topk].astype(jnp.int32)
    weight = small[:, 2 * topk :]
    selected = ids % experts_here == local_expert
    column = ids // experts_here * high + slot
    one_hot = jnp.logical_and(
        column[:, :, None] == jnp.arange(group_count * high, dtype=jnp.int32), selected[:, :, None]
    ).astype(jnp.float32)
    placement = jnp.sum(one_hot, axis=1).astype(jnp.bfloat16)
    send_weight = jnp.sum(one_hot * weight[:, :, None], axis=(0, 1)).reshape(group_count, 1, high)
    send_rows = lax.dot_general(
        placement, rows, (((0,), (0,)), ((), ())), preferred_element_type=jnp.float32
    ).reshape(group_count, high, width)
    last = jnp.arange(high) == high - 1
    weight_row = jnp.pad(send_weight, ((0, 0), (0, 0), (0, width - high)))
    send = jnp.where(last[None, :, None], weight_row, send_rows).astype(jnp.bfloat16)
    buffer = exchange(send, "group")

    buffer_weight = buffer[:, high - 1, :capacity].astype(jnp.float32).reshape(slots, 1)
    buffer_rows = buffer[:, :capacity].reshape(slots, width)
    back_proj = across(buffer_rows, w_down)
    grad_gate, grad_up, gate_piece = gradients(
        back_proj, buffer_weight, pre_act[0].astype(jnp.float32), pre_act[1].astype(jnp.float32)
    )
    pieces = (across(grad_gate, w_gate) + across(grad_up, w_up)).reshape(group_count, capacity, width)
    gate_row = jnp.pad(
        gate_piece.reshape(group_count, 1, capacity), ((0, 0), (0, 0), (0, width - capacity))
    )
    pieces = jnp.pad(pieces, ((0, 0), (0, high - capacity), (0, 0)))
    back = exchange(jnp.where(last[None, :, None], gate_row, pieces).astype(jnp.bfloat16), "group")

    owned = jnp.dot(
        placement, back.reshape(group_count * high, width), preferred_element_type=jnp.float32
    ).astype(jnp.bfloat16)
    gates = back[:, high - 1, :high].reshape(group_count * high).astype(jnp.float32)
    gate_rows = jnp.sum(one_hot * gates, axis=2)
    final = exchange(pack(owned, gate_rows).reshape(inner_count, own, -1), "inner")
    total = jnp.sum(final.astype(jnp.float32), axis=0)
    return total[:, :width].astype(jnp.bfloat16), total[:, width : width + topk]


def solution(mesh):
    if mesh.size <= 64:
        group_count, inner_count = mesh.devices.shape
        devices = mesh.devices.reshape(group_count // CORES, CORES, inner_count)
        mesh, axes, on_device = Mesh(devices, ("row", "core", "inner")), ("row", "core", "inner"), flat
    else:
        axes, on_device = ("group", "inner"), staged
    token, hidden = P(axes, None), P(None, axes)
    return jax.shard_map(
        on_device,
        mesh=mesh,
        in_specs=(token, token, token, token, hidden, hidden, token, P(None, None, axes)),
        out_specs=(token, token),
        check_vma=False,
    )
```

```python
import functools

import jax
import jax.numpy as jnp
from jax import lax
from jax.experimental import pallas as pl
from jax.experimental.pallas import tpu as pltpu
from jax.sharding import Mesh, PartitionSpec as P

LANES = 128
CORES = 2
SAVED_ROWS = 32


def exchange(array, axis):
    return lax.all_to_all(array, axis, split_axis=0, concat_axis=0, tiled=True)


def pack(rows, *small):
    width = sum(s.shape[1] for s in small)
    fill = jnp.zeros((rows.shape[0], -width % LANES), rows.dtype)
    return jnp.concatenate([rows, *(s.astype(rows.dtype) for s in small), fill], axis=1)


def gradients(back_proj, weight, pre_gate, pre_up):
    gate_sig = jax.nn.sigmoid(pre_gate)
    swish_gate = pre_gate * gate_sig
    gate_piece = jnp.sum(swish_gate * pre_up * back_proj, axis=1, keepdims=True)
    scaled = weight * back_proj
    grad_up = (scaled * swish_gate).astype(jnp.bfloat16)
    grad_gate = (scaled * pre_up * gate_sig * (1.0 + pre_gate * (1.0 - gate_sig))).astype(
        jnp.bfloat16
    )
    return grad_gate, grad_up, gate_piece


def across(a, b):
    return lax.dot_general(a, b, (((1,), (1,)), ((), ())), preferred_element_type=jnp.float32)


def sizes(group_count, inner_count):
    split_count = min(8, inner_count // 4)
    return split_count, inner_count // split_count


def pack_kernel(
    out_grad, ids, slots, weights, w_gate, w_up, w_down, pre_act,
    sent, both, down, rows, words, reals, saved, small, sems,
):
    width, topk = w_gate.shape[0], ids.shape[1]
    copies = [
        pltpu.make_async_copy(source, target, sems.at[at])
        for at, (source, target) in enumerate(
            (
                (ids, words.at[0]),
                (slots, words.at[1]),
                (weights, reals),
                (out_grad, rows),
                (pre_act, saved),
                (w_gate, both.at[:width]),
                (w_up, both.at[width : 2 * width]),
                (w_down, down),
            )
        )
    ]
    for copy in copies:
        copy.start()
    small[...] = jnp.zeros_like(small)
    both[2 * width :] = jnp.zeros((both.shape[0] - 2 * width, both.shape[1]), both.dtype)
    for copy in copies[:5]:
        copy.wait()
    for at, part in enumerate((words[0], words[1], reals[...])):
        small[:, at * topk : (at + 1) * topk] = part.astype(jnp.float32)
    tail = small[...].astype(sent.dtype)
    own_rows = rows[...]
    for peer in range(sent.shape[0]):
        sent[peer, :, :width] = own_rows
        sent[peer, :, width:] = tail
    for at in range(2):
        first = 2 * width + at * SAVED_ROWS
        both[first : first + saved.shape[1]] = saved[at]
    for copy in copies[5:]:
        copy.wait()


def expert_kernel(topk, slots, arrived, both1, down1, both2, down2, out):
    half, packed = arrived.shape
    width = packed - LANES
    row_count = lax.axis_size("row")
    capacity = slots // (row_count * CORES)
    split_count, experts_here = sizes(row_count * CORES, lax.axis_size("inner"))
    core = lax.axis_index("core")
    group_row = lax.axis_index("row") * CORES
    local_expert = lax.axis_index("inner") // split_count
    small = arrived[:, width:].astype(jnp.float32)
    lane = lax.broadcasted_iota(jnp.int32, small.shape, 1)
    source = lax.broadcasted_iota(jnp.int32, (half, slots), 0) // (half // row_count)
    first = (source * CORES + core) * capacity
    column = lax.broadcasted_iota(jnp.int32, (half, slots), 1)

    def routed(group_core):
        expert = (group_row + group_core) * experts_here + local_expert
        mine = jnp.where(
            jnp.logical_and(small == expert.astype(jnp.float32), lane < topk), 1.0, 0.0
        )
        slot = jnp.sum(pltpu.roll(mine, topk, 1) * small, axis=1, keepdims=True)
        weight = jnp.sum(pltpu.roll(mine, 2 * topk, 1) * small, axis=1, keepdims=True)
        chosen = jnp.sum(mine, axis=1, keepdims=True)
        hit = jnp.logical_and(first + slot.astype(jnp.int32) == column, chosen > 0.5)
        return mine, weight, jnp.where(hit, 1.0, 0.0).astype(jnp.bfloat16)

    def backward(routing, back_proj, both):
        mine, weight, one_hot = routing
        pre_gate, pre_up = [
            jnp.dot(
                one_hot,
                both[2 * width + at * SAVED_ROWS : 2 * width + at * SAVED_ROWS + slots],
                preferred_element_type=jnp.float32,
            )
            for at in range(2)
        ]
        grad_gate, grad_up, gate_piece = gradients(back_proj, weight, pre_gate, pre_up)
        return grad_gate, grad_up, mine * gate_piece

    rows = arrived[:, :width]
    own, other = routed(core), routed(1 - core)
    grad_gate1, grad_up1, gates1 = backward(own, across(rows, down1[...]), both1)
    grad_gate2, grad_up2, gates2 = backward(other, across(rows, down2[...]), both2)
    grads = jnp.concatenate([grad_gate1, grad_up1, grad_gate2, grad_up2], axis=1)
    step = 512 if width % 512 == 0 else LANES
    for at in range(0, width, step):
        weights = [b[first + at : first + at + step] for b in (both1, both2) for first in (0, width)]
        pieces = across(grads, jnp.concatenate(weights, axis=1))
        out[:, at : at + step] = pieces.astype(out.dtype)
    out[:, width:] = (gates1 + gates2).astype(out.dtype)


def stay_in(space, *arrays):
    return [pltpu.with_memory_space_constraint(a, space) for a in arrays]


def swap_cores(array):
    return lax.ppermute(array, "core", [(0, 1), (1, 0)])


def flat(out_grad, routing_weight, expert_ids, slot_index, w_gate, w_up, w_down, pre_act):
    row_count = lax.axis_size("row")
    inner_count = lax.axis_size("inner")
    own, width = out_grad.shape
    topk = expert_ids.shape[1]
    peers = row_count * inner_count
    half = peers * own
    slots, hidden = pre_act.shape[1:]
    packed = width + LANES
    in_vmem = pl.BlockSpec(memory_space=pltpu.VMEM)
    in_hbm = pl.BlockSpec(memory_space=pltpu.HBM)
    bf16 = out_grad.dtype

    sent, both, down = pl.pallas_call(
        pack_kernel,
        out_shape=[
            jax.ShapeDtypeStruct((peers, own, packed), bf16),
            pltpu.VMEM((2 * width + 2 * SAVED_ROWS, hidden), bf16),
            pltpu.VMEM(w_down.shape, bf16),
        ],
        in_specs=[in_hbm] * 8,
        out_specs=[in_vmem] * 3,
        scratch_shapes=[
            pltpu.VMEM((own, width), bf16),
            pltpu.VMEM((2, own, topk), expert_ids.dtype),
            pltpu.VMEM((own, topk), bf16),
            pltpu.VMEM(pre_act.shape, bf16),
            pltpu.VMEM((own, LANES), jnp.float32),
            pltpu.SemaphoreType.DMA((8,)),
        ],
        name="pack_rows",
    )(
        *stay_in(
            pltpu.HBM,
            *(out_grad, expert_ids, slot_index, routing_weight),
            *(w_gate, w_up, w_down, pre_act),
        )
    )
    both2, down2 = swap_cores(both), swap_cores(down)
    arrived = exchange(sent, ("row", "inner")).reshape(half, packed)
    pieces = pl.pallas_call(
        functools.partial(expert_kernel, topk, slots),
        out_shape=jax.ShapeDtypeStruct((half, packed), bf16),
        in_specs=[in_vmem] * 5,
        out_specs=in_vmem,
        compiler_params=pltpu.CompilerParams(vmem_limit_bytes=16 * 2**20),
        cost_estimate=pl.CostEstimate(
            flops=12 * half * w_down.size,
            bytes_accessed=2 * (both.nbytes + down.nbytes + arrived.nbytes),
            transcendentals=2 * half * hidden,
        ),
        name="expert_pieces",
    )(arrived, *stay_in(pltpu.VMEM, both, down, both2, down2))
    returned = exchange(pieces.reshape(peers, own, packed), ("row", "inner"))
    rows, gates = returned[:, :, :width], returned[:, :, width : width + topk]
    grad_rows = jnp.sum(rows.astype(jnp.float32), axis=0).astype(out_grad.dtype)
    return grad_rows, jnp.sum(gates.astype(jnp.float32), axis=0)


def staged(out_grad, routing_weight, expert_ids, slot_index, w_gate, w_up, w_down, pre_act):
    group_count = lax.axis_size("group")
    inner_count = lax.axis_size("inner")
    own, width = out_grad.shape
    topk = expert_ids.shape[1]
    split_count, experts_here = sizes(group_count, inner_count)
    local_expert = lax.axis_index("inner") // split_count
    block = inner_count * own
    slots = pre_act.shape[1]
    capacity = slots // group_count
    high = -(-(capacity + 1) // 8) * 8

    payload = pack(out_grad, expert_ids, slot_index, routing_weight)
    sent = jnp.broadcast_to(payload[None], (inner_count,) + payload.shape)
    arrived = exchange(sent, "inner").reshape(block, payload.shape[1])
    rows = arrived[:, :width]
    small = arrived[:, width : width + 3 * topk].astype(jnp.float32)
    ids = small[:, :topk].astype(jnp.int32)
    slot = small[:, topk : 2 * topk].astype(jnp.int32)
    weight = small[:, 2 * topk :]
    selected = ids % experts_here == local_expert
    column = ids // experts_here * high + slot
    one_hot = jnp.logical_and(
        column[:, :, None] == jnp.arange(group_count * high, dtype=jnp.int32), selected[:, :, None]
    ).astype(jnp.float32)
    placement = jnp.sum(one_hot, axis=1).astype(jnp.bfloat16)
    send_weight = jnp.sum(one_hot * weight[:, :, None], axis=(0, 1)).reshape(group_count, 1, high)
    send_rows = lax.dot_general(
        placement, rows, (((0,), (0,)), ((), ())), preferred_element_type=jnp.float32
    ).reshape(group_count, high, width)
    last = jnp.arange(high) == high - 1
    weight_row = jnp.pad(send_weight, ((0, 0), (0, 0), (0, width - high)))
    send = jnp.where(last[None, :, None], weight_row, send_rows).astype(jnp.bfloat16)
    buffer = exchange(send, "group")

    buffer_weight = buffer[:, high - 1, :capacity].astype(jnp.float32).reshape(slots, 1)
    buffer_rows = buffer[:, :capacity].reshape(slots, width)
    back_proj = across(buffer_rows, w_down)
    grad_gate, grad_up, gate_piece = gradients(
        back_proj, buffer_weight, pre_act[0].astype(jnp.float32), pre_act[1].astype(jnp.float32)
    )
    pieces = (across(grad_gate, w_gate) + across(grad_up, w_up)).reshape(group_count, capacity, width)
    gate_row = jnp.pad(
        gate_piece.reshape(group_count, 1, capacity), ((0, 0), (0, 0), (0, width - capacity))
    )
    pieces = jnp.pad(pieces, ((0, 0), (0, high - capacity), (0, 0)))
    back = exchange(jnp.where(last[None, :, None], gate_row, pieces).astype(jnp.bfloat16), "group")

    owned = jnp.dot(
        placement, back.reshape(group_count * high, width), preferred_element_type=jnp.float32
    ).astype(jnp.bfloat16)
    gates = back[:, high - 1, :high].reshape(group_count * high).astype(jnp.float32)
    gate_rows = jnp.sum(one_hot * gates, axis=2)
    final = exchange(pack(owned, gate_rows).reshape(inner_count, own, -1), "inner")
    total = jnp.sum(final.astype(jnp.float32), axis=0)
    return total[:, :width].astype(jnp.bfloat16), total[:, width : width + topk]


def solution(mesh):
    if mesh.size <= 64:
        group_count, inner_count = mesh.devices.shape
        devices = mesh.devices.reshape(group_count // CORES, CORES, inner_count)
        mesh, axes, on_device = Mesh(devices, ("row", "core", "inner")), ("row", "core", "inner"), flat
    else:
        axes, on_device = ("group", "inner"), staged
    token, hidden = P(axes, None), P(None, axes)
    return jax.shard_map(
        on_device,
        mesh=mesh,
        in_specs=(token, token, token, token, hidden, hidden, token, P(None, None, axes)),
        out_specs=(token, token),
        check_vma=False,
    )
```

```python
import functools

import jax
import jax.numpy as jnp
from jax import lax
from jax.experimental import pallas as pl
from jax.experimental.pallas import tpu as pltpu
from jax.sharding import Mesh, PartitionSpec as P

LANES = 128
CORES = 2
SAVED_ROWS = 32


def exchange(array, axis):
    return lax.all_to_all(array, axis, split_axis=0, concat_axis=0, tiled=True)


def pack(rows, *small):
    width = sum(s.shape[1] for s in small)
    fill = jnp.zeros((rows.shape[0], -width % LANES), rows.dtype)
    return jnp.concatenate([rows, *(s.astype(rows.dtype) for s in small), fill], axis=1)


def gradients(back_proj, weight, pre_gate, pre_up):
    gate_sig = jax.nn.sigmoid(pre_gate)
    swish_gate = pre_gate * gate_sig
    gate_piece = jnp.sum(swish_gate * pre_up * back_proj, axis=1, keepdims=True)
    scaled = weight * back_proj
    grad_up = (scaled * swish_gate).astype(jnp.bfloat16)
    grad_gate = (scaled * pre_up * gate_sig * (1.0 + pre_gate * (1.0 - gate_sig))).astype(
        jnp.bfloat16
    )
    return grad_gate, grad_up, gate_piece


def across(a, b):
    return lax.dot_general(a, b, (((1,), (1,)), ((), ())), preferred_element_type=jnp.float32)


def sizes(group_count, inner_count):
    split_count = min(8, inner_count // 4)
    return split_count, inner_count // split_count


def pack_kernel(
    out_grad, ids, slots, weights, w_gate, w_up, w_down, pre_act,
    sent, both, down, words, reals, saved, small, sems,
):
    width, topk = w_gate.shape[0], ids.shape[1]
    copies = [
        pltpu.make_async_copy(source, target, sems.at[at])
        for at, (source, target) in enumerate(
            (
                (ids, words.at[0]),
                (slots, words.at[1]),
                (weights, reals),
                (pre_act, saved),
                *((out_grad, sent.at[peer, :, :width]) for peer in range(sent.shape[0])),
                (w_gate, both.at[:width]),
                (w_up, both.at[width : 2 * width]),
                (w_down, down),
            )
        )
    ]
    for copy in copies:
        copy.start()
    small[...] = jnp.zeros_like(small)
    both[2 * width :] = jnp.zeros((both.shape[0] - 2 * width, both.shape[1]), both.dtype)
    for copy in copies[:4]:
        copy.wait()
    for at, part in enumerate((words[0], words[1], reals[...])):
        small[:, at * topk : (at + 1) * topk] = part.astype(jnp.float32)
    tail = small[...].astype(sent.dtype)
    for peer in range(sent.shape[0]):
        sent[peer, :, width:] = tail
    for at in range(2):
        first = 2 * width + at * SAVED_ROWS
        both[first : first + saved.shape[1]] = saved[at]
    for copy in copies[4:]:
        copy.wait()


def expert_kernel(topk, slots, arrived, both1, down1, both2, down2, out):
    half, packed = arrived.shape
    width = packed - LANES
    row_count = lax.axis_size("row")
    capacity = slots // (row_count * CORES)
    split_count, experts_here = sizes(row_count * CORES, lax.axis_size("inner"))
    core = lax.axis_index("core")
    group_row = lax.axis_index("row") * CORES
    local_expert = lax.axis_index("inner") // split_count
    small = arrived[:, width:].astype(jnp.float32)
    lane = lax.broadcasted_iota(jnp.int32, small.shape, 1)
    source = lax.broadcasted_iota(jnp.int32, (half, slots), 0) // (half // row_count)
    first = (source * CORES + core) * capacity
    column = lax.broadcasted_iota(jnp.int32, (half, slots), 1)

    def routed(group_core):
        expert = (group_row + group_core) * experts_here + local_expert
        mine = jnp.where(
            jnp.logical_and(small == expert.astype(jnp.float32), lane < topk), 1.0, 0.0
        )
        slot = jnp.sum(pltpu.roll(mine, topk, 1) * small, axis=1, keepdims=True)
        weight = jnp.sum(pltpu.roll(mine, 2 * topk, 1) * small, axis=1, keepdims=True)
        chosen = jnp.sum(mine, axis=1, keepdims=True)
        hit = jnp.logical_and(first + slot.astype(jnp.int32) == column, chosen > 0.5)
        return mine, weight, jnp.where(hit, 1.0, 0.0).astype(jnp.bfloat16)

    def backward(routing, back_proj, both):
        mine, weight, one_hot = routing
        pre_gate, pre_up = [
            jnp.dot(
                one_hot,
                both[2 * width + at * SAVED_ROWS : 2 * width + at * SAVED_ROWS + slots],
                preferred_element_type=jnp.float32,
            )
            for at in range(2)
        ]
        grad_gate, grad_up, gate_piece = gradients(back_proj, weight, pre_gate, pre_up)
        return grad_gate, grad_up, mine * gate_piece

    rows = arrived[:, :width]
    own, other = routed(core), routed(1 - core)
    grad_gate1, grad_up1, gates1 = backward(own, across(rows, down1[...]), both1)
    grad_gate2, grad_up2, gates2 = backward(other, across(rows, down2[...]), both2)
    grads = jnp.concatenate([grad_gate1, grad_up1, grad_gate2, grad_up2], axis=1)
    step = 512 if width % 512 == 0 else LANES
    for at in range(0, width, step):
        weights = [b[first + at : first + at + step] for b in (both1, both2) for first in (0, width)]
        pieces = across(grads, jnp.concatenate(weights, axis=1))
        out[:, at : at + step] = pieces.astype(out.dtype)
    out[:, width:] = (gates1 + gates2).astype(out.dtype)


def stay_in(space, *arrays):
    return [pltpu.with_memory_space_constraint(a, space) for a in arrays]


def swap_cores(array):
    return lax.ppermute(array, "core", [(0, 1), (1, 0)])


def flat(out_grad, routing_weight, expert_ids, slot_index, w_gate, w_up, w_down, pre_act):
    row_count = lax.axis_size("row")
    inner_count = lax.axis_size("inner")
    own, width = out_grad.shape
    topk = expert_ids.shape[1]
    peers = row_count * inner_count
    half = peers * own
    slots, hidden = pre_act.shape[1:]
    packed = width + LANES
    in_vmem = pl.BlockSpec(memory_space=pltpu.VMEM)
    in_hbm = pl.BlockSpec(memory_space=pltpu.HBM)
    bf16 = out_grad.dtype

    sent, both, down = pl.pallas_call(
        pack_kernel,
        out_shape=[
            jax.ShapeDtypeStruct((peers, own, packed), bf16),
            pltpu.VMEM((2 * width + 2 * SAVED_ROWS, hidden), bf16),
            pltpu.VMEM(w_down.shape, bf16),
        ],
        in_specs=[in_hbm] * 8,
        out_specs=[in_vmem] * 3,
        scratch_shapes=[
            pltpu.VMEM((2, own, topk), expert_ids.dtype),
            pltpu.VMEM((own, topk), bf16),
            pltpu.VMEM(pre_act.shape, bf16),
            pltpu.VMEM((own, LANES), jnp.float32),
            pltpu.SemaphoreType.DMA((7 + peers,)),
        ],
        name="pack_rows",
    )(
        *stay_in(
            pltpu.HBM,
            *(out_grad, expert_ids, slot_index, routing_weight),
            *(w_gate, w_up, w_down, pre_act),
        )
    )
    both2, down2 = swap_cores(both), swap_cores(down)
    arrived = exchange(sent, ("row", "inner")).reshape(half, packed)
    pieces = pl.pallas_call(
        functools.partial(expert_kernel, topk, slots),
        out_shape=jax.ShapeDtypeStruct((half, packed), bf16),
        in_specs=[in_vmem] * 5,
        out_specs=in_vmem,
        compiler_params=pltpu.CompilerParams(vmem_limit_bytes=16 * 2**20),
        cost_estimate=pl.CostEstimate(
            flops=12 * half * w_down.size,
            bytes_accessed=2 * (both.nbytes + down.nbytes + arrived.nbytes),
            transcendentals=2 * half * hidden,
        ),
        name="expert_pieces",
    )(arrived, both, down, both2, down2)
    returned = exchange(pieces.reshape(peers, own, packed), ("row", "inner"))
    rows, gates = returned[:, :, :width], returned[:, :, width : width + topk]
    grad_rows = jnp.sum(rows.astype(jnp.float32), axis=0).astype(out_grad.dtype)
    return grad_rows, jnp.sum(gates.astype(jnp.float32), axis=0)


def staged(out_grad, routing_weight, expert_ids, slot_index, w_gate, w_up, w_down, pre_act):
    group_count = lax.axis_size("group")
    inner_count = lax.axis_size("inner")
    own, width = out_grad.shape
    topk = expert_ids.shape[1]
    split_count, experts_here = sizes(group_count, inner_count)
    local_expert = lax.axis_index("inner") // split_count
    block = inner_count * own
    slots = pre_act.shape[1]
    capacity = slots // group_count
    high = -(-(capacity + 1) // 8) * 8

    payload = pack(out_grad, expert_ids, slot_index, routing_weight)
    sent = jnp.broadcast_to(payload[None], (inner_count,) + payload.shape)
    arrived = exchange(sent, "inner").reshape(block, payload.shape[1])
    rows = arrived[:, :width]
    small = arrived[:, width : width + 3 * topk].astype(jnp.float32)
    ids = small[:, :topk].astype(jnp.int32)
    slot = small[:, topk : 2 * topk].astype(jnp.int32)
    weight = small[:, 2 * topk :]
    selected = ids % experts_here == local_expert
    column = ids // experts_here * high + slot
    one_hot = jnp.logical_and(
        column[:, :, None] == jnp.arange(group_count * high, dtype=jnp.int32), selected[:, :, None]
    ).astype(jnp.float32)
    placement = jnp.sum(one_hot, axis=1).astype(jnp.bfloat16)
    send_weight = jnp.sum(one_hot * weight[:, :, None], axis=(0, 1)).reshape(group_count, 1, high)
    send_rows = lax.dot_general(
        placement, rows, (((0,), (0,)), ((), ())), preferred_element_type=jnp.float32
    ).reshape(group_count, high, width)
    last = jnp.arange(high) == high - 1
    weight_row = jnp.pad(send_weight, ((0, 0), (0, 0), (0, width - high)))
    send = jnp.where(last[None, :, None], weight_row, send_rows).astype(jnp.bfloat16)
    buffer = exchange(send, "group")

    buffer_weight = buffer[:, high - 1, :capacity].astype(jnp.float32).reshape(slots, 1)
    buffer_rows = buffer[:, :capacity].reshape(slots, width)
    back_proj = across(buffer_rows, w_down)
    grad_gate, grad_up, gate_piece = gradients(
        back_proj, buffer_weight, pre_act[0].astype(jnp.float32), pre_act[1].astype(jnp.float32)
    )
    pieces = (across(grad_gate, w_gate) + across(grad_up, w_up)).reshape(group_count, capacity, width)
    gate_row = jnp.pad(
        gate_piece.reshape(group_count, 1, capacity), ((0, 0), (0, 0), (0, width - capacity))
    )
    pieces = jnp.pad(pieces, ((0, 0), (0, high - capacity), (0, 0)))
    back = exchange(jnp.where(last[None, :, None], gate_row, pieces).astype(jnp.bfloat16), "group")

    owned = jnp.dot(
        placement, back.reshape(group_count * high, width), preferred_element_type=jnp.float32
    ).astype(jnp.bfloat16)
    gates = back[:, high - 1, :high].reshape(group_count * high).astype(jnp.float32)
    gate_rows = jnp.sum(one_hot * gates, axis=2)
    final = exchange(pack(owned, gate_rows).reshape(inner_count, own, -1), "inner")
    total = jnp.sum(final.astype(jnp.float32), axis=0)
    return total[:, :width].astype(jnp.bfloat16), total[:, width : width + topk]


def solution(mesh):
    if mesh.size <= 64:
        group_count, inner_count = mesh.devices.shape
        devices = mesh.devices.reshape(group_count // CORES, CORES, inner_count)
        mesh, axes, on_device = Mesh(devices, ("row", "core", "inner")), ("row", "core", "inner"), flat
    else:
        axes, on_device = ("group", "inner"), staged
    token, hidden = P(axes, None), P(None, axes)
    return jax.shard_map(
        on_device,
        mesh=mesh,
        in_specs=(token, token, token, token, hidden, hidden, token, P(None, None, axes)),
        out_specs=(token, token),
        check_vma=False,
    )
```

```python
import functools

import jax
import jax.numpy as jnp
from jax import lax
from jax.experimental import pallas as pl
from jax.experimental.pallas import tpu as pltpu
from jax.sharding import Mesh, PartitionSpec as P

LANES = 128
CORES = 2
SAVED_ROWS = 32


def exchange(array, axis):
    return lax.all_to_all(array, axis, split_axis=0, concat_axis=0, tiled=True)


def pack(rows, *small):
    width = sum(s.shape[1] for s in small)
    fill = jnp.zeros((rows.shape[0], -width % LANES), rows.dtype)
    return jnp.concatenate([rows, *(s.astype(rows.dtype) for s in small), fill], axis=1)


def gradients(back_proj, weight, pre_gate, pre_up):
    gate_sig = jax.nn.sigmoid(pre_gate)
    swish_gate = pre_gate * gate_sig
    gate_piece = jnp.sum(swish_gate * pre_up * back_proj, axis=1, keepdims=True)
    scaled = weight * back_proj
    grad_up = (scaled * swish_gate).astype(jnp.bfloat16)
    grad_gate = (scaled * pre_up * gate_sig * (1.0 + pre_gate * (1.0 - gate_sig))).astype(
        jnp.bfloat16
    )
    return grad_gate, grad_up, gate_piece


def across(a, b):
    return lax.dot_general(a, b, (((1,), (1,)), ((), ())), preferred_element_type=jnp.float32)


def sizes(group_count, inner_count):
    split_count = min(8, inner_count // 4)
    return split_count, inner_count // split_count


def pack_kernel(
    out_grad, ids, slots, weights, w_gate, w_up, w_down, pre_act,
    sent, both, down, rows, words, reals, saved, small, sems,
):
    width, topk = w_gate.shape[0], ids.shape[1]
    copies = [
        pltpu.make_async_copy(source, target, sems.at[at])
        for at, (source, target) in enumerate(
            (
                (ids, words.at[0]),
                (slots, words.at[1]),
                (weights, reals),
                (out_grad, rows),
                (pre_act, saved),
                (w_gate, both.at[:width]),
                (w_up, both.at[width : 2 * width]),
                (w_down, down),
            )
        )
    ]
    for copy in copies:
        copy.start()
    small[...] = jnp.zeros_like(small)
    both[2 * width :] = jnp.zeros((both.shape[0] - 2 * width, both.shape[1]), both.dtype)
    for copy in copies[:5]:
        copy.wait()
    for at, part in enumerate((words[0], words[1], reals[...])):
        small[:, at * topk : (at + 1) * topk] = part.astype(jnp.float32)
    tail = small[...].astype(sent.dtype)
    own_rows = rows[...]
    for peer in range(sent.shape[0]):
        sent[peer, :, :width] = own_rows
        sent[peer, :, width:] = tail
    for at in range(2):
        first = 2 * width + at * SAVED_ROWS
        both[first : first + saved.shape[1]] = saved[at]
    for copy in copies[5:]:
        copy.wait()


def expert_kernel(topk, slots, arrived, both1, down1, both2, down2, out):
    half, packed = arrived.shape
    width = packed - LANES
    row_count = lax.axis_size("row")
    capacity = slots // (row_count * CORES)
    split_count, experts_here = sizes(row_count * CORES, lax.axis_size("inner"))
    core = lax.axis_index("core")
    group_row = lax.axis_index("row") * CORES
    local_expert = lax.axis_index("inner") // split_count
    small = arrived[:, width:].astype(jnp.float32)
    lane = lax.broadcasted_iota(jnp.int32, small.shape, 1)
    source = lax.broadcasted_iota(jnp.int32, (half, slots), 0) // (half // row_count)
    first = (source * CORES + core) * capacity
    column = lax.broadcasted_iota(jnp.int32, (half, slots), 1)

    def routed(group_core):
        expert = (group_row + group_core) * experts_here + local_expert
        mine = jnp.where(
            jnp.logical_and(small == expert.astype(jnp.float32), lane < topk), 1.0, 0.0
        )
        slot = jnp.sum(pltpu.roll(mine, topk, 1) * small, axis=1, keepdims=True)
        weight = jnp.sum(pltpu.roll(mine, 2 * topk, 1) * small, axis=1, keepdims=True)
        chosen = jnp.sum(mine, axis=1, keepdims=True)
        hit = jnp.logical_and(first + slot.astype(jnp.int32) == column, chosen > 0.5)
        return mine, weight, jnp.where(hit, 1.0, 0.0).astype(jnp.bfloat16)

    def backward(routing, back_proj, both):
        mine, weight, one_hot = routing
        pre_gate, pre_up = [
            jnp.dot(
                one_hot,
                both[2 * width + at * SAVED_ROWS : 2 * width + at * SAVED_ROWS + slots],
                preferred_element_type=jnp.float32,
            )
            for at in range(2)
        ]
        grad_gate, grad_up, gate_piece = gradients(back_proj, weight, pre_gate, pre_up)
        return grad_gate, grad_up, mine * gate_piece

    rows = arrived[:, :width]
    own, other = routed(core), routed(1 - core)
    grad_gate1, grad_up1, gates1 = backward(own, across(rows, down1[...]), both1)
    grad_gate2, grad_up2, gates2 = backward(other, across(rows, down2[...]), both2)
    grads = jnp.concatenate([grad_gate1, grad_up1, grad_gate2, grad_up2], axis=1)
    step = 512 if width % 512 == 0 else LANES
    for at in range(0, width, step):
        weights = [b[first + at : first + at + step] for b in (both1, both2) for first in (0, width)]
        pieces = across(grads, jnp.concatenate(weights, axis=1))
        out[:, at : at + step] = pieces.astype(out.dtype)
    out[:, width:] = (gates1 + gates2).astype(out.dtype)


def stay_in(space, *arrays):
    return [pltpu.with_memory_space_constraint(a, space) for a in arrays]


def swap_cores(array):
    return lax.ppermute(array, "core", [(0, 1), (1, 0)])


def flat(out_grad, routing_weight, expert_ids, slot_index, w_gate, w_up, w_down, pre_act):
    row_count = lax.axis_size("row")
    inner_count = lax.axis_size("inner")
    own, width = out_grad.shape
    topk = expert_ids.shape[1]
    peers = row_count * inner_count
    half = peers * own
    slots, hidden = pre_act.shape[1:]
    packed = width + LANES
    in_vmem = pl.BlockSpec(memory_space=pltpu.VMEM)
    in_hbm = pl.BlockSpec(memory_space=pltpu.HBM)
    bf16 = out_grad.dtype

    sent, both, down = pl.pallas_call(
        pack_kernel,
        out_shape=[
            jax.ShapeDtypeStruct((peers, own, packed), bf16),
            pltpu.VMEM((2 * width + 2 * SAVED_ROWS, hidden), bf16),
            pltpu.VMEM(w_down.shape, bf16),
        ],
        in_specs=[in_hbm] * 8,
        out_specs=[in_vmem] * 3,
        scratch_shapes=[
            pltpu.VMEM((own, width), bf16),
            pltpu.VMEM((2, own, topk), expert_ids.dtype),
            pltpu.VMEM((own, topk), bf16),
            pltpu.VMEM(pre_act.shape, bf16),
            pltpu.VMEM((own, LANES), jnp.float32),
            pltpu.SemaphoreType.DMA((8,)),
        ],
        compiler_params=pltpu.CompilerParams(vmem_limit_bytes=16 * 2**20),
        name="pack_rows",
    )(
        *stay_in(
            pltpu.HBM,
            *(out_grad, expert_ids, slot_index, routing_weight),
            *(w_gate, w_up, w_down, pre_act),
        )
    )
    both2, down2 = swap_cores(both), swap_cores(down)
    arrived = exchange(sent, ("row", "inner")).reshape(half, packed)
    pieces = pl.pallas_call(
        functools.partial(expert_kernel, topk, slots),
        out_shape=jax.ShapeDtypeStruct((half, packed), bf16),
        in_specs=[in_vmem] * 5,
        out_specs=in_vmem,
        compiler_params=pltpu.CompilerParams(vmem_limit_bytes=16 * 2**20),
        cost_estimate=pl.CostEstimate(
            flops=12 * half * w_down.size,
            bytes_accessed=2 * (both.nbytes + down.nbytes + arrived.nbytes),
            transcendentals=2 * half * hidden,
        ),
        name="expert_pieces",
    )(arrived, both, down, both2, down2)
    returned = exchange(pieces.reshape(peers, own, packed), ("row", "inner"))
    rows, gates = returned[:, :, :width], returned[:, :, width : width + topk]
    grad_rows = jnp.sum(rows.astype(jnp.float32), axis=0).astype(out_grad.dtype)
    return grad_rows, jnp.sum(gates.astype(jnp.float32), axis=0)


def staged(out_grad, routing_weight, expert_ids, slot_index, w_gate, w_up, w_down, pre_act):
    group_count = lax.axis_size("group")
    inner_count = lax.axis_size("inner")
    own, width = out_grad.shape
    topk = expert_ids.shape[1]
    split_count, experts_here = sizes(group_count, inner_count)
    local_expert = lax.axis_index("inner") // split_count
    block = inner_count * own
    slots = pre_act.shape[1]
    capacity = slots // group_count
    high = -(-(capacity + 1) // 8) * 8

    payload = pack(out_grad, expert_ids, slot_index, routing_weight)
    sent = jnp.broadcast_to(payload[None], (inner_count,) + payload.shape)
    arrived = exchange(sent, "inner").reshape(block, payload.shape[1])
    rows = arrived[:, :width]
    small = arrived[:, width : width + 3 * topk].astype(jnp.float32)
    ids = small[:, :topk].astype(jnp.int32)
    slot = small[:, topk : 2 * topk].astype(jnp.int32)
    weight = small[:, 2 * topk :]
    selected = ids % experts_here == local_expert
    column = ids // experts_here * high + slot
    one_hot = jnp.logical_and(
        column[:, :, None] == jnp.arange(group_count * high, dtype=jnp.int32), selected[:, :, None]
    ).astype(jnp.float32)
    placement = jnp.sum(one_hot, axis=1).astype(jnp.bfloat16)
    send_weight = jnp.sum(one_hot * weight[:, :, None], axis=(0, 1)).reshape(group_count, 1, high)
    send_rows = lax.dot_general(
        placement, rows, (((0,), (0,)), ((), ())), preferred_element_type=jnp.float32
    ).reshape(group_count, high, width)
    last = jnp.arange(high) == high - 1
    weight_row = jnp.pad(send_weight, ((0, 0), (0, 0), (0, width - high)))
    send = jnp.where(last[None, :, None], weight_row, send_rows).astype(jnp.bfloat16)
    buffer = exchange(send, "group")

    buffer_weight = buffer[:, high - 1, :capacity].astype(jnp.float32).reshape(slots, 1)
    buffer_rows = buffer[:, :capacity].reshape(slots, width)
    back_proj = across(buffer_rows, w_down)
    grad_gate, grad_up, gate_piece = gradients(
        back_proj, buffer_weight, pre_act[0].astype(jnp.float32), pre_act[1].astype(jnp.float32)
    )
    pieces = (across(grad_gate, w_gate) + across(grad_up, w_up)).reshape(group_count, capacity, width)
    gate_row = jnp.pad(
        gate_piece.reshape(group_count, 1, capacity), ((0, 0), (0, 0), (0, width - capacity))
    )
    pieces = jnp.pad(pieces, ((0, 0), (0, high - capacity), (0, 0)))
    back = exchange(jnp.where(last[None, :, None], gate_row, pieces).astype(jnp.bfloat16), "group")

    owned = jnp.dot(
        placement, back.reshape(group_count * high, width), preferred_element_type=jnp.float32
    ).astype(jnp.bfloat16)
    gates = back[:, high - 1, :high].reshape(group_count * high).astype(jnp.float32)
    gate_rows = jnp.sum(one_hot * gates, axis=2)
    final = exchange(pack(owned, gate_rows).reshape(inner_count, own, -1), "inner")
    total = jnp.sum(final.astype(jnp.float32), axis=0)
    return total[:, :width].astype(jnp.bfloat16), total[:, width : width + topk]


def solution(mesh):
    if mesh.size <= 64:
        group_count, inner_count = mesh.devices.shape
        devices = mesh.devices.reshape(group_count // CORES, CORES, inner_count)
        mesh, axes, on_device = Mesh(devices, ("row", "core", "inner")), ("row", "core", "inner"), flat
    else:
        axes, on_device = ("group", "inner"), staged
    token, hidden = P(axes, None), P(None, axes)
    return jax.shard_map(
        on_device,
        mesh=mesh,
        in_specs=(token, token, token, token, hidden, hidden, token, P(None, None, axes)),
        out_specs=(token, token),
        check_vma=False,
    )
```

```python
import functools

import jax
import jax.numpy as jnp
from jax import lax
from jax.experimental import pallas as pl
from jax.experimental.pallas import tpu as pltpu
from jax.sharding import Mesh, PartitionSpec as P

LANES = 128
CORES = 2
SAVED_ROWS = 32


def exchange(array, axis):
    return lax.all_to_all(array, axis, split_axis=0, concat_axis=0, tiled=True)


def pack(rows, *small):
    width = sum(s.shape[1] for s in small)
    fill = jnp.zeros((rows.shape[0], -width % LANES), rows.dtype)
    return jnp.concatenate([rows, *(s.astype(rows.dtype) for s in small), fill], axis=1)


def gradients(back_proj, weight, pre_gate, pre_up):
    gate_sig = jax.nn.sigmoid(pre_gate)
    swish_gate = pre_gate * gate_sig
    gate_piece = jnp.sum(swish_gate * pre_up * back_proj, axis=1, keepdims=True)
    scaled = weight * back_proj
    grad_up = (scaled * swish_gate).astype(jnp.bfloat16)
    grad_gate = (scaled * pre_up * gate_sig * (1.0 + pre_gate * (1.0 - gate_sig))).astype(
        jnp.bfloat16
    )
    return grad_gate, grad_up, gate_piece


def across(a, b):
    return lax.dot_general(a, b, (((1,), (1,)), ((), ())), preferred_element_type=jnp.float32)


def sizes(group_count, inner_count):
    split_count = min(8, inner_count // 4)
    return split_count, inner_count // split_count


def pack_kernel(
    out_grad, ids, slots, weights, w_gate, w_up, w_down, pre_act,
    sent, both, down, rows, words, reals, saved, small, sems,
):
    width, topk = w_gate.shape[0], ids.shape[1]
    copies = [
        pltpu.make_async_copy(source, target, sems.at[at])
        for at, (source, target) in enumerate(
            (
                (ids, words.at[0]),
                (slots, words.at[1]),
                (weights, reals),
                (out_grad, rows),
                (pre_act, saved),
                (w_gate, both.at[:width]),
                (w_up, both.at[width : 2 * width]),
                (w_down, down),
            )
        )
    ]
    for copy in copies:
        copy.start()
    small[...] = jnp.zeros_like(small)
    both[2 * width :] = jnp.zeros((both.shape[0] - 2 * width, both.shape[1]), both.dtype)
    for copy in copies[:5]:
        copy.wait()
    for at, part in enumerate((words[0], words[1], reals[...])):
        small[:, at * topk : (at + 1) * topk] = part.astype(jnp.float32)
    tail = small[...].astype(sent.dtype)
    own_rows = rows[...]
    for peer in range(sent.shape[0]):
        sent[peer, :, :width] = own_rows
        sent[peer, :, width:] = tail
    for at in range(2):
        first = 2 * width + at * SAVED_ROWS
        both[first : first + saved.shape[1]] = saved[at]
    for copy in copies[5:]:
        copy.wait()


def expert_kernel(topk, slots, arrived, both1, down1, both2, down2, out):
    half, packed = arrived.shape
    width = packed - LANES
    row_count = lax.axis_size("row")
    capacity = slots // (row_count * CORES)
    split_count, experts_here = sizes(row_count * CORES, lax.axis_size("inner"))
    core = lax.axis_index("core")
    group_row = lax.axis_index("row") * CORES
    local_expert = lax.axis_index("inner") // split_count
    small = arrived[:, width:].astype(jnp.float32)
    lane = lax.broadcasted_iota(jnp.int32, small.shape, 1)
    source = lax.broadcasted_iota(jnp.int32, (half, slots), 0) // (half // row_count)
    first = (source * CORES + core) * capacity
    column = lax.broadcasted_iota(jnp.int32, (half, slots), 1)

    def routed(group_core):
        expert = (group_row + group_core) * experts_here + local_expert
        mine = jnp.where(
            jnp.logical_and(small == expert.astype(jnp.float32), lane < topk), 1.0, 0.0
        )
        slot = jnp.sum(pltpu.roll(mine, topk, 1) * small, axis=1, keepdims=True)
        weight = jnp.sum(pltpu.roll(mine, 2 * topk, 1) * small, axis=1, keepdims=True)
        chosen = jnp.sum(mine, axis=1, keepdims=True)
        hit = jnp.logical_and(first + slot.astype(jnp.int32) == column, chosen > 0.5)
        return mine, weight, jnp.where(hit, 1.0, 0.0).astype(jnp.bfloat16)

    def backward(routing, back_proj, both):
        mine, weight, one_hot = routing
        pre_gate, pre_up = [
            jnp.dot(
                one_hot,
                both[2 * width + at * SAVED_ROWS : 2 * width + at * SAVED_ROWS + slots],
                preferred_element_type=jnp.float32,
            )
            for at in range(2)
        ]
        grad_gate, grad_up, gate_piece = gradients(back_proj, weight, pre_gate, pre_up)
        return grad_gate, grad_up, mine * gate_piece

    rows = arrived[:, :width]
    own, other = routed(core), routed(1 - core)
    grad_gate1, grad_up1, gates1 = backward(own, across(rows, down1[...]), both1)
    grad_gate2, grad_up2, gates2 = backward(other, across(rows, down2[...]), both2)
    grads = jnp.concatenate([grad_gate1, grad_up1, grad_gate2, grad_up2], axis=1)
    step = 512 if width % 512 == 0 else LANES
    for at in range(0, width, step):
        weights = [b[first + at : first + at + step] for b in (both1, both2) for first in (0, width)]
        pieces = across(grads, jnp.concatenate(weights, axis=1))
        out[:, at : at + step] = pieces.astype(out.dtype)
    out[:, width:] = (gates1 + gates2).astype(out.dtype)


def stay_in(space, *arrays):
    return [pltpu.with_memory_space_constraint(a, space) for a in arrays]


def swap_cores(array):
    return lax.ppermute(array, "core", [(0, 1), (1, 0)])


def flat(out_grad, routing_weight, expert_ids, slot_index, w_gate, w_up, w_down, pre_act):
    row_count = lax.axis_size("row")
    inner_count = lax.axis_size("inner")
    own, width = out_grad.shape
    topk = expert_ids.shape[1]
    peers = row_count * inner_count
    half = peers * own
    slots, hidden = pre_act.shape[1:]
    packed = width + LANES
    in_vmem = pl.BlockSpec(memory_space=pltpu.VMEM)
    in_hbm = pl.BlockSpec(memory_space=pltpu.HBM)
    bf16 = out_grad.dtype

    sent, both, down = pl.pallas_call(
        pack_kernel,
        out_shape=[
            jax.ShapeDtypeStruct((peers, own, packed), bf16),
            pltpu.VMEM((2 * width + 2 * SAVED_ROWS, hidden), bf16),
            pltpu.VMEM(w_down.shape, bf16),
        ],
        in_specs=[in_hbm] * 8,
        out_specs=[in_vmem] * 3,
        scratch_shapes=[
            pltpu.VMEM((own, width), bf16),
            pltpu.VMEM((2, own, topk), expert_ids.dtype),
            pltpu.VMEM((own, topk), bf16),
            pltpu.VMEM(pre_act.shape, bf16),
            pltpu.VMEM((own, LANES), jnp.float32),
            pltpu.SemaphoreType.DMA((8,)),
        ],
        compiler_params=pltpu.CompilerParams(vmem_limit_bytes=16 * 2**20),
        name="pack_rows",
    )(
        *stay_in(
            pltpu.HBM,
            *(out_grad, expert_ids, slot_index, routing_weight),
            *(w_gate, w_up, w_down, pre_act),
        )
    )
    both2, down2 = swap_cores(both), swap_cores(down)
    arrived = exchange(sent, ("row", "inner")).reshape(half, packed)
    pieces = pl.pallas_call(
        functools.partial(expert_kernel, topk, slots),
        out_shape=jax.ShapeDtypeStruct((half, packed), bf16),
        in_specs=[in_vmem] * 5,
        out_specs=in_vmem,
        compiler_params=pltpu.CompilerParams(vmem_limit_bytes=16 * 2**20),
        cost_estimate=pl.CostEstimate(
            flops=12 * half * w_down.size,
            bytes_accessed=2 * (both.nbytes + down.nbytes + arrived.nbytes),
            transcendentals=2 * half * hidden,
        ),
        name="expert_pieces",
    )(arrived, *stay_in(pltpu.VMEM, both, down, both2, down2))
    returned = exchange(pieces.reshape(peers, own, packed), ("row", "inner"))
    rows, gates = returned[:, :, :width], returned[:, :, width : width + topk]
    grad_rows = jnp.sum(rows.astype(jnp.float32), axis=0).astype(out_grad.dtype)
    return grad_rows, jnp.sum(gates.astype(jnp.float32), axis=0)


def staged(out_grad, routing_weight, expert_ids, slot_index, w_gate, w_up, w_down, pre_act):
    group_count = lax.axis_size("group")
    inner_count = lax.axis_size("inner")
    own, width = out_grad.shape
    topk = expert_ids.shape[1]
    split_count, experts_here = sizes(group_count, inner_count)
    local_expert = lax.axis_index("inner") // split_count
    block = inner_count * own
    slots = pre_act.shape[1]
    capacity = slots // group_count
    high = -(-(capacity + 1) // 8) * 8

    payload = pack(out_grad, expert_ids, slot_index, routing_weight)
    sent = jnp.broadcast_to(payload[None], (inner_count,) + payload.shape)
    arrived = exchange(sent, "inner").reshape(block, payload.shape[1])
    rows = arrived[:, :width]
    small = arrived[:, width : width + 3 * topk].astype(jnp.float32)
    ids = small[:, :topk].astype(jnp.int32)
    slot = small[:, topk : 2 * topk].astype(jnp.int32)
    weight = small[:, 2 * topk :]
    selected = ids % experts_here == local_expert
    column = ids // experts_here * high + slot
    one_hot = jnp.logical_and(
        column[:, :, None] == jnp.arange(group_count * high, dtype=jnp.int32), selected[:, :, None]
    ).astype(jnp.float32)
    placement = jnp.sum(one_hot, axis=1).astype(jnp.bfloat16)
    send_weight = jnp.sum(one_hot * weight[:, :, None], axis=(0, 1)).reshape(group_count, 1, high)
    send_rows = lax.dot_general(
        placement, rows, (((0,), (0,)), ((), ())), preferred_element_type=jnp.float32
    ).reshape(group_count, high, width)
    last = jnp.arange(high) == high - 1
    weight_row = jnp.pad(send_weight, ((0, 0), (0, 0), (0, width - high)))
    send = jnp.where(last[None, :, None], weight_row, send_rows).astype(jnp.bfloat16)
    buffer = exchange(send, "group")

    buffer_weight = buffer[:, high - 1, :capacity].astype(jnp.float32).reshape(slots, 1)
    buffer_rows = buffer[:, :capacity].reshape(slots, width)
    back_proj = across(buffer_rows, w_down)
    grad_gate, grad_up, gate_piece = gradients(
        back_proj, buffer_weight, pre_act[0].astype(jnp.float32), pre_act[1].astype(jnp.float32)
    )
    pieces = (across(grad_gate, w_gate) + across(grad_up, w_up)).reshape(group_count, capacity, width)
    gate_row = jnp.pad(
        gate_piece.reshape(group_count, 1, capacity), ((0, 0), (0, 0), (0, width - capacity))
    )
    pieces = jnp.pad(pieces, ((0, 0), (0, high - capacity), (0, 0)))
    back = exchange(jnp.where(last[None, :, None], gate_row, pieces).astype(jnp.bfloat16), "group")

    owned = jnp.dot(
        placement, back.reshape(group_count * high, width), preferred_element_type=jnp.float32
    ).astype(jnp.bfloat16)
    gates = back[:, high - 1, :high].reshape(group_count * high).astype(jnp.float32)
    gate_rows = jnp.sum(one_hot * gates, axis=2)
    final = exchange(pack(owned, gate_rows).reshape(inner_count, own, -1), "inner")
    total = jnp.sum(final.astype(jnp.float32), axis=0)
    return total[:, :width].astype(jnp.bfloat16), total[:, width : width + topk]


def solution(mesh):
    if mesh.size <= 64:
        group_count, inner_count = mesh.devices.shape
        devices = mesh.devices.reshape(group_count // CORES, CORES, inner_count)
        mesh, axes, on_device = Mesh(devices, ("row", "core", "inner")), ("row", "core", "inner"), flat
    else:
        axes, on_device = ("group", "inner"), staged
    token, hidden = P(axes, None), P(None, axes)
    return jax.shard_map(
        on_device,
        mesh=mesh,
        in_specs=(token, token, token, token, hidden, hidden, token, P(None, None, axes)),
        out_specs=(token, token),
        check_vma=False,
    )
```

```python
import functools

import jax
import jax.numpy as jnp
from jax import lax
from jax.experimental import pallas as pl
from jax.experimental.pallas import tpu as pltpu
from jax.sharding import Mesh, PartitionSpec as P

LANES = 128
CORES = 2
SAVED_ROWS = 32


def exchange(array, axis):
    return lax.all_to_all(array, axis, split_axis=0, concat_axis=0, tiled=True)


def pack(rows, *small):
    width = sum(s.shape[1] for s in small)
    fill = jnp.zeros((rows.shape[0], -width % LANES), rows.dtype)
    return jnp.concatenate([rows, *(s.astype(rows.dtype) for s in small), fill], axis=1)


def gradients(back_proj, weight, pre_gate, pre_up):
    gate_sig = jax.nn.sigmoid(pre_gate)
    swish_gate = pre_gate * gate_sig
    gate_piece = jnp.sum(swish_gate * pre_up * back_proj, axis=1, keepdims=True)
    scaled = weight * back_proj
    grad_up = (scaled * swish_gate).astype(jnp.bfloat16)
    grad_gate = (scaled * pre_up * gate_sig * (1.0 + pre_gate * (1.0 - gate_sig))).astype(
        jnp.bfloat16
    )
    return grad_gate, grad_up, gate_piece


def across(a, b):
    return lax.dot_general(a, b, (((1,), (1,)), ((), ())), preferred_element_type=jnp.float32)


def sizes(group_count, inner_count):
    split_count = min(8, inner_count // 4)
    return split_count, inner_count // split_count


def pack_kernel(
    out_grad, ids, slots, weights, w_gate, w_up, w_down, pre_act,
    sent, both, down, rows, words, reals, saved, small, sems,
):
    width, topk = w_gate.shape[0], ids.shape[1]
    copies = [
        pltpu.make_async_copy(source, target, sems.at[at])
        for at, (source, target) in enumerate(
            (
                (ids, words.at[0]),
                (slots, words.at[1]),
                (weights, reals),
                (out_grad, rows),
                (pre_act, saved),
                (w_gate, both.at[:width]),
                (w_up, both.at[width : 2 * width]),
                (w_down, down),
            )
        )
    ]
    for copy in copies:
        copy.start()
    small[...] = jnp.zeros_like(small)
    both[2 * width :] = jnp.zeros((both.shape[0] - 2 * width, both.shape[1]), both.dtype)
    for copy in copies[:5]:
        copy.wait()
    for at, part in enumerate((words[0], words[1], reals[...])):
        small[:, at * topk : (at + 1) * topk] = part.astype(jnp.float32)
    tail = small[...].astype(sent.dtype)
    own_rows = rows[...]
    for peer in range(sent.shape[0]):
        sent[peer, :, :width] = own_rows
        sent[peer, :, width:] = tail
    for at in range(2):
        first = 2 * width + at * SAVED_ROWS
        both[first : first + saved.shape[1]] = saved[at]
    for copy in copies[5:]:
        copy.wait()


def expert_kernel(own_rows, topk, slots, *refs):
    arrived, outs = refs[:own_rows], refs[own_rows + 4 :]
    both1, down1, both2, down2 = refs[own_rows : own_rows + 4]
    half, width = own_rows * arrived[0].shape[0], arrived[0].shape[1] - LANES
    row_count = lax.axis_size("row")
    peers = row_count * lax.axis_size("inner")
    capacity = slots // (row_count * CORES)
    split_count, experts_here = sizes(row_count * CORES, lax.axis_size("inner"))
    core = lax.axis_index("core")
    group_row = lax.axis_index("row") * CORES
    local_expert = lax.axis_index("inner") // split_count
    small = jnp.concatenate([part[:, width:] for part in arrived]).astype(jnp.float32)
    lane = lax.broadcasted_iota(jnp.int32, small.shape, 1)
    peer = lax.broadcasted_iota(jnp.int32, (half, slots), 0) % peers
    source = peer // (peers // row_count)
    first = (source * CORES + core) * capacity
    column = lax.broadcasted_iota(jnp.int32, (half, slots), 1)

    def routed(group_core):
        expert = (group_row + group_core) * experts_here + local_expert
        mine = jnp.where(
            jnp.logical_and(small == expert.astype(jnp.float32), lane < topk), 1.0, 0.0
        )
        slot = jnp.sum(pltpu.roll(mine, topk, 1) * small, axis=1, keepdims=True)
        weight = jnp.sum(pltpu.roll(mine, 2 * topk, 1) * small, axis=1, keepdims=True)
        chosen = jnp.sum(mine, axis=1, keepdims=True)
        hit = jnp.logical_and(first + slot.astype(jnp.int32) == column, chosen > 0.5)
        return mine, weight, jnp.where(hit, 1.0, 0.0).astype(jnp.bfloat16)

    def backward(routing, back_proj, both):
        mine, weight, one_hot = routing
        pre_gate, pre_up = [
            jnp.dot(
                one_hot,
                both[2 * width + at * SAVED_ROWS : 2 * width + at * SAVED_ROWS + slots],
                preferred_element_type=jnp.float32,
            )
            for at in range(2)
        ]
        grad_gate, grad_up, gate_piece = gradients(back_proj, weight, pre_gate, pre_up)
        return grad_gate, grad_up, mine * gate_piece

    def store(cols, values):
        for at, out in enumerate(outs):
            out[:, cols] = values[at * peers : (at + 1) * peers].astype(out.dtype)

    rows = jnp.concatenate([part[:, :width] for part in arrived])
    own, other = routed(core), routed(1 - core)
    grad_gate1, grad_up1, gates1 = backward(own, across(rows, down1[...]), both1)
    grad_gate2, grad_up2, gates2 = backward(other, across(rows, down2[...]), both2)
    grads = jnp.concatenate([grad_gate1, grad_up1, grad_gate2, grad_up2], axis=1)
    step = 512 if width % 512 == 0 else LANES
    for at in range(0, width, step):
        weights = [b[first + at : first + at + step] for b in (both1, both2) for first in (0, width)]
        store(slice(at, at + step), across(grads, jnp.concatenate(weights, axis=1)))
    store(slice(width, width + LANES), gates1 + gates2)


def stay_in(space, *arrays):
    return [pltpu.with_memory_space_constraint(a, space) for a in arrays]


def swap_cores(array):
    return lax.ppermute(array, "core", [(0, 1), (1, 0)])


def flat(out_grad, routing_weight, expert_ids, slot_index, w_gate, w_up, w_down, pre_act):
    row_count = lax.axis_size("row")
    inner_count = lax.axis_size("inner")
    own, width = out_grad.shape
    topk = expert_ids.shape[1]
    peers = row_count * inner_count
    half = peers * own
    slots, hidden = pre_act.shape[1:]
    packed = width + LANES
    in_vmem = pl.BlockSpec(memory_space=pltpu.VMEM)
    in_hbm = pl.BlockSpec(memory_space=pltpu.HBM)
    bf16 = out_grad.dtype

    sent, both, down = pl.pallas_call(
        pack_kernel,
        out_shape=[
            jax.ShapeDtypeStruct((peers, own, packed), bf16),
            pltpu.VMEM((2 * width + 2 * SAVED_ROWS, hidden), bf16),
            pltpu.VMEM(w_down.shape, bf16),
        ],
        in_specs=[in_hbm] * 8,
        out_specs=[in_vmem] * 3,
        scratch_shapes=[
            pltpu.VMEM((own, width), bf16),
            pltpu.VMEM((2, own, topk), expert_ids.dtype),
            pltpu.VMEM((own, topk), bf16),
            pltpu.VMEM(pre_act.shape, bf16),
            pltpu.VMEM((own, LANES), jnp.float32),
            pltpu.SemaphoreType.DMA((8,)),
        ],
        compiler_params=pltpu.CompilerParams(vmem_limit_bytes=16 * 2**20),
        name="pack_rows",
    )(
        *stay_in(
            pltpu.HBM,
            *(out_grad, expert_ids, slot_index, routing_weight),
            *(w_gate, w_up, w_down, pre_act),
        )
    )
    both2, down2 = swap_cores(both), swap_cores(down)
    arrived = exchange(sent, ("row", "inner"))
    pieces = pl.pallas_call(
        functools.partial(expert_kernel, own, topk, slots),
        out_shape=[jax.ShapeDtypeStruct((peers, packed), bf16)] * own,
        in_specs=[in_vmem] * (own + 4),
        out_specs=[in_vmem] * own,
        compiler_params=pltpu.CompilerParams(vmem_limit_bytes=16 * 2**20),
        cost_estimate=pl.CostEstimate(
            flops=12 * half * w_down.size,
            bytes_accessed=2 * (both.nbytes + down.nbytes + arrived.nbytes),
            transcendentals=2 * half * hidden,
        ),
        name="expert_pieces",
    )(
        *(arrived[:, at] for at in range(own)),
        *stay_in(pltpu.VMEM, both, down, both2, down2),
    )
    returned = exchange(jnp.stack(pieces, axis=1), ("row", "inner"))
    rows, gates = returned[:, :, :width], returned[:, :, width : width + topk]
    grad_rows = jnp.sum(rows.astype(jnp.float32), axis=0).astype(out_grad.dtype)
    return grad_rows, jnp.sum(gates.astype(jnp.float32), axis=0)


def staged(out_grad, routing_weight, expert_ids, slot_index, w_gate, w_up, w_down, pre_act):
    group_count = lax.axis_size("group")
    inner_count = lax.axis_size("inner")
    own, width = out_grad.shape
    topk = expert_ids.shape[1]
    split_count, experts_here = sizes(group_count, inner_count)
    local_expert = lax.axis_index("inner") // split_count
    block = inner_count * own
    slots = pre_act.shape[1]
    capacity = slots // group_count
    high = -(-(capacity + 1) // 8) * 8

    payload = pack(out_grad, expert_ids, slot_index, routing_weight)
    sent = jnp.broadcast_to(payload[None], (inner_count,) + payload.shape)
    arrived = exchange(sent, "inner").reshape(block, payload.shape[1])
    rows = arrived[:, :width]
    small = arrived[:, width : width + 3 * topk].astype(jnp.float32)
    ids = small[:, :topk].astype(jnp.int32)
    slot = small[:, topk : 2 * topk].astype(jnp.int32)
    weight = small[:, 2 * topk :]
    selected = ids % experts_here == local_expert
    column = ids // experts_here * high + slot
    one_hot = jnp.logical_and(
        column[:, :, None] == jnp.arange(group_count * high, dtype=jnp.int32), selected[:, :, None]
    ).astype(jnp.float32)
    placement = jnp.sum(one_hot, axis=1).astype(jnp.bfloat16)
    send_weight = jnp.sum(one_hot * weight[:, :, None], axis=(0, 1)).reshape(group_count, 1, high)
    send_rows = lax.dot_general(
        placement, rows, (((0,), (0,)), ((), ())), preferred_element_type=jnp.float32
    ).reshape(group_count, high, width)
    last = jnp.arange(high) == high - 1
    weight_row = jnp.pad(send_weight, ((0, 0), (0, 0), (0, width - high)))
    send = jnp.where(last[None, :, None], weight_row, send_rows).astype(jnp.bfloat16)
    buffer = exchange(send, "group")

    buffer_weight = buffer[:, high - 1, :capacity].astype(jnp.float32).reshape(slots, 1)
    buffer_rows = buffer[:, :capacity].reshape(slots, width)
    back_proj = across(buffer_rows, w_down)
    grad_gate, grad_up, gate_piece = gradients(
        back_proj, buffer_weight, pre_act[0].astype(jnp.float32), pre_act[1].astype(jnp.float32)
    )
    pieces = (across(grad_gate, w_gate) + across(grad_up, w_up)).reshape(group_count, capacity, width)
    gate_row = jnp.pad(
        gate_piece.reshape(group_count, 1, capacity), ((0, 0), (0, 0), (0, width - capacity))
    )
    pieces = jnp.pad(pieces, ((0, 0), (0, high - capacity), (0, 0)))
    back = exchange(jnp.where(last[None, :, None], gate_row, pieces).astype(jnp.bfloat16), "group")

    owned = jnp.dot(
        placement, back.reshape(group_count * high, width), preferred_element_type=jnp.float32
    ).astype(jnp.bfloat16)
    gates = back[:, high - 1, :high].reshape(group_count * high).astype(jnp.float32)
    gate_rows = jnp.sum(one_hot * gates, axis=2)
    final = exchange(pack(owned, gate_rows).reshape(inner_count, own, -1), "inner")
    total = jnp.sum(final.astype(jnp.float32), axis=0)
    return total[:, :width].astype(jnp.bfloat16), total[:, width : width + topk]


def solution(mesh):
    if mesh.size <= 64:
        group_count, inner_count = mesh.devices.shape
        devices = mesh.devices.reshape(group_count // CORES, CORES, inner_count)
        mesh, axes, on_device = Mesh(devices, ("row", "core", "inner")), ("row", "core", "inner"), flat
    else:
        axes, on_device = ("group", "inner"), staged
    token, hidden = P(axes, None), P(None, axes)
    return jax.shard_map(
        on_device,
        mesh=mesh,
        in_specs=(token, token, token, token, hidden, hidden, token, P(None, None, axes)),
        out_specs=(token, token),
        check_vma=False,
    )
```

```python
import functools

import jax
import jax.numpy as jnp
from jax import lax
from jax.experimental import pallas as pl
from jax.experimental.pallas import tpu as pltpu
from jax.sharding import Mesh, PartitionSpec as P

LANES = 128
CORES = 2
SAVED_ROWS = 32


def exchange(array, axis):
    return lax.all_to_all(array, axis, split_axis=0, concat_axis=0, tiled=True)


def pack(rows, *small):
    width = sum(s.shape[1] for s in small)
    fill = jnp.zeros((rows.shape[0], -width % LANES), rows.dtype)
    return jnp.concatenate([rows, *(s.astype(rows.dtype) for s in small), fill], axis=1)


def gradients(back_proj, weight, pre_gate, pre_up):
    gate_sig = jax.nn.sigmoid(pre_gate)
    swish_gate = pre_gate * gate_sig
    gate_piece = jnp.sum(swish_gate * pre_up * back_proj, axis=1, keepdims=True)
    scaled = weight * back_proj
    grad_up = (scaled * swish_gate).astype(jnp.bfloat16)
    grad_gate = (scaled * pre_up * gate_sig * (1.0 + pre_gate * (1.0 - gate_sig))).astype(
        jnp.bfloat16
    )
    return grad_gate, grad_up, gate_piece


def across(a, b):
    return lax.dot_general(a, b, (((1,), (1,)), ((), ())), preferred_element_type=jnp.float32)


def sizes(group_count, inner_count):
    split_count = min(8, inner_count // 4)
    return split_count, inner_count // split_count


def block_rows(width):
    return 512 if width % 512 == 0 else LANES


def pack_kernel(
    out_grad, ids, slots, weights, w_gate, w_up, w_down, pre_act,
    sent, both, down, rows, words, reals, saved, small, sems,
):
    width, topk = w_gate.shape[0], ids.shape[1]
    copies = [
        pltpu.make_async_copy(source, target, sems.at[at])
        for at, (source, target) in enumerate(
            (
                (ids, words.at[0]),
                (slots, words.at[1]),
                (weights, reals),
                (out_grad, rows),
                (pre_act, saved),
                (w_gate, both.at[:width]),
                (w_up, both.at[width : 2 * width]),
                (w_down, down),
            )
        )
    ]
    for copy in copies:
        copy.start()
    small[...] = jnp.zeros_like(small)
    both[2 * width :] = jnp.zeros((both.shape[0] - 2 * width, both.shape[1]), both.dtype)
    for copy in copies[:5]:
        copy.wait()
    for at, part in enumerate((words[0], words[1], reals[...])):
        small[:, at * topk : (at + 1) * topk] = part.astype(jnp.float32)
    tail = small[...].astype(sent.dtype)
    own_rows = rows[...]
    for peer in range(sent.shape[0]):
        sent[peer, :, :width] = own_rows
        sent[peer, :, width:] = tail
    for at in range(2):
        first = 2 * width + at * SAVED_ROWS
        both[first : first + saved.shape[1]] = saved[at]
    for copy in copies[5:]:
        copy.wait()


def expert_kernel(
    topk, slots, arrived, both1, down1, both2_hbm, down2_hbm, out, both2, down2, sems
):
    half, packed = arrived.shape
    width = packed - LANES
    step = block_rows(width)
    spans = [(2 * width, 2 * SAVED_ROWS)]
    spans += [(first + at, step) for at in range(0, width, step) for first in (0, width)]
    copies = [pltpu.make_async_copy(down2_hbm, down2, sems.at[0])]
    copies += [
        pltpu.make_async_copy(
            both2_hbm.at[first : first + rows], both2.at[first : first + rows], sems.at[1 + at]
        )
        for at, (first, rows) in enumerate(spans)
    ]
    for copy in copies:
        copy.start()
    row_count = lax.axis_size("row")
    capacity = slots // (row_count * CORES)
    split_count, experts_here = sizes(row_count * CORES, lax.axis_size("inner"))
    core = lax.axis_index("core")
    group_row = lax.axis_index("row") * CORES
    local_expert = lax.axis_index("inner") // split_count
    small = arrived[:, width:].astype(jnp.float32)
    lane = lax.broadcasted_iota(jnp.int32, small.shape, 1)
    source = lax.broadcasted_iota(jnp.int32, (half, slots), 0) // (half // row_count)
    first = (source * CORES + core) * capacity
    column = lax.broadcasted_iota(jnp.int32, (half, slots), 1)

    def routed(group_core):
        expert = (group_row + group_core) * experts_here + local_expert
        mine = jnp.where(
            jnp.logical_and(small == expert.astype(jnp.float32), lane < topk), 1.0, 0.0
        )
        slot = jnp.sum(pltpu.roll(mine, topk, 1) * small, axis=1, keepdims=True)
        weight = jnp.sum(pltpu.roll(mine, 2 * topk, 1) * small, axis=1, keepdims=True)
        chosen = jnp.sum(mine, axis=1, keepdims=True)
        hit = jnp.logical_and(first + slot.astype(jnp.int32) == column, chosen > 0.5)
        return mine, weight, jnp.where(hit, 1.0, 0.0).astype(jnp.bfloat16)

    def backward(routing, back_proj, both):
        mine, weight, one_hot = routing
        pre_gate, pre_up = [
            jnp.dot(
                one_hot,
                both[2 * width + at * SAVED_ROWS : 2 * width + at * SAVED_ROWS + slots],
                preferred_element_type=jnp.float32,
            )
            for at in range(2)
        ]
        grad_gate, grad_up, gate_piece = gradients(back_proj, weight, pre_gate, pre_up)
        return grad_gate, grad_up, mine * gate_piece

    rows = arrived[:, :width]
    own, other = routed(core), routed(1 - core)
    grad_gate1, grad_up1, gates1 = backward(own, across(rows, down1[...]), both1)
    copies[0].wait()
    copies[1].wait()
    grad_gate2, grad_up2, gates2 = backward(other, across(rows, down2[...]), both2)
    grads = jnp.concatenate([grad_gate1, grad_up1, grad_gate2, grad_up2], axis=1)
    for number, at in enumerate(range(0, width, step)):
        copies[2 + 2 * number].wait()
        copies[3 + 2 * number].wait()
        weights = [b[first + at : first + at + step] for b in (both1, both2) for first in (0, width)]
        pieces = across(grads, jnp.concatenate(weights, axis=1))
        out[:, at : at + step] = pieces.astype(out.dtype)
    out[:, width:] = (gates1 + gates2).astype(out.dtype)


def stay_in(space, *arrays):
    return [pltpu.with_memory_space_constraint(a, space) for a in arrays]


def swap_cores(array):
    return lax.ppermute(array, "core", [(0, 1), (1, 0)])


def flat(out_grad, routing_weight, expert_ids, slot_index, w_gate, w_up, w_down, pre_act):
    row_count = lax.axis_size("row")
    inner_count = lax.axis_size("inner")
    own, width = out_grad.shape
    topk = expert_ids.shape[1]
    peers = row_count * inner_count
    half = peers * own
    slots, hidden = pre_act.shape[1:]
    packed = width + LANES
    in_vmem = pl.BlockSpec(memory_space=pltpu.VMEM)
    in_hbm = pl.BlockSpec(memory_space=pltpu.HBM)
    bf16 = out_grad.dtype

    sent, both, down = pl.pallas_call(
        pack_kernel,
        out_shape=[
            jax.ShapeDtypeStruct((peers, own, packed), bf16),
            pltpu.VMEM((2 * width + 2 * SAVED_ROWS, hidden), bf16),
            pltpu.VMEM(w_down.shape, bf16),
        ],
        in_specs=[in_hbm] * 8,
        out_specs=[in_vmem] * 3,
        scratch_shapes=[
            pltpu.VMEM((own, width), bf16),
            pltpu.VMEM((2, own, topk), expert_ids.dtype),
            pltpu.VMEM((own, topk), bf16),
            pltpu.VMEM(pre_act.shape, bf16),
            pltpu.VMEM((own, LANES), jnp.float32),
            pltpu.SemaphoreType.DMA((8,)),
        ],
        compiler_params=pltpu.CompilerParams(vmem_limit_bytes=16 * 2**20),
        name="pack_rows",
    )(
        *stay_in(
            pltpu.HBM,
            *(out_grad, expert_ids, slot_index, routing_weight),
            *(w_gate, w_up, w_down, pre_act),
        )
    )
    both2, down2 = swap_cores(both), swap_cores(down)
    arrived = exchange(sent, ("row", "inner")).reshape(half, packed)
    pieces = pl.pallas_call(
        functools.partial(expert_kernel, topk, slots),
        out_shape=jax.ShapeDtypeStruct((half, packed), bf16),
        in_specs=[in_vmem] * 3 + [in_hbm] * 2,
        out_specs=in_vmem,
        scratch_shapes=[
            pltpu.VMEM(both.shape, bf16),
            pltpu.VMEM(down.shape, bf16),
            pltpu.SemaphoreType.DMA((2 + 2 * (width // block_rows(width)),)),
        ],
        compiler_params=pltpu.CompilerParams(vmem_limit_bytes=16 * 2**20),
        cost_estimate=pl.CostEstimate(
            flops=12 * half * w_down.size,
            bytes_accessed=2 * (both.nbytes + down.nbytes + arrived.nbytes),
            transcendentals=2 * half * hidden,
        ),
        name="expert_pieces",
    )(arrived, both, down, *stay_in(pltpu.HBM, both2, down2))
    returned = exchange(pieces.reshape(peers, own, packed), ("row", "inner"))
    rows, gates = returned[:, :, :width], returned[:, :, width : width + topk]
    grad_rows = jnp.sum(rows.astype(jnp.float32), axis=0).astype(out_grad.dtype)
    return grad_rows, jnp.sum(gates.astype(jnp.float32), axis=0)


def staged(out_grad, routing_weight, expert_ids, slot_index, w_gate, w_up, w_down, pre_act):
    group_count = lax.axis_size("group")
    inner_count = lax.axis_size("inner")
    own, width = out_grad.shape
    topk = expert_ids.shape[1]
    split_count, experts_here = sizes(group_count, inner_count)
    local_expert = lax.axis_index("inner") // split_count
    block = inner_count * own
    slots = pre_act.shape[1]
    capacity = slots // group_count
    high = -(-(capacity + 1) // 8) * 8

    payload = pack(out_grad, expert_ids, slot_index, routing_weight)
    sent = jnp.broadcast_to(payload[None], (inner_count,) + payload.shape)
    arrived = exchange(sent, "inner").reshape(block, payload.shape[1])
    rows = arrived[:, :width]
    small = arrived[:, width : width + 3 * topk].astype(jnp.float32)
    ids = small[:, :topk].astype(jnp.int32)
    slot = small[:, topk : 2 * topk].astype(jnp.int32)
    weight = small[:, 2 * topk :]
    selected = ids % experts_here == local_expert
    column = ids // experts_here * high + slot
    one_hot = jnp.logical_and(
        column[:, :, None] == jnp.arange(group_count * high, dtype=jnp.int32), selected[:, :, None]
    ).astype(jnp.float32)
    placement = jnp.sum(one_hot, axis=1).astype(jnp.bfloat16)
    send_weight = jnp.sum(one_hot * weight[:, :, None], axis=(0, 1)).reshape(group_count, 1, high)
    send_rows = lax.dot_general(
        placement, rows, (((0,), (0,)), ((), ())), preferred_element_type=jnp.float32
    ).reshape(group_count, high, width)
    last = jnp.arange(high) == high - 1
    weight_row = jnp.pad(send_weight, ((0, 0), (0, 0), (0, width - high)))
    send = jnp.where(last[None, :, None], weight_row, send_rows).astype(jnp.bfloat16)
    buffer = exchange(send, "group")

    buffer_weight = buffer[:, high - 1, :capacity].astype(jnp.float32).reshape(slots, 1)
    buffer_rows = buffer[:, :capacity].reshape(slots, width)
    back_proj = across(buffer_rows, w_down)
    grad_gate, grad_up, gate_piece = gradients(
        back_proj, buffer_weight, pre_act[0].astype(jnp.float32), pre_act[1].astype(jnp.float32)
    )
    pieces = (across(grad_gate, w_gate) + across(grad_up, w_up)).reshape(group_count, capacity, width)
    gate_row = jnp.pad(
        gate_piece.reshape(group_count, 1, capacity), ((0, 0), (0, 0), (0, width - capacity))
    )
    pieces = jnp.pad(pieces, ((0, 0), (0, high - capacity), (0, 0)))
    back = exchange(jnp.where(last[None, :, None], gate_row, pieces).astype(jnp.bfloat16), "group")

    owned = jnp.dot(
        placement, back.reshape(group_count * high, width), preferred_element_type=jnp.float32
    ).astype(jnp.bfloat16)
    gates = back[:, high - 1, :high].reshape(group_count * high).astype(jnp.float32)
    gate_rows = jnp.sum(one_hot * gates, axis=2)
    final = exchange(pack(owned, gate_rows).reshape(inner_count, own, -1), "inner")
    total = jnp.sum(final.astype(jnp.float32), axis=0)
    return total[:, :width].astype(jnp.bfloat16), total[:, width : width + topk]


def solution(mesh):
    if mesh.size <= 64:
        group_count, inner_count = mesh.devices.shape
        devices = mesh.devices.reshape(group_count // CORES, CORES, inner_count)
        mesh, axes, on_device = Mesh(devices, ("row", "core", "inner")), ("row", "core", "inner"), flat
    else:
        axes, on_device = ("group", "inner"), staged
    token, hidden = P(axes, None), P(None, axes)
    return jax.shard_map(
        on_device,
        mesh=mesh,
        in_specs=(token, token, token, token, hidden, hidden, token, P(None, None, axes)),
        out_specs=(token, token),
        check_vma=False,
    )
```

```python
import functools

import jax
import jax.numpy as jnp
from jax import lax
from jax.experimental import pallas as pl
from jax.experimental.pallas import tpu as pltpu
from jax.sharding import Mesh, PartitionSpec as P

LANES = 128
CORES = 2
SAVED_ROWS = 32


def exchange(array, axis):
    return lax.all_to_all(array, axis, split_axis=0, concat_axis=0, tiled=True)


def pack(rows, *small):
    width = sum(s.shape[1] for s in small)
    fill = jnp.zeros((rows.shape[0], -width % LANES), rows.dtype)
    return jnp.concatenate([rows, *(s.astype(rows.dtype) for s in small), fill], axis=1)


def gradients(back_proj, weight, pre_gate, pre_up):
    gate_sig = jax.nn.sigmoid(pre_gate)
    swish_gate = pre_gate * gate_sig
    gate_piece = jnp.sum(swish_gate * pre_up * back_proj, axis=1, keepdims=True)
    scaled = weight * back_proj
    grad_up = (scaled * swish_gate).astype(jnp.bfloat16)
    grad_gate = (scaled * pre_up * gate_sig * (1.0 + pre_gate * (1.0 - gate_sig))).astype(
        jnp.bfloat16
    )
    return grad_gate, grad_up, gate_piece


def across(a, b):
    return lax.dot_general(a, b, (((1,), (1,)), ((), ())), preferred_element_type=jnp.float32)


def sizes(group_count, inner_count):
    split_count = min(8, inner_count // 4)
    return split_count, inner_count // split_count


def pack_kernel(
    out_grad, ids, slots, weights, w_gate, w_up, w_down, pre_act,
    sent, both, rows, words, reals, saved, small, sems,
):
    width, topk = w_gate.shape[0], ids.shape[1]
    first_down = 2 * width + 2 * SAVED_ROWS
    copies = [
        pltpu.make_async_copy(source, target, sems.at[at])
        for at, (source, target) in enumerate(
            (
                (ids, words.at[0]),
                (slots, words.at[1]),
                (weights, reals),
                (out_grad, rows),
                (pre_act, saved),
                (w_gate, both.at[:width]),
                (w_up, both.at[width : 2 * width]),
                *(
                    (w_down.at[:, at : at + LANES], both.at[first_down + at : first_down + at + LANES])
                    for at in range(0, width, LANES)
                ),
            )
        )
    ]
    for copy in copies:
        copy.start()
    small[...] = jnp.zeros_like(small)
    both[2 * width : first_down] = jnp.zeros((2 * SAVED_ROWS, LANES), both.dtype)
    for copy in copies[:5]:
        copy.wait()
    for at, part in enumerate((words[0], words[1], reals[...])):
        small[:, at * topk : (at + 1) * topk] = part.astype(jnp.float32)
    tail = small[...].astype(sent.dtype)
    own_rows = rows[...]
    for peer in range(sent.shape[0]):
        sent[peer, :, :width] = own_rows
        sent[peer, :, width:] = tail
    for at in range(2):
        first = 2 * width + at * SAVED_ROWS
        both[first : first + saved.shape[1]] = saved[at]
    for copy in copies[5:]:
        copy.wait()


def expert_kernel(own_rows, topk, slots, *refs):
    arrived, outs = refs[:own_rows], refs[own_rows + 2 :]
    both1, both2 = refs[own_rows : own_rows + 2]
    half, width = own_rows * arrived[0].shape[0], arrived[0].shape[1] - LANES
    row_count = lax.axis_size("row")
    peers = row_count * lax.axis_size("inner")
    capacity = slots // (row_count * CORES)
    split_count, experts_here = sizes(row_count * CORES, lax.axis_size("inner"))
    core = lax.axis_index("core")
    group_row = lax.axis_index("row") * CORES
    local_expert = lax.axis_index("inner") // split_count
    small = jnp.concatenate([part[:, width:] for part in arrived]).astype(jnp.float32)
    lane = lax.broadcasted_iota(jnp.int32, small.shape, 1)
    peer = lax.broadcasted_iota(jnp.int32, (half, slots), 0) % peers
    source = peer // (peers // row_count)
    first = (source * CORES + core) * capacity
    column = lax.broadcasted_iota(jnp.int32, (half, slots), 1)

    def routed(group_core):
        expert = (group_row + group_core) * experts_here + local_expert
        mine = jnp.where(
            jnp.logical_and(small == expert.astype(jnp.float32), lane < topk), 1.0, 0.0
        )
        slot = jnp.sum(pltpu.roll(mine, topk, 1) * small, axis=1, keepdims=True)
        weight = jnp.sum(pltpu.roll(mine, 2 * topk, 1) * small, axis=1, keepdims=True)
        chosen = jnp.sum(mine, axis=1, keepdims=True)
        hit = jnp.logical_and(first + slot.astype(jnp.int32) == column, chosen > 0.5)
        return mine, weight, jnp.where(hit, 1.0, 0.0).astype(jnp.bfloat16)

    def backward(routing, back_proj, both):
        mine, weight, one_hot = routing
        pre_gate, pre_up = [
            jnp.dot(
                one_hot,
                both[2 * width + at * SAVED_ROWS : 2 * width + at * SAVED_ROWS + slots],
                preferred_element_type=jnp.float32,
            )
            for at in range(2)
        ]
        grad_gate, grad_up, gate_piece = gradients(back_proj, weight, pre_gate, pre_up)
        return grad_gate, grad_up, mine * gate_piece

    def store(cols, values):
        for at, out in enumerate(outs):
            out[:, cols] = values[at * peers : (at + 1) * peers].astype(out.dtype)

    def back(both):
        first = 2 * width + 2 * SAVED_ROWS
        blocks = [both[first + at : first + at + LANES] for at in range(0, width, LANES)]
        return across(rows, jnp.concatenate(blocks, axis=1))

    rows = jnp.concatenate([part[:, :width] for part in arrived])
    own, other = routed(core), routed(1 - core)
    grad_gate1, grad_up1, gates1 = backward(own, back(both1), both1)
    grad_gate2, grad_up2, gates2 = backward(other, back(both2), both2)
    grads = jnp.concatenate([grad_gate1, grad_up1, grad_gate2, grad_up2], axis=1)
    step = 512 if width % 512 == 0 else LANES
    for at in range(0, width, step):
        weights = [b[first + at : first + at + step] for b in (both1, both2) for first in (0, width)]
        store(slice(at, at + step), across(grads, jnp.concatenate(weights, axis=1)))
    store(slice(width, width + LANES), gates1 + gates2)


def stay_in(space, *arrays):
    return [pltpu.with_memory_space_constraint(a, space) for a in arrays]


def swap_cores(array):
    return lax.ppermute(array, "core", [(0, 1), (1, 0)])


def flat(out_grad, routing_weight, expert_ids, slot_index, w_gate, w_up, w_down, pre_act):
    row_count = lax.axis_size("row")
    inner_count = lax.axis_size("inner")
    own, width = out_grad.shape
    topk = expert_ids.shape[1]
    peers = row_count * inner_count
    half = peers * own
    slots, hidden = pre_act.shape[1:]
    packed = width + LANES
    in_vmem = pl.BlockSpec(memory_space=pltpu.VMEM)
    in_hbm = pl.BlockSpec(memory_space=pltpu.HBM)
    bf16 = out_grad.dtype

    sent, both = pl.pallas_call(
        pack_kernel,
        out_shape=[
            jax.ShapeDtypeStruct((peers, own, packed), bf16),
            pltpu.VMEM((3 * width + 2 * SAVED_ROWS, hidden), bf16),
        ],
        in_specs=[in_hbm] * 8,
        out_specs=[in_vmem] * 2,
        scratch_shapes=[
            pltpu.VMEM((own, width), bf16),
            pltpu.VMEM((2, own, topk), expert_ids.dtype),
            pltpu.VMEM((own, topk), bf16),
            pltpu.VMEM(pre_act.shape, bf16),
            pltpu.VMEM((own, LANES), jnp.float32),
            pltpu.SemaphoreType.DMA((7 + width // LANES,)),
        ],
        compiler_params=pltpu.CompilerParams(vmem_limit_bytes=16 * 2**20),
        name="pack_rows",
    )(
        *stay_in(
            pltpu.HBM,
            *(out_grad, expert_ids, slot_index, routing_weight),
            *(w_gate, w_up, w_down, pre_act),
        )
    )
    both2 = swap_cores(both)
    arrived = exchange(sent, ("row", "inner"))
    pieces = pl.pallas_call(
        functools.partial(expert_kernel, own, topk, slots),
        out_shape=[jax.ShapeDtypeStruct((peers, packed), bf16)] * own,
        in_specs=[in_vmem] * (own + 2),
        out_specs=[in_vmem] * own,
        compiler_params=pltpu.CompilerParams(vmem_limit_bytes=16 * 2**20),
        cost_estimate=pl.CostEstimate(
            flops=12 * half * w_down.size,
            bytes_accessed=2 * (both.nbytes + arrived.nbytes),
            transcendentals=2 * half * hidden,
        ),
        name="expert_pieces",
    )(
        *(arrived[:, at] for at in range(own)),
        *stay_in(pltpu.VMEM, both, both2),
    )
    returned = exchange(jnp.stack(pieces, axis=1), ("row", "inner"))
    rows, gates = returned[:, :, :width], returned[:, :, width : width + topk]
    grad_rows = jnp.sum(rows.astype(jnp.float32), axis=0).astype(out_grad.dtype)
    return grad_rows, jnp.sum(gates.astype(jnp.float32), axis=0)


def staged(out_grad, routing_weight, expert_ids, slot_index, w_gate, w_up, w_down, pre_act):
    group_count = lax.axis_size("group")
    inner_count = lax.axis_size("inner")
    own, width = out_grad.shape
    topk = expert_ids.shape[1]
    split_count, experts_here = sizes(group_count, inner_count)
    local_expert = lax.axis_index("inner") // split_count
    block = inner_count * own
    slots = pre_act.shape[1]
    capacity = slots // group_count
    high = -(-(capacity + 1) // 8) * 8

    payload = pack(out_grad, expert_ids, slot_index, routing_weight)
    sent = jnp.broadcast_to(payload[None], (inner_count,) + payload.shape)
    arrived = exchange(sent, "inner").reshape(block, payload.shape[1])
    rows = arrived[:, :width]
    small = arrived[:, width : width + 3 * topk].astype(jnp.float32)
    ids = small[:, :topk].astype(jnp.int32)
    slot = small[:, topk : 2 * topk].astype(jnp.int32)
    weight = small[:, 2 * topk :]
    selected = ids % experts_here == local_expert
    column = ids // experts_here * high + slot
    one_hot = jnp.logical_and(
        column[:, :, None] == jnp.arange(group_count * high, dtype=jnp.int32), selected[:, :, None]
    ).astype(jnp.float32)
    placement = jnp.sum(one_hot, axis=1).astype(jnp.bfloat16)
    send_weight = jnp.sum(one_hot * weight[:, :, None], axis=(0, 1)).reshape(group_count, 1, high)
    send_rows = lax.dot_general(
        placement, rows, (((0,), (0,)), ((), ())), preferred_element_type=jnp.float32
    ).reshape(group_count, high, width)
    last = jnp.arange(high) == high - 1
    weight_row = jnp.pad(send_weight, ((0, 0), (0, 0), (0, width - high)))
    send = jnp.where(last[None, :, None], weight_row, send_rows).astype(jnp.bfloat16)
    buffer = exchange(send, "group")

    buffer_weight = buffer[:, high - 1, :capacity].astype(jnp.float32).reshape(slots, 1)
    buffer_rows = buffer[:, :capacity].reshape(slots, width)
    back_proj = across(buffer_rows, w_down)
    grad_gate, grad_up, gate_piece = gradients(
        back_proj, buffer_weight, pre_act[0].astype(jnp.float32), pre_act[1].astype(jnp.float32)
    )
    pieces = (across(grad_gate, w_gate) + across(grad_up, w_up)).reshape(group_count, capacity, width)
    gate_row = jnp.pad(
        gate_piece.reshape(group_count, 1, capacity), ((0, 0), (0, 0), (0, width - capacity))
    )
    pieces = jnp.pad(pieces, ((0, 0), (0, high - capacity), (0, 0)))
    back = exchange(jnp.where(last[None, :, None], gate_row, pieces).astype(jnp.bfloat16), "group")

    owned = jnp.dot(
        placement, back.reshape(group_count * high, width), preferred_element_type=jnp.float32
    ).astype(jnp.bfloat16)
    gates = back[:, high - 1, :high].reshape(group_count * high).astype(jnp.float32)
    gate_rows = jnp.sum(one_hot * gates, axis=2)
    final = exchange(pack(owned, gate_rows).reshape(inner_count, own, -1), "inner")
    total = jnp.sum(final.astype(jnp.float32), axis=0)
    return total[:, :width].astype(jnp.bfloat16), total[:, width : width + topk]


def solution(mesh):
    if mesh.size <= 64:
        group_count, inner_count = mesh.devices.shape
        devices = mesh.devices.reshape(group_count // CORES, CORES, inner_count)
        mesh, axes, on_device = Mesh(devices, ("row", "core", "inner")), ("row", "core", "inner"), flat
    else:
        axes, on_device = ("group", "inner"), staged
    token, hidden = P(axes, None), P(None, axes)
    return jax.shard_map(
        on_device,
        mesh=mesh,
        in_specs=(token, token, token, token, hidden, hidden, token, P(None, None, axes)),
        out_specs=(token, token),
        check_vma=False,
    )
```

```python
import functools

import jax
import jax.numpy as jnp
from jax import lax
from jax.experimental import pallas as pl
from jax.experimental.pallas import tpu as pltpu
from jax.sharding import Mesh, PartitionSpec as P

LANES = 128
CORES = 2
SAVED_ROWS = 32


def exchange(array, axis):
    return lax.all_to_all(array, axis, split_axis=0, concat_axis=0, tiled=True)


def pack(rows, *small):
    width = sum(s.shape[1] for s in small)
    fill = jnp.zeros((rows.shape[0], -width % LANES), rows.dtype)
    return jnp.concatenate([rows, *(s.astype(rows.dtype) for s in small), fill], axis=1)


def gradients(back_proj, weight, pre_gate, pre_up):
    gate_sig = jax.nn.sigmoid(pre_gate)
    swish_gate = pre_gate * gate_sig
    gate_piece = jnp.sum(swish_gate * pre_up * back_proj, axis=1, keepdims=True)
    scaled = weight * back_proj
    grad_up = (scaled * swish_gate).astype(jnp.bfloat16)
    grad_gate = (scaled * pre_up * gate_sig * (1.0 + pre_gate * (1.0 - gate_sig))).astype(
        jnp.bfloat16
    )
    return grad_gate, grad_up, gate_piece


def across(a, b):
    return lax.dot_general(a, b, (((1,), (1,)), ((), ())), preferred_element_type=jnp.float32)


def sizes(group_count, inner_count):
    split_count = min(8, inner_count // 4)
    return split_count, inner_count // split_count


def pack_kernel(
    out_grad, ids, slots, weights, w_gate, w_up, w_down, pre_act,
    sent, both, rows, words, reals, saved, small, sems,
):
    width, topk = w_gate.shape[0], ids.shape[1]
    first_down = 2 * width + 2 * SAVED_ROWS
    copies = [
        pltpu.make_async_copy(source, target, sems.at[at])
        for at, (source, target) in enumerate(
            (
                (ids, words.at[0]),
                (slots, words.at[1]),
                (weights, reals),
                (out_grad, rows),
                (pre_act, saved),
                (w_gate, both.at[:width]),
                (w_up, both.at[width : 2 * width]),
                *(
                    (w_down.at[:, at : at + LANES], both.at[first_down + at : first_down + at + LANES])
                    for at in range(0, width, LANES)
                ),
            )
        )
    ]
    for copy in copies:
        copy.start()
    small[...] = jnp.zeros_like(small)
    both[2 * width : first_down] = jnp.zeros((2 * SAVED_ROWS, LANES), both.dtype)
    for copy in copies[:5]:
        copy.wait()
    for at, part in enumerate((words[0], words[1], reals[...])):
        small[:, at * topk : (at + 1) * topk] = part.astype(jnp.float32)
    tail = small[...].astype(sent.dtype)
    own_rows = rows[...]
    for peer in range(sent.shape[0]):
        sent[peer, :, :width] = own_rows
        sent[peer, :, width:] = tail
    for at in range(2):
        first = 2 * width + at * SAVED_ROWS
        both[first : first + saved.shape[1]] = saved[at]
    for copy in copies[5:]:
        copy.wait()


def expert_kernel(topk, slots, arrived, both1, both2, out):
    half, width = arrived.shape[0], arrived.shape[1] - LANES
    row_count = lax.axis_size("row")
    peers = row_count * lax.axis_size("inner")
    capacity = slots // (row_count * CORES)
    split_count, experts_here = sizes(row_count * CORES, lax.axis_size("inner"))
    core = lax.axis_index("core")
    group_row = lax.axis_index("row") * CORES
    local_expert = lax.axis_index("inner") // split_count
    small = arrived[:, width:].astype(jnp.float32)
    lane = lax.broadcasted_iota(jnp.int32, small.shape, 1)
    peer = lax.broadcasted_iota(jnp.int32, (half, slots), 0) % peers
    source = peer // (peers // row_count)
    first = (source * CORES + core) * capacity
    column = lax.broadcasted_iota(jnp.int32, (half, slots), 1)

    def routed(group_core):
        expert = (group_row + group_core) * experts_here + local_expert
        mine = jnp.where(
            jnp.logical_and(small == expert.astype(jnp.float32), lane < topk), 1.0, 0.0
        )
        slot = jnp.sum(pltpu.roll(mine, topk, 1) * small, axis=1, keepdims=True)
        weight = jnp.sum(pltpu.roll(mine, 2 * topk, 1) * small, axis=1, keepdims=True)
        chosen = jnp.sum(mine, axis=1, keepdims=True)
        hit = jnp.logical_and(first + slot.astype(jnp.int32) == column, chosen > 0.5)
        return mine, weight, jnp.where(hit, 1.0, 0.0).astype(jnp.bfloat16)

    def backward(routing, back_proj, both):
        mine, weight, one_hot = routing
        pre_gate, pre_up = [
            jnp.dot(
                one_hot,
                both[2 * width + at * SAVED_ROWS : 2 * width + at * SAVED_ROWS + slots],
                preferred_element_type=jnp.float32,
            )
            for at in range(2)
        ]
        grad_gate, grad_up, gate_piece = gradients(back_proj, weight, pre_gate, pre_up)
        return grad_gate, grad_up, mine * gate_piece

    def back(both):
        first = 2 * width + 2 * SAVED_ROWS
        blocks = [both[first + at : first + at + LANES] for at in range(0, width, LANES)]
        return across(rows, jnp.concatenate(blocks, axis=1))

    rows = arrived[:, :width]
    own, other = routed(core), routed(1 - core)
    grad_gate1, grad_up1, gates1 = backward(own, back(both1), both1)
    grad_gate2, grad_up2, gates2 = backward(other, back(both2), both2)
    grads = jnp.concatenate([grad_gate1, grad_up1, grad_gate2, grad_up2], axis=1)
    step = 512 if width % 512 == 0 else LANES
    for at in range(0, width, step):
        weights = [b[first + at : first + at + step] for b in (both1, both2) for first in (0, width)]
        pieces = across(grads, jnp.concatenate(weights, axis=1))
        out[:, at : at + step] = pieces.astype(out.dtype)
    out[:, width:] = (gates1 + gates2).astype(out.dtype)


def stay_in(space, *arrays):
    return [pltpu.with_memory_space_constraint(a, space) for a in arrays]


def swap_cores(array):
    return lax.ppermute(array, "core", [(0, 1), (1, 0)])


def flat(out_grad, routing_weight, expert_ids, slot_index, w_gate, w_up, w_down, pre_act):
    row_count = lax.axis_size("row")
    inner_count = lax.axis_size("inner")
    own, width = out_grad.shape
    topk = expert_ids.shape[1]
    peers = row_count * inner_count
    half = peers * own
    slots, hidden = pre_act.shape[1:]
    packed = width + LANES
    in_vmem = pl.BlockSpec(memory_space=pltpu.VMEM)
    in_hbm = pl.BlockSpec(memory_space=pltpu.HBM)
    bf16 = out_grad.dtype

    sent, both = pl.pallas_call(
        pack_kernel,
        out_shape=[
            jax.ShapeDtypeStruct((peers, own, packed), bf16),
            pltpu.VMEM((3 * width + 2 * SAVED_ROWS, hidden), bf16),
        ],
        in_specs=[in_hbm] * 8,
        out_specs=[in_vmem] * 2,
        scratch_shapes=[
            pltpu.VMEM((own, width), bf16),
            pltpu.VMEM((2, own, topk), expert_ids.dtype),
            pltpu.VMEM((own, topk), bf16),
            pltpu.VMEM(pre_act.shape, bf16),
            pltpu.VMEM((own, LANES), jnp.float32),
            pltpu.SemaphoreType.DMA((7 + width // LANES,)),
        ],
        compiler_params=pltpu.CompilerParams(vmem_limit_bytes=16 * 2**20),
        name="pack_rows",
    )(
        *stay_in(
            pltpu.HBM,
            *(out_grad, expert_ids, slot_index, routing_weight),
            *(w_gate, w_up, w_down, pre_act),
        )
    )
    both2 = swap_cores(both)
    arrived = exchange(sent, ("row", "inner"))
    arrived = jnp.swapaxes(arrived, 0, 1).reshape(half, packed)
    pieces = pl.pallas_call(
        functools.partial(expert_kernel, topk, slots),
        out_shape=jax.ShapeDtypeStruct((half, packed), bf16),
        in_specs=[in_vmem] * 3,
        out_specs=in_vmem,
        compiler_params=pltpu.CompilerParams(vmem_limit_bytes=16 * 2**20),
        cost_estimate=pl.CostEstimate(
            flops=12 * half * w_down.size,
            bytes_accessed=2 * (both.nbytes + arrived.nbytes),
            transcendentals=2 * half * hidden,
        ),
        name="expert_pieces",
    )(arrived, *stay_in(pltpu.VMEM, both, both2))
    pieces = jnp.swapaxes(pieces.reshape(own, peers, packed), 0, 1)
    returned = exchange(pieces, ("row", "inner"))
    rows, gates = returned[:, :, :width], returned[:, :, width : width + topk]
    grad_rows = jnp.sum(rows.astype(jnp.float32), axis=0).astype(out_grad.dtype)
    return grad_rows, jnp.sum(gates.astype(jnp.float32), axis=0)


def staged(out_grad, routing_weight, expert_ids, slot_index, w_gate, w_up, w_down, pre_act):
    group_count = lax.axis_size("group")
    inner_count = lax.axis_size("inner")
    own, width = out_grad.shape
    topk = expert_ids.shape[1]
    split_count, experts_here = sizes(group_count, inner_count)
    local_expert = lax.axis_index("inner") // split_count
    block = inner_count * own
    slots = pre_act.shape[1]
    capacity = slots // group_count
    high = -(-(capacity + 1) // 8) * 8

    payload = pack(out_grad, expert_ids, slot_index, routing_weight)
    sent = jnp.broadcast_to(payload[None], (inner_count,) + payload.shape)
    arrived = exchange(sent, "inner").reshape(block, payload.shape[1])
    rows = arrived[:, :width]
    small = arrived[:, width : width + 3 * topk].astype(jnp.float32)
    ids = small[:, :topk].astype(jnp.int32)
    slot = small[:, topk : 2 * topk].astype(jnp.int32)
    weight = small[:, 2 * topk :]
    selected = ids % experts_here == local_expert
    column = ids // experts_here * high + slot
    one_hot = jnp.logical_and(
        column[:, :, None] == jnp.arange(group_count * high, dtype=jnp.int32), selected[:, :, None]
    ).astype(jnp.float32)
    placement = jnp.sum(one_hot, axis=1).astype(jnp.bfloat16)
    send_weight = jnp.sum(one_hot * weight[:, :, None], axis=(0, 1)).reshape(group_count, 1, high)
    send_rows = lax.dot_general(
        placement, rows, (((0,), (0,)), ((), ())), preferred_element_type=jnp.float32
    ).reshape(group_count, high, width)
    last = jnp.arange(high) == high - 1
    weight_row = jnp.pad(send_weight, ((0, 0), (0, 0), (0, width - high)))
    send = jnp.where(last[None, :, None], weight_row, send_rows).astype(jnp.bfloat16)
    buffer = exchange(send, "group")

    buffer_weight = buffer[:, high - 1, :capacity].astype(jnp.float32).reshape(slots, 1)
    buffer_rows = buffer[:, :capacity].reshape(slots, width)
    back_proj = across(buffer_rows, w_down)
    grad_gate, grad_up, gate_piece = gradients(
        back_proj, buffer_weight, pre_act[0].astype(jnp.float32), pre_act[1].astype(jnp.float32)
    )
    pieces = (across(grad_gate, w_gate) + across(grad_up, w_up)).reshape(group_count, capacity, width)
    gate_row = jnp.pad(
        gate_piece.reshape(group_count, 1, capacity), ((0, 0), (0, 0), (0, width - capacity))
    )
    pieces = jnp.pad(pieces, ((0, 0), (0, high - capacity), (0, 0)))
    back = exchange(jnp.where(last[None, :, None], gate_row, pieces).astype(jnp.bfloat16), "group")

    owned = jnp.dot(
        placement, back.reshape(group_count * high, width), preferred_element_type=jnp.float32
    ).astype(jnp.bfloat16)
    gates = back[:, high - 1, :high].reshape(group_count * high).astype(jnp.float32)
    gate_rows = jnp.sum(one_hot * gates, axis=2)
    final = exchange(pack(owned, gate_rows).reshape(inner_count, own, -1), "inner")
    total = jnp.sum(final.astype(jnp.float32), axis=0)
    return total[:, :width].astype(jnp.bfloat16), total[:, width : width + topk]


def solution(mesh):
    if mesh.size <= 64:
        group_count, inner_count = mesh.devices.shape
        devices = mesh.devices.reshape(group_count // CORES, CORES, inner_count)
        mesh, axes, on_device = Mesh(devices, ("row", "core", "inner")), ("row", "core", "inner"), flat
    else:
        axes, on_device = ("group", "inner"), staged
    token, hidden = P(axes, None), P(None, axes)
    return jax.shard_map(
        on_device,
        mesh=mesh,
        in_specs=(token, token, token, token, hidden, hidden, token, P(None, None, axes)),
        out_specs=(token, token),
        check_vma=False,
    )
```

```python
import functools

import jax
import jax.numpy as jnp
from jax import lax
from jax.experimental import pallas as pl
from jax.experimental.pallas import tpu as pltpu
from jax.sharding import Mesh, PartitionSpec as P

LANES = 128
CORES = 2
SAVED_ROWS = 32
WEIGHT_COPIES = 4


def exchange(array, axis):
    return lax.all_to_all(array, axis, split_axis=0, concat_axis=0, tiled=True)


def pack(rows, *small):
    width = sum(s.shape[1] for s in small)
    fill = jnp.zeros((rows.shape[0], -width % LANES), rows.dtype)
    return jnp.concatenate([rows, *(s.astype(rows.dtype) for s in small), fill], axis=1)


def gradients(back_proj, weight, pre_gate, pre_up):
    gate_sig = jax.nn.sigmoid(pre_gate)
    swish_gate = pre_gate * gate_sig
    gate_piece = jnp.sum(swish_gate * pre_up * back_proj, axis=1, keepdims=True)
    scaled = weight * back_proj
    grad_up = (scaled * swish_gate).astype(jnp.bfloat16)
    grad_gate = (scaled * pre_up * gate_sig * (1.0 + pre_gate * (1.0 - gate_sig))).astype(
        jnp.bfloat16
    )
    return grad_gate, grad_up, gate_piece


def across(a, b):
    return lax.dot_general(a, b, (((1,), (1,)), ((), ())), preferred_element_type=jnp.float32)


def sizes(group_count, inner_count):
    split_count = min(8, inner_count // 4)
    return split_count, inner_count // split_count


def pack_kernel(
    out_grad, ids, slots, weights, w_gate, w_up, w_down, pre_act,
    sent, both, rows, words, reals, saved, small, sems,
):
    width, topk = w_gate.shape[0], ids.shape[1]
    first_down = 2 * width + 2 * SAVED_ROWS
    part = width // WEIGHT_COPIES
    copies = [
        pltpu.make_async_copy(source, target, sems.at[at])
        for at, (source, target) in enumerate(
            (
                (ids, words.at[0]),
                (slots, words.at[1]),
                (weights, reals),
                (out_grad, rows),
                (pre_act, saved),
                *(
                    (source.at[at : at + part], both.at[first + at : first + at + part])
                    for source, first in ((w_gate, 0), (w_up, width))
                    for at in range(0, width, part)
                ),
                *(
                    (w_down.at[:, at : at + LANES], both.at[first_down + at : first_down + at + LANES])
                    for at in range(0, width, LANES)
                ),
            )
        )
    ]
    for copy in copies:
        copy.start()
    small[...] = jnp.zeros_like(small)
    both[2 * width : first_down] = jnp.zeros((2 * SAVED_ROWS, LANES), both.dtype)
    for copy in copies[:5]:
        copy.wait()
    for at, part in enumerate((words[0], words[1], reals[...])):
        small[:, at * topk : (at + 1) * topk] = part.astype(jnp.float32)
    tail = small[...].astype(sent.dtype)
    own_rows = rows[...]
    for peer in range(sent.shape[0]):
        sent[peer, :, :width] = own_rows
        sent[peer, :, width:] = tail
    for at in range(2):
        first = 2 * width + at * SAVED_ROWS
        both[first : first + saved.shape[1]] = saved[at]
    for copy in copies[5:]:
        copy.wait()


def expert_kernel(topk, slots, arrived, both1, both2, out):
    half, width = arrived.shape[0], arrived.shape[1] - LANES
    row_count = lax.axis_size("row")
    peers = row_count * lax.axis_size("inner")
    capacity = slots // (row_count * CORES)
    split_count, experts_here = sizes(row_count * CORES, lax.axis_size("inner"))
    core = lax.axis_index("core")
    group_row = lax.axis_index("row") * CORES
    local_expert = lax.axis_index("inner") // split_count
    small = arrived[:, width:].astype(jnp.float32)
    lane = lax.broadcasted_iota(jnp.int32, small.shape, 1)
    peer = lax.broadcasted_iota(jnp.int32, (half, slots), 0) % peers
    source = peer // (peers // row_count)
    first = (source * CORES + core) * capacity
    column = lax.broadcasted_iota(jnp.int32, (half, slots), 1)

    def routed(group_core):
        expert = (group_row + group_core) * experts_here + local_expert
        mine = jnp.where(
            jnp.logical_and(small == expert.astype(jnp.float32), lane < topk), 1.0, 0.0
        )
        slot = jnp.sum(pltpu.roll(mine, topk, 1) * small, axis=1, keepdims=True)
        weight = jnp.sum(pltpu.roll(mine, 2 * topk, 1) * small, axis=1, keepdims=True)
        chosen = jnp.sum(mine, axis=1, keepdims=True)
        hit = jnp.logical_and(first + slot.astype(jnp.int32) == column, chosen > 0.5)
        return mine, weight, jnp.where(hit, 1.0, 0.0).astype(jnp.bfloat16)

    def backward(routing, back_proj, both):
        mine, weight, one_hot = routing
        pre_gate, pre_up = [
            jnp.dot(
                one_hot,
                both[2 * width + at * SAVED_ROWS : 2 * width + at * SAVED_ROWS + slots],
                preferred_element_type=jnp.float32,
            )
            for at in range(2)
        ]
        grad_gate, grad_up, gate_piece = gradients(back_proj, weight, pre_gate, pre_up)
        return grad_gate, grad_up, mine * gate_piece

    def back(both):
        first = 2 * width + 2 * SAVED_ROWS
        blocks = [both[first + at : first + at + LANES] for at in range(0, width, LANES)]
        return across(rows, jnp.concatenate(blocks, axis=1))

    rows = arrived[:, :width]
    own, other = routed(core), routed(1 - core)
    grad_gate1, grad_up1, gates1 = backward(own, back(both1), both1)
    grad_gate2, grad_up2, gates2 = backward(other, back(both2), both2)
    grads = jnp.concatenate([grad_gate1, grad_up1, grad_gate2, grad_up2], axis=1)
    step = 512 if width % 512 == 0 else LANES
    for at in range(0, width, step):
        weights = [b[first + at : first + at + step] for b in (both1, both2) for first in (0, width)]
        pieces = across(grads, jnp.concatenate(weights, axis=1))
        out[:, at : at + step] = pieces.astype(out.dtype)
    out[:, width:] = (gates1 + gates2).astype(out.dtype)


def final_kernel(pieces, grad_rows, grad_gate, rows, gates, sems):
    width, topk = rows.shape[1], gates.shape[1]

    def summed(cols):
        total = pieces[0, :, cols].astype(jnp.float32)
        for peer in range(1, pieces.shape[0]):
            total = total + pieces[peer, :, cols].astype(jnp.float32)
        return total

    copies = [pltpu.make_async_copy(gates, grad_gate, sems.at[0])]
    gates[...] = summed(slice(width, width + LANES))[:, :topk]
    copies[0].start()
    for at in range(2):
        cols = slice(at * width // 2, (at + 1) * width // 2)
        rows[:, cols] = summed(cols).astype(rows.dtype)
        copies.append(
            pltpu.make_async_copy(rows.at[:, cols], grad_rows.at[:, cols], sems.at[1 + at])
        )
        copies[-1].start()
    for copy in copies:
        copy.wait()


def stay_in(space, *arrays):
    return [pltpu.with_memory_space_constraint(a, space) for a in arrays]


def swap_cores(array):
    return lax.ppermute(array, "core", [(0, 1), (1, 0)])


def flat(out_grad, routing_weight, expert_ids, slot_index, w_gate, w_up, w_down, pre_act):
    row_count = lax.axis_size("row")
    inner_count = lax.axis_size("inner")
    own, width = out_grad.shape
    topk = expert_ids.shape[1]
    peers = row_count * inner_count
    half = peers * own
    slots, hidden = pre_act.shape[1:]
    packed = width + LANES
    in_vmem = pl.BlockSpec(memory_space=pltpu.VMEM)
    in_hbm = pl.BlockSpec(memory_space=pltpu.HBM)
    bf16 = out_grad.dtype

    sent, both = pl.pallas_call(
        pack_kernel,
        out_shape=[
            jax.ShapeDtypeStruct((peers, own, packed), bf16),
            pltpu.VMEM((3 * width + 2 * SAVED_ROWS, hidden), bf16),
        ],
        in_specs=[in_hbm] * 8,
        out_specs=[in_vmem] * 2,
        scratch_shapes=[
            pltpu.VMEM((own, width), bf16),
            pltpu.VMEM((2, own, topk), expert_ids.dtype),
            pltpu.VMEM((own, topk), bf16),
            pltpu.VMEM(pre_act.shape, bf16),
            pltpu.VMEM((own, LANES), jnp.float32),
            pltpu.SemaphoreType.DMA((5 + 2 * WEIGHT_COPIES + width // LANES,)),
        ],
        compiler_params=pltpu.CompilerParams(vmem_limit_bytes=16 * 2**20),
        name="pack_rows",
    )(
        *stay_in(
            pltpu.HBM,
            *(out_grad, expert_ids, slot_index, routing_weight),
            *(w_gate, w_up, w_down, pre_act),
        )
    )
    both2 = swap_cores(both)
    arrived = exchange(sent, ("row", "inner"))
    arrived = jnp.swapaxes(arrived, 0, 1).reshape(half, packed)
    pieces = pl.pallas_call(
        functools.partial(expert_kernel, topk, slots),
        out_shape=jax.ShapeDtypeStruct((half, packed), bf16),
        in_specs=[in_vmem] * 3,
        out_specs=in_vmem,
        compiler_params=pltpu.CompilerParams(vmem_limit_bytes=16 * 2**20),
        cost_estimate=pl.CostEstimate(
            flops=12 * half * w_down.size,
            bytes_accessed=2 * (both.nbytes + arrived.nbytes),
            transcendentals=2 * half * hidden,
        ),
        name="expert_pieces",
    )(arrived, *stay_in(pltpu.VMEM, both, both2))
    pieces = jnp.swapaxes(pieces.reshape(own, peers, packed), 0, 1)
    returned = exchange(pieces, ("row", "inner"))
    return pl.pallas_call(
        final_kernel,
        out_shape=[
            jax.ShapeDtypeStruct((own, width), bf16),
            jax.ShapeDtypeStruct((own, topk), jnp.float32),
        ],
        in_specs=[in_vmem],
        out_specs=[in_hbm] * 2,
        scratch_shapes=[
            pltpu.VMEM((own, width), bf16),
            pltpu.VMEM((own, topk), jnp.float32),
            pltpu.SemaphoreType.DMA((3,)),
        ],
        compiler_params=pltpu.CompilerParams(vmem_limit_bytes=16 * 2**20),
        name="sum_pieces",
    )(returned)


def staged(out_grad, routing_weight, expert_ids, slot_index, w_gate, w_up, w_down, pre_act):
    group_count = lax.axis_size("group")
    inner_count = lax.axis_size("inner")
    own, width = out_grad.shape
    topk = expert_ids.shape[1]
    split_count, experts_here = sizes(group_count, inner_count)
    local_expert = lax.axis_index("inner") // split_count
    block = inner_count * own
    slots = pre_act.shape[1]
    capacity = slots // group_count
    high = -(-(capacity + 1) // 8) * 8

    payload = pack(out_grad, expert_ids, slot_index, routing_weight)
    sent = jnp.broadcast_to(payload[None], (inner_count,) + payload.shape)
    arrived = exchange(sent, "inner").reshape(block, payload.shape[1])
    rows = arrived[:, :width]
    small = arrived[:, width : width + 3 * topk].astype(jnp.float32)
    ids = small[:, :topk].astype(jnp.int32)
    slot = small[:, topk : 2 * topk].astype(jnp.int32)
    weight = small[:, 2 * topk :]
    selected = ids % experts_here == local_expert
    column = ids // experts_here * high + slot
    one_hot = jnp.logical_and(
        column[:, :, None] == jnp.arange(group_count * high, dtype=jnp.int32), selected[:, :, None]
    ).astype(jnp.float32)
    placement = jnp.sum(one_hot, axis=1).astype(jnp.bfloat16)
    send_weight = jnp.sum(one_hot * weight[:, :, None], axis=(0, 1)).reshape(group_count, 1, high)
    send_rows = lax.dot_general(
        placement, rows, (((0,), (0,)), ((), ())), preferred_element_type=jnp.float32
    ).reshape(group_count, high, width)
    last = jnp.arange(high) == high - 1
    weight_row = jnp.pad(send_weight, ((0, 0), (0, 0), (0, width - high)))
    send = jnp.where(last[None, :, None], weight_row, send_rows).astype(jnp.bfloat16)
    buffer = exchange(send, "group")

    buffer_weight = buffer[:, high - 1, :capacity].astype(jnp.float32).reshape(slots, 1)
    buffer_rows = buffer[:, :capacity].reshape(slots, width)
    back_proj = across(buffer_rows, w_down)
    grad_gate, grad_up, gate_piece = gradients(
        back_proj, buffer_weight, pre_act[0].astype(jnp.float32), pre_act[1].astype(jnp.float32)
    )
    pieces = (across(grad_gate, w_gate) + across(grad_up, w_up)).reshape(group_count, capacity, width)
    gate_row = jnp.pad(
        gate_piece.reshape(group_count, 1, capacity), ((0, 0), (0, 0), (0, width - capacity))
    )
    pieces = jnp.pad(pieces, ((0, 0), (0, high - capacity), (0, 0)))
    back = exchange(jnp.where(last[None, :, None], gate_row, pieces).astype(jnp.bfloat16), "group")

    owned = jnp.dot(
        placement, back.reshape(group_count * high, width), preferred_element_type=jnp.float32
    ).astype(jnp.bfloat16)
    gates = back[:, high - 1, :high].reshape(group_count * high).astype(jnp.float32)
    gate_rows = jnp.sum(one_hot * gates, axis=2)
    final = exchange(pack(owned, gate_rows).reshape(inner_count, own, -1), "inner")
    total = jnp.sum(final.astype(jnp.float32), axis=0)
    return total[:, :width].astype(jnp.bfloat16), total[:, width : width + topk]


def solution(mesh):
    if mesh.size <= 64:
        group_count, inner_count = mesh.devices.shape
        devices = mesh.devices.reshape(group_count // CORES, CORES, inner_count)
        mesh, axes, on_device = Mesh(devices, ("row", "core", "inner")), ("row", "core", "inner"), flat
    else:
        axes, on_device = ("group", "inner"), staged
    token, hidden = P(axes, None), P(None, axes)
    return jax.shard_map(
        on_device,
        mesh=mesh,
        in_specs=(token, token, token, token, hidden, hidden, token, P(None, None, axes)),
        out_specs=(token, token),
        check_vma=False,
    )
```

```python
import functools

import jax
import jax.numpy as jnp
from jax import lax
from jax.experimental import pallas as pl
from jax.experimental.pallas import tpu as pltpu
from jax.sharding import Mesh, PartitionSpec as P

LANES = 128
CORES = 2
SAVED_ROWS = 32


def exchange(array, axis):
    return lax.all_to_all(array, axis, split_axis=0, concat_axis=0, tiled=True)


def pack(rows, *small):
    width = sum(s.shape[1] for s in small)
    fill = jnp.zeros((rows.shape[0], -width % LANES), rows.dtype)
    return jnp.concatenate([rows, *(s.astype(rows.dtype) for s in small), fill], axis=1)


def gradients(back_proj, weight, pre_gate, pre_up):
    gate_sig = jax.nn.sigmoid(pre_gate)
    swish_gate = pre_gate * gate_sig
    gate_piece = jnp.sum(swish_gate * pre_up * back_proj, axis=1, keepdims=True)
    scaled = weight * back_proj
    grad_up = (scaled * swish_gate).astype(jnp.bfloat16)
    grad_gate = (scaled * pre_up * gate_sig * (1.0 + pre_gate * (1.0 - gate_sig))).astype(
        jnp.bfloat16
    )
    return grad_gate, grad_up, gate_piece


def across(a, b):
    return lax.dot_general(a, b, (((1,), (1,)), ((), ())), preferred_element_type=jnp.float32)


def sizes(group_count, inner_count):
    split_count = min(8, inner_count // 4)
    return split_count, inner_count // split_count


def pack_kernel(
    out_grad, ids, slots, weights, w_gate, w_up, w_down, pre_act,
    sent, both, rows, words, reals, saved, small, sems,
):
    width, topk = w_gate.shape[0], ids.shape[1]
    first_down = 2 * width + 2 * SAVED_ROWS
    copies = [
        pltpu.make_async_copy(source, target, sems.at[at])
        for at, (source, target) in enumerate(
            (
                (ids, words.at[0]),
                (slots, words.at[1]),
                (weights, reals),
                (out_grad, rows),
                (pre_act, saved),
                (w_gate, both.at[:width]),
                (w_up, both.at[width : 2 * width]),
                *(
                    (w_down.at[:, at : at + LANES], both.at[first_down + at : first_down + at + LANES])
                    for at in range(0, width, LANES)
                ),
            )
        )
    ]
    for copy in copies:
        copy.start()
    small[...] = jnp.zeros_like(small)
    both[2 * width : first_down] = jnp.zeros((2 * SAVED_ROWS, LANES), both.dtype)
    for copy in copies[:5]:
        copy.wait()
    for at, part in enumerate((words[0], words[1], reals[...])):
        small[:, at * topk : (at + 1) * topk] = part.astype(jnp.float32)
    tail = small[...].astype(sent.dtype)
    own_rows = rows[...]
    for peer in range(sent.shape[0]):
        sent[peer, :, :width] = own_rows
        sent[peer, :, width:] = tail
    for at in range(2):
        first = 2 * width + at * SAVED_ROWS
        both[first : first + saved.shape[1]] = saved[at]
    for copy in copies[5:]:
        copy.wait()


def expert_kernel(topk, slots, arrived, both1, both2, out):
    half, width = arrived.shape[0], arrived.shape[1] - LANES
    row_count = lax.axis_size("row")
    peers = row_count * lax.axis_size("inner")
    capacity = slots // (row_count * CORES)
    split_count, experts_here = sizes(row_count * CORES, lax.axis_size("inner"))
    core = lax.axis_index("core")
    group_row = lax.axis_index("row") * CORES
    local_expert = lax.axis_index("inner") // split_count
    small = arrived[:, width:].astype(jnp.float32)
    lane = lax.broadcasted_iota(jnp.int32, small.shape, 1)
    peer = lax.broadcasted_iota(jnp.int32, (half, slots), 0) % peers
    source = peer // (peers // row_count)
    first = (source * CORES + core) * capacity
    column = lax.broadcasted_iota(jnp.int32, (half, slots), 1)

    def routed(group_core):
        expert = (group_row + group_core) * experts_here + local_expert
        mine = jnp.where(
            jnp.logical_and(small == expert.astype(jnp.float32), lane < topk), 1.0, 0.0
        )
        slot = jnp.sum(pltpu.roll(mine, topk, 1) * small, axis=1, keepdims=True)
        weight = jnp.sum(pltpu.roll(mine, 2 * topk, 1) * small, axis=1, keepdims=True)
        chosen = jnp.sum(mine, axis=1, keepdims=True)
        hit = jnp.logical_and(first + slot.astype(jnp.int32) == column, chosen > 0.5)
        return mine, weight, jnp.where(hit, 1.0, 0.0).astype(jnp.bfloat16)

    def backward(routing, back_proj, both):
        mine, weight, one_hot = routing
        pre_gate, pre_up = [
            jnp.dot(
                one_hot,
                both[2 * width + at * SAVED_ROWS : 2 * width + at * SAVED_ROWS + slots],
                preferred_element_type=jnp.float32,
            )
            for at in range(2)
        ]
        grad_gate, grad_up, gate_piece = gradients(back_proj, weight, pre_gate, pre_up)
        return grad_gate, grad_up, mine * gate_piece

    first_down = 2 * width + 2 * SAVED_ROWS
    down = [
        jnp.concatenate([b[first_down + at : first_down + at + LANES] for b in (both1, both2)])
        for at in range(0, width, LANES)
    ]
    back = across(arrived[:, :width], jnp.concatenate(down, axis=1))
    own, other = routed(core), routed(1 - core)
    grad_gate1, grad_up1, gates1 = backward(own, back[:, :LANES], both1)
    grad_gate2, grad_up2, gates2 = backward(other, back[:, LANES:], both2)
    grads = jnp.concatenate([grad_gate1, grad_up1, grad_gate2, grad_up2], axis=1)
    step = 512 if width % 512 == 0 else LANES
    for at in range(0, width, step):
        weights = [b[first + at : first + at + step] for b in (both1, both2) for first in (0, width)]
        pieces = across(grads, jnp.concatenate(weights, axis=1))
        out[:, at : at + step] = pieces.astype(out.dtype)
    out[:, width:] = (gates1 + gates2).astype(out.dtype)


def final_kernel(pieces, grad_rows, grad_gate, rows, gates, sems):
    width, topk = rows.shape[1], gates.shape[1]

    def summed(cols):
        total = pieces[0, :, cols].astype(jnp.float32)
        for peer in range(1, pieces.shape[0]):
            total = total + pieces[peer, :, cols].astype(jnp.float32)
        return total

    copies = [pltpu.make_async_copy(gates, grad_gate, sems.at[0])]
    gates[...] = summed(slice(width, width + LANES))[:, :topk]
    copies[0].start()
    for at in range(2):
        cols = slice(at * width // 2, (at + 1) * width // 2)
        rows[:, cols] = summed(cols).astype(rows.dtype)
        copies.append(
            pltpu.make_async_copy(rows.at[:, cols], grad_rows.at[:, cols], sems.at[1 + at])
        )
        copies[-1].start()
    for copy in copies:
        copy.wait()


def stay_in(space, *arrays):
    return [pltpu.with_memory_space_constraint(a, space) for a in arrays]


def swap_cores(array):
    return lax.ppermute(array, "core", [(0, 1), (1, 0)])


def flat(out_grad, routing_weight, expert_ids, slot_index, w_gate, w_up, w_down, pre_act):
    row_count = lax.axis_size("row")
    inner_count = lax.axis_size("inner")
    own, width = out_grad.shape
    topk = expert_ids.shape[1]
    peers = row_count * inner_count
    half = peers * own
    slots, hidden = pre_act.shape[1:]
    packed = width + LANES
    in_vmem = pl.BlockSpec(memory_space=pltpu.VMEM)
    in_hbm = pl.BlockSpec(memory_space=pltpu.HBM)
    bf16 = out_grad.dtype

    sent, both = pl.pallas_call(
        pack_kernel,
        out_shape=[
            jax.ShapeDtypeStruct((peers, own, packed), bf16),
            pltpu.VMEM((3 * width + 2 * SAVED_ROWS, hidden), bf16),
        ],
        in_specs=[in_hbm] * 8,
        out_specs=[in_vmem] * 2,
        scratch_shapes=[
            pltpu.VMEM((own, width), bf16),
            pltpu.VMEM((2, own, topk), expert_ids.dtype),
            pltpu.VMEM((own, topk), bf16),
            pltpu.VMEM(pre_act.shape, bf16),
            pltpu.VMEM((own, LANES), jnp.float32),
            pltpu.SemaphoreType.DMA((7 + width // LANES,)),
        ],
        compiler_params=pltpu.CompilerParams(vmem_limit_bytes=16 * 2**20),
        name="pack_rows",
    )(
        *stay_in(
            pltpu.HBM,
            *(out_grad, expert_ids, slot_index, routing_weight),
            *(w_gate, w_up, w_down, pre_act),
        )
    )
    both2 = swap_cores(both)
    arrived = exchange(sent, ("row", "inner"))
    arrived = jnp.swapaxes(arrived, 0, 1).reshape(half, packed)
    pieces = pl.pallas_call(
        functools.partial(expert_kernel, topk, slots),
        out_shape=jax.ShapeDtypeStruct((half, packed), bf16),
        in_specs=[in_vmem] * 3,
        out_specs=in_vmem,
        compiler_params=pltpu.CompilerParams(vmem_limit_bytes=16 * 2**20),
        cost_estimate=pl.CostEstimate(
            flops=12 * half * w_down.size,
            bytes_accessed=2 * (both.nbytes + arrived.nbytes),
            transcendentals=2 * half * hidden,
        ),
        name="expert_pieces",
    )(arrived, *stay_in(pltpu.VMEM, both, both2))
    pieces = jnp.swapaxes(pieces.reshape(own, peers, packed), 0, 1)
    returned = exchange(pieces, ("row", "inner"))
    return pl.pallas_call(
        final_kernel,
        out_shape=[
            jax.ShapeDtypeStruct((own, width), bf16),
            jax.ShapeDtypeStruct((own, topk), jnp.float32),
        ],
        in_specs=[in_vmem],
        out_specs=[in_hbm] * 2,
        scratch_shapes=[
            pltpu.VMEM((own, width), bf16),
            pltpu.VMEM((own, topk), jnp.float32),
            pltpu.SemaphoreType.DMA((3,)),
        ],
        compiler_params=pltpu.CompilerParams(vmem_limit_bytes=16 * 2**20),
        name="sum_pieces",
    )(returned)


def staged(out_grad, routing_weight, expert_ids, slot_index, w_gate, w_up, w_down, pre_act):
    group_count = lax.axis_size("group")
    inner_count = lax.axis_size("inner")
    own, width = out_grad.shape
    topk = expert_ids.shape[1]
    split_count, experts_here = sizes(group_count, inner_count)
    local_expert = lax.axis_index("inner") // split_count
    block = inner_count * own
    slots = pre_act.shape[1]
    capacity = slots // group_count
    high = -(-(capacity + 1) // 8) * 8

    payload = pack(out_grad, expert_ids, slot_index, routing_weight)
    sent = jnp.broadcast_to(payload[None], (inner_count,) + payload.shape)
    arrived = exchange(sent, "inner").reshape(block, payload.shape[1])
    rows = arrived[:, :width]
    small = arrived[:, width : width + 3 * topk].astype(jnp.float32)
    ids = small[:, :topk].astype(jnp.int32)
    slot = small[:, topk : 2 * topk].astype(jnp.int32)
    weight = small[:, 2 * topk :]
    selected = ids % experts_here == local_expert
    column = ids // experts_here * high + slot
    one_hot = jnp.logical_and(
        column[:, :, None] == jnp.arange(group_count * high, dtype=jnp.int32), selected[:, :, None]
    ).astype(jnp.float32)
    placement = jnp.sum(one_hot, axis=1).astype(jnp.bfloat16)
    send_weight = jnp.sum(one_hot * weight[:, :, None], axis=(0, 1)).reshape(group_count, 1, high)
    send_rows = lax.dot_general(
        placement, rows, (((0,), (0,)), ((), ())), preferred_element_type=jnp.float32
    ).reshape(group_count, high, width)
    last = jnp.arange(high) == high - 1
    weight_row = jnp.pad(send_weight, ((0, 0), (0, 0), (0, width - high)))
    send = jnp.where(last[None, :, None], weight_row, send_rows).astype(jnp.bfloat16)
    buffer = exchange(send, "group")

    buffer_weight = buffer[:, high - 1, :capacity].astype(jnp.float32).reshape(slots, 1)
    buffer_rows = buffer[:, :capacity].reshape(slots, width)
    back_proj = across(buffer_rows, w_down)
    grad_gate, grad_up, gate_piece = gradients(
        back_proj, buffer_weight, pre_act[0].astype(jnp.float32), pre_act[1].astype(jnp.float32)
    )
    pieces = (across(grad_gate, w_gate) + across(grad_up, w_up)).reshape(group_count, capacity, width)
    gate_row = jnp.pad(
        gate_piece.reshape(group_count, 1, capacity), ((0, 0), (0, 0), (0, width - capacity))
    )
    pieces = jnp.pad(pieces, ((0, 0), (0, high - capacity), (0, 0)))
    back = exchange(jnp.where(last[None, :, None], gate_row, pieces).astype(jnp.bfloat16), "group")

    owned = jnp.dot(
        placement, back.reshape(group_count * high, width), preferred_element_type=jnp.float32
    ).astype(jnp.bfloat16)
    gates = back[:, high - 1, :high].reshape(group_count * high).astype(jnp.float32)
    gate_rows = jnp.sum(one_hot * gates, axis=2)
    final = exchange(pack(owned, gate_rows).reshape(inner_count, own, -1), "inner")
    total = jnp.sum(final.astype(jnp.float32), axis=0)
    return total[:, :width].astype(jnp.bfloat16), total[:, width : width + topk]


def solution(mesh):
    if mesh.size <= 64:
        group_count, inner_count = mesh.devices.shape
        devices = mesh.devices.reshape(group_count // CORES, CORES, inner_count)
        mesh, axes, on_device = Mesh(devices, ("row", "core", "inner")), ("row", "core", "inner"), flat
    else:
        axes, on_device = ("group", "inner"), staged
    token, hidden = P(axes, None), P(None, axes)
    return jax.shard_map(
        on_device,
        mesh=mesh,
        in_specs=(token, token, token, token, hidden, hidden, token, P(None, None, axes)),
        out_specs=(token, token),
        check_vma=False,
    )
```

```python
import functools

import jax
import jax.numpy as jnp
from jax import lax
from jax.experimental import pallas as pl
from jax.experimental.pallas import tpu as pltpu
from jax.sharding import Mesh, PartitionSpec as P

LANES = 128
CORES = 2
SAVED_ROWS = 32


def exchange(array, axis):
    return lax.all_to_all(array, axis, split_axis=0, concat_axis=0, tiled=True)


def pack(rows, *small):
    width = sum(s.shape[1] for s in small)
    fill = jnp.zeros((rows.shape[0], -width % LANES), rows.dtype)
    return jnp.concatenate([rows, *(s.astype(rows.dtype) for s in small), fill], axis=1)


def gradients(back_proj, weight, pre_gate, pre_up):
    gate_sig = jax.nn.sigmoid(pre_gate)
    swish_gate = pre_gate * gate_sig
    gate_piece = jnp.sum(swish_gate * pre_up * back_proj, axis=1, keepdims=True)
    scaled = weight * back_proj
    grad_up = (scaled * swish_gate).astype(jnp.bfloat16)
    grad_gate = (scaled * pre_up * gate_sig * (1.0 + pre_gate * (1.0 - gate_sig))).astype(
        jnp.bfloat16
    )
    return grad_gate, grad_up, gate_piece


def across(a, b):
    return lax.dot_general(a, b, (((1,), (1,)), ((), ())), preferred_element_type=jnp.float32)


def sizes(group_count, inner_count):
    split_count = min(8, inner_count // 4)
    return split_count, inner_count // split_count


def pack_kernel(
    out_grad, ids, slots, weights, w_gate, w_up, w_down, pre_act,
    sent, both, rows, words, reals, saved, small, sems,
):
    width, topk = w_gate.shape[0], ids.shape[1]
    first_down = 2 * width + 2 * SAVED_ROWS
    copies = [
        pltpu.make_async_copy(source, target, sems.at[at])
        for at, (source, target) in enumerate(
            (
                (ids, words.at[0]),
                (slots, words.at[1]),
                (weights, reals),
                (out_grad, rows),
                (pre_act, saved),
                (w_gate, both.at[:width]),
                (w_up, both.at[width : 2 * width]),
                *(
                    (w_down.at[:, at : at + LANES], both.at[first_down + at : first_down + at + LANES])
                    for at in range(0, width, LANES)
                ),
            )
        )
    ]
    for copy in copies:
        copy.start()
    small[...] = jnp.zeros_like(small)
    both[2 * width : first_down] = jnp.zeros((2 * SAVED_ROWS, LANES), both.dtype)
    for copy in copies[:5]:
        copy.wait()
    for at, part in enumerate((words[0], words[1], reals[...])):
        small[:, at * topk : (at + 1) * topk] = part.astype(jnp.float32)
    tail = small[...].astype(sent.dtype)
    own_rows = rows[...]
    for peer in range(sent.shape[0]):
        sent[peer, :, :width] = own_rows
        sent[peer, :, width:] = tail
    for at in range(2):
        first = 2 * width + at * SAVED_ROWS
        both[first : first + saved.shape[1]] = saved[at]
    for copy in copies[5:]:
        copy.wait()


def expert_kernel(topk, slots, arrived, both1, both2, out):
    half, width = arrived.shape[0], arrived.shape[1] - LANES
    row_count = lax.axis_size("row")
    peers = row_count * lax.axis_size("inner")
    capacity = slots // (row_count * CORES)
    split_count, experts_here = sizes(row_count * CORES, lax.axis_size("inner"))
    core = lax.axis_index("core")
    group_row = lax.axis_index("row") * CORES
    local_expert = lax.axis_index("inner") // split_count
    small = arrived[:, width:].astype(jnp.float32)
    lane = lax.broadcasted_iota(jnp.int32, small.shape, 1)
    peer = lax.broadcasted_iota(jnp.int32, (half, slots), 0) % peers
    source = peer // (peers // row_count)
    first = (source * CORES + core) * capacity
    column = lax.broadcasted_iota(jnp.int32, (half, slots), 1)

    def routed(group_core):
        expert = (group_row + group_core) * experts_here + local_expert
        mine = jnp.where(
            jnp.logical_and(small == expert.astype(jnp.float32), lane < topk), 1.0, 0.0
        )
        slot = jnp.sum(pltpu.roll(mine, topk, 1) * small, axis=1, keepdims=True)
        weight = jnp.sum(pltpu.roll(mine, 2 * topk, 1) * small, axis=1, keepdims=True)
        chosen = jnp.sum(mine, axis=1, keepdims=True)
        hit = jnp.logical_and(first + slot.astype(jnp.int32) == column, chosen > 0.5)
        return mine, weight, jnp.where(hit, 1.0, 0.0).astype(jnp.bfloat16)

    def backward(routing, back_proj, both):
        mine, weight, one_hot = routing
        pre_gate, pre_up = [
            jnp.dot(
                one_hot,
                both[2 * width + at * SAVED_ROWS : 2 * width + at * SAVED_ROWS + slots],
                preferred_element_type=jnp.float32,
            )
            for at in range(2)
        ]
        grad_gate, grad_up, gate_piece = gradients(back_proj, weight, pre_gate, pre_up)
        return grad_gate, grad_up, mine * gate_piece

    def back(both):
        first = 2 * width + 2 * SAVED_ROWS
        blocks = [both[first + at : first + at + LANES] for at in range(0, width, LANES)]
        return across(rows, jnp.concatenate(blocks, axis=1))

    rows = arrived[:, :width]
    own, other = routed(core), routed(1 - core)
    grad_gate1, grad_up1, gates1 = backward(own, back(both1), both1)
    grad_gate2, grad_up2, gates2 = backward(other, back(both2), both2)
    grads1 = jnp.concatenate([grad_gate1, grad_up1], axis=1)
    grads2 = jnp.concatenate([grad_gate2, grad_up2], axis=1)

    def pieces(grads, both, at):
        weights = [both[first + at : first + at + step] for first in (0, width)]
        return across(grads, jnp.concatenate(weights, axis=1))

    step = 512 if width % 512 == 0 else LANES
    for at in range(0, width, step):
        total = pieces(grads1, both1, at) + pieces(grads2, both2, at)
        out[:, at : at + step] = total.astype(out.dtype)
    out[:, width:] = (gates1 + gates2).astype(out.dtype)


def final_kernel(pieces, grad_rows, grad_gate, rows, gates, sems):
    width, topk = rows.shape[1], gates.shape[1]

    def summed(cols):
        total = pieces[0, :, cols].astype(jnp.float32)
        for peer in range(1, pieces.shape[0]):
            total = total + pieces[peer, :, cols].astype(jnp.float32)
        return total

    copies = [pltpu.make_async_copy(gates, grad_gate, sems.at[0])]
    gates[...] = summed(slice(width, width + LANES))[:, :topk]
    copies[0].start()
    for at in range(2):
        cols = slice(at * width // 2, (at + 1) * width // 2)
        rows[:, cols] = summed(cols).astype(rows.dtype)
        copies.append(
            pltpu.make_async_copy(rows.at[:, cols], grad_rows.at[:, cols], sems.at[1 + at])
        )
        copies[-1].start()
    for copy in copies:
        copy.wait()


def stay_in(space, *arrays):
    return [pltpu.with_memory_space_constraint(a, space) for a in arrays]


def swap_cores(array):
    return lax.ppermute(array, "core", [(0, 1), (1, 0)])


def flat(out_grad, routing_weight, expert_ids, slot_index, w_gate, w_up, w_down, pre_act):
    row_count = lax.axis_size("row")
    inner_count = lax.axis_size("inner")
    own, width = out_grad.shape
    topk = expert_ids.shape[1]
    peers = row_count * inner_count
    half = peers * own
    slots, hidden = pre_act.shape[1:]
    packed = width + LANES
    in_vmem = pl.BlockSpec(memory_space=pltpu.VMEM)
    in_hbm = pl.BlockSpec(memory_space=pltpu.HBM)
    bf16 = out_grad.dtype

    sent, both = pl.pallas_call(
        pack_kernel,
        out_shape=[
            jax.ShapeDtypeStruct((peers, own, packed), bf16),
            pltpu.VMEM((3 * width + 2 * SAVED_ROWS, hidden), bf16),
        ],
        in_specs=[in_hbm] * 8,
        out_specs=[in_vmem] * 2,
        scratch_shapes=[
            pltpu.VMEM((own, width), bf16),
            pltpu.VMEM((2, own, topk), expert_ids.dtype),
            pltpu.VMEM((own, topk), bf16),
            pltpu.VMEM(pre_act.shape, bf16),
            pltpu.VMEM((own, LANES), jnp.float32),
            pltpu.SemaphoreType.DMA((7 + width // LANES,)),
        ],
        compiler_params=pltpu.CompilerParams(vmem_limit_bytes=16 * 2**20),
        name="pack_rows",
    )(
        *stay_in(
            pltpu.HBM,
            *(out_grad, expert_ids, slot_index, routing_weight),
            *(w_gate, w_up, w_down, pre_act),
        )
    )
    both2 = swap_cores(both)
    arrived = exchange(sent, ("row", "inner"))
    arrived = jnp.swapaxes(arrived, 0, 1).reshape(half, packed)
    pieces = pl.pallas_call(
        functools.partial(expert_kernel, topk, slots),
        out_shape=jax.ShapeDtypeStruct((half, packed), bf16),
        in_specs=[in_vmem] * 3,
        out_specs=in_vmem,
        compiler_params=pltpu.CompilerParams(vmem_limit_bytes=16 * 2**20),
        cost_estimate=pl.CostEstimate(
            flops=12 * half * w_down.size,
            bytes_accessed=2 * (both.nbytes + arrived.nbytes),
            transcendentals=2 * half * hidden,
        ),
        name="expert_pieces",
    )(arrived, *stay_in(pltpu.VMEM, both, both2))
    pieces = jnp.swapaxes(pieces.reshape(own, peers, packed), 0, 1)
    returned = exchange(pieces, ("row", "inner"))
    return pl.pallas_call(
        final_kernel,
        out_shape=[
            jax.ShapeDtypeStruct((own, width), bf16),
            jax.ShapeDtypeStruct((own, topk), jnp.float32),
        ],
        in_specs=[in_vmem],
        out_specs=[in_hbm] * 2,
        scratch_shapes=[
            pltpu.VMEM((own, width), bf16),
            pltpu.VMEM((own, topk), jnp.float32),
            pltpu.SemaphoreType.DMA((3,)),
        ],
        compiler_params=pltpu.CompilerParams(vmem_limit_bytes=16 * 2**20),
        name="sum_pieces",
    )(returned)


def staged(out_grad, routing_weight, expert_ids, slot_index, w_gate, w_up, w_down, pre_act):
    group_count = lax.axis_size("group")
    inner_count = lax.axis_size("inner")
    own, width = out_grad.shape
    topk = expert_ids.shape[1]
    split_count, experts_here = sizes(group_count, inner_count)
    local_expert = lax.axis_index("inner") // split_count
    block = inner_count * own
    slots = pre_act.shape[1]
    capacity = slots // group_count
    high = -(-(capacity + 1) // 8) * 8

    payload = pack(out_grad, expert_ids, slot_index, routing_weight)
    sent = jnp.broadcast_to(payload[None], (inner_count,) + payload.shape)
    arrived = exchange(sent, "inner").reshape(block, payload.shape[1])
    rows = arrived[:, :width]
    small = arrived[:, width : width + 3 * topk].astype(jnp.float32)
    ids = small[:, :topk].astype(jnp.int32)
    slot = small[:, topk : 2 * topk].astype(jnp.int32)
    weight = small[:, 2 * topk :]
    selected = ids % experts_here == local_expert
    column = ids // experts_here * high + slot
    one_hot = jnp.logical_and(
        column[:, :, None] == jnp.arange(group_count * high, dtype=jnp.int32), selected[:, :, None]
    ).astype(jnp.float32)
    placement = jnp.sum(one_hot, axis=1).astype(jnp.bfloat16)
    send_weight = jnp.sum(one_hot * weight[:, :, None], axis=(0, 1)).reshape(group_count, 1, high)
    send_rows = lax.dot_general(
        placement, rows, (((0,), (0,)), ((), ())), preferred_element_type=jnp.float32
    ).reshape(group_count, high, width)
    last = jnp.arange(high) == high - 1
    weight_row = jnp.pad(send_weight, ((0, 0), (0, 0), (0, width - high)))
    send = jnp.where(last[None, :, None], weight_row, send_rows).astype(jnp.bfloat16)
    buffer = exchange(send, "group")

    buffer_weight = buffer[:, high - 1, :capacity].astype(jnp.float32).reshape(slots, 1)
    buffer_rows = buffer[:, :capacity].reshape(slots, width)
    back_proj = across(buffer_rows, w_down)
    grad_gate, grad_up, gate_piece = gradients(
        back_proj, buffer_weight, pre_act[0].astype(jnp.float32), pre_act[1].astype(jnp.float32)
    )
    pieces = (across(grad_gate, w_gate) + across(grad_up, w_up)).reshape(group_count, capacity, width)
    gate_row = jnp.pad(
        gate_piece.reshape(group_count, 1, capacity), ((0, 0), (0, 0), (0, width - capacity))
    )
    pieces = jnp.pad(pieces, ((0, 0), (0, high - capacity), (0, 0)))
    back = exchange(jnp.where(last[None, :, None], gate_row, pieces).astype(jnp.bfloat16), "group")

    owned = jnp.dot(
        placement, back.reshape(group_count * high, width), preferred_element_type=jnp.float32
    ).astype(jnp.bfloat16)
    gates = back[:, high - 1, :high].reshape(group_count * high).astype(jnp.float32)
    gate_rows = jnp.sum(one_hot * gates, axis=2)
    final = exchange(pack(owned, gate_rows).reshape(inner_count, own, -1), "inner")
    total = jnp.sum(final.astype(jnp.float32), axis=0)
    return total[:, :width].astype(jnp.bfloat16), total[:, width : width + topk]


def solution(mesh):
    if mesh.size <= 64:
        group_count, inner_count = mesh.devices.shape
        devices = mesh.devices.reshape(group_count // CORES, CORES, inner_count)
        mesh, axes, on_device = Mesh(devices, ("row", "core", "inner")), ("row", "core", "inner"), flat
    else:
        axes, on_device = ("group", "inner"), staged
    token, hidden = P(axes, None), P(None, axes)
    return jax.shard_map(
        on_device,
        mesh=mesh,
        in_specs=(token, token, token, token, hidden, hidden, token, P(None, None, axes)),
        out_specs=(token, token),
        check_vma=False,
    )
```

```python
import functools

import jax
import jax.numpy as jnp
from jax import lax
from jax.experimental import pallas as pl
from jax.experimental.pallas import tpu as pltpu
from jax.sharding import Mesh, PartitionSpec as P

LANES = 128
CORES = 2
SAVED_ROWS = 32


def exchange(array, axis):
    return lax.all_to_all(array, axis, split_axis=0, concat_axis=0, tiled=True)


def pack(rows, *small):
    width = sum(s.shape[1] for s in small)
    fill = jnp.zeros((rows.shape[0], -width % LANES), rows.dtype)
    return jnp.concatenate([rows, *(s.astype(rows.dtype) for s in small), fill], axis=1)


def gradients(back_proj, weight, pre_gate, pre_up):
    gate_sig = jax.nn.sigmoid(pre_gate)
    swish_gate = pre_gate * gate_sig
    gate_piece = jnp.sum(swish_gate * pre_up * back_proj, axis=1, keepdims=True)
    scaled = weight * back_proj
    grad_up = (scaled * swish_gate).astype(jnp.bfloat16)
    grad_gate = (scaled * pre_up * gate_sig * (1.0 + pre_gate * (1.0 - gate_sig))).astype(
        jnp.bfloat16
    )
    return grad_gate, grad_up, gate_piece


def across(a, b):
    return lax.dot_general(a, b, (((1,), (1,)), ((), ())), preferred_element_type=jnp.float32)


def sizes(group_count, inner_count):
    split_count = min(8, inner_count // 4)
    return split_count, inner_count // split_count


def pack_kernel(
    out_grad, ids, slots, weights, w_gate, w_up, w_down, pre_act,
    sent, both, rows, words, reals, saved, small, sems,
):
    width, topk = w_gate.shape[0], ids.shape[1]
    first_down = 2 * width + 2 * SAVED_ROWS
    copies = [
        pltpu.make_async_copy(source, target, sems.at[at])
        for at, (source, target) in enumerate(
            (
                (ids, words.at[0]),
                (slots, words.at[1]),
                (weights, reals),
                (out_grad, rows),
                (pre_act, saved),
                (w_gate, both.at[:width]),
                (w_up, both.at[width : 2 * width]),
                *(
                    (w_down.at[:, at : at + LANES], both.at[first_down + at : first_down + at + LANES])
                    for at in range(0, width, LANES)
                ),
            )
        )
    ]
    for copy in copies:
        copy.start()
    small[...] = jnp.zeros_like(small)
    both[2 * width : first_down] = jnp.zeros((2 * SAVED_ROWS, LANES), both.dtype)
    for copy in copies[:5]:
        copy.wait()
    for at, part in enumerate((words[0], words[1], reals[...])):
        small[:, at * topk : (at + 1) * topk] = part.astype(jnp.float32)
    tail = small[...].astype(sent.dtype)
    own_rows = rows[...]
    for peer in range(sent.shape[0]):
        sent[peer, :, :width] = own_rows
        sent[peer, :, width:] = tail
    for at in range(2):
        first = 2 * width + at * SAVED_ROWS
        both[first : first + saved.shape[1]] = saved[at]
    for copy in copies[5:]:
        copy.wait()


def expert_kernel(topk, slots, arrived, both1, both2, out):
    half, width = arrived.shape[0], arrived.shape[1] - LANES
    row_count = lax.axis_size("row")
    peers = row_count * lax.axis_size("inner")
    capacity = slots // (row_count * CORES)
    split_count, experts_here = sizes(row_count * CORES, lax.axis_size("inner"))
    core = lax.axis_index("core")
    group_row = lax.axis_index("row") * CORES
    local_expert = lax.axis_index("inner") // split_count
    small = arrived[:, width:].astype(jnp.float32)
    lane = lax.broadcasted_iota(jnp.int32, small.shape, 1)
    peer = lax.broadcasted_iota(jnp.int32, (half, slots), 0) % peers
    source = peer // (peers // row_count)
    first = (source * CORES + core) * capacity
    column = lax.broadcasted_iota(jnp.int32, (half, slots), 1)

    def routed(group_core):
        expert = (group_row + group_core) * experts_here + local_expert
        mine = jnp.where(
            jnp.logical_and(small == expert.astype(jnp.float32), lane < topk), 1.0, 0.0
        )
        slot = jnp.sum(pltpu.roll(mine, topk, 1) * small, axis=1, keepdims=True)
        weight = jnp.sum(pltpu.roll(mine, 2 * topk, 1) * small, axis=1, keepdims=True)
        chosen = jnp.sum(mine, axis=1, keepdims=True)
        hit = jnp.logical_and(first + slot.astype(jnp.int32) == column, chosen > 0.5)
        return mine, weight, jnp.where(hit, 1.0, 0.0).astype(jnp.bfloat16)

    def backward(routing, back_proj, both):
        mine, weight, one_hot = routing
        pre_gate, pre_up = [
            jnp.dot(
                one_hot,
                both[2 * width + at * SAVED_ROWS : 2 * width + at * SAVED_ROWS + slots],
                preferred_element_type=jnp.float32,
            )
            for at in range(2)
        ]
        grad_gate, grad_up, gate_piece = gradients(back_proj, weight, pre_gate, pre_up)
        return grad_gate, grad_up, mine * gate_piece

    def back(both):
        first = 2 * width + 2 * SAVED_ROWS
        blocks = [both[first + at : first + at + LANES] for at in range(0, width, LANES)]
        return across(rows, jnp.concatenate(blocks, axis=1))

    rows = arrived[:, :width]
    own, other = routed(core), routed(1 - core)
    grad_gate1, grad_up1, gates1 = backward(own, back(both1), both1)
    grad_gate2, grad_up2, gates2 = backward(other, back(both2), both2)
    grads = jnp.concatenate([grad_gate1, grad_up1, grad_gate2, grad_up2], axis=1)
    step = width // 4
    for at in range(0, width, step):
        weights = [b[first + at : first + at + step] for b in (both1, both2) for first in (0, width)]
        pieces = across(grads, jnp.concatenate(weights, axis=1))
        out[:, at : at + step] = pieces.astype(out.dtype)
    out[:, width:] = (gates1 + gates2).astype(out.dtype)


def final_kernel(pieces, grad_rows, grad_gate, rows, gates, sems):
    width, topk = rows.shape[1], gates.shape[1]

    def summed(cols):
        total = pieces[0, :, cols].astype(jnp.float32)
        for peer in range(1, pieces.shape[0]):
            total = total + pieces[peer, :, cols].astype(jnp.float32)
        return total

    copies = [pltpu.make_async_copy(gates, grad_gate, sems.at[0])]
    gates[...] = summed(slice(width, width + LANES))[:, :topk]
    copies[0].start()
    for at in range(2):
        cols = slice(at * width // 2, (at + 1) * width // 2)
        rows[:, cols] = summed(cols).astype(rows.dtype)
        copies.append(
            pltpu.make_async_copy(rows.at[:, cols], grad_rows.at[:, cols], sems.at[1 + at])
        )
        copies[-1].start()
    for copy in copies:
        copy.wait()


def stay_in(space, *arrays):
    return [pltpu.with_memory_space_constraint(a, space) for a in arrays]


def swap_cores(array):
    return lax.ppermute(array, "core", [(0, 1), (1, 0)])


def flat(out_grad, routing_weight, expert_ids, slot_index, w_gate, w_up, w_down, pre_act):
    row_count = lax.axis_size("row")
    inner_count = lax.axis_size("inner")
    own, width = out_grad.shape
    topk = expert_ids.shape[1]
    peers = row_count * inner_count
    half = peers * own
    slots, hidden = pre_act.shape[1:]
    packed = width + LANES
    in_vmem = pl.BlockSpec(memory_space=pltpu.VMEM)
    in_hbm = pl.BlockSpec(memory_space=pltpu.HBM)
    bf16 = out_grad.dtype

    sent, both = pl.pallas_call(
        pack_kernel,
        out_shape=[
            jax.ShapeDtypeStruct((peers, own, packed), bf16),
            pltpu.VMEM((3 * width + 2 * SAVED_ROWS, hidden), bf16),
        ],
        in_specs=[in_hbm] * 8,
        out_specs=[in_vmem] * 2,
        scratch_shapes=[
            pltpu.VMEM((own, width), bf16),
            pltpu.VMEM((2, own, topk), expert_ids.dtype),
            pltpu.VMEM((own, topk), bf16),
            pltpu.VMEM(pre_act.shape, bf16),
            pltpu.VMEM((own, LANES), jnp.float32),
            pltpu.SemaphoreType.DMA((7 + width // LANES,)),
        ],
        compiler_params=pltpu.CompilerParams(vmem_limit_bytes=16 * 2**20),
        name="pack_rows",
    )(
        *stay_in(
            pltpu.HBM,
            *(out_grad, expert_ids, slot_index, routing_weight),
            *(w_gate, w_up, w_down, pre_act),
        )
    )
    both2 = swap_cores(both)
    arrived = exchange(sent, ("row", "inner"))
    arrived = jnp.swapaxes(arrived, 0, 1).reshape(half, packed)
    pieces = pl.pallas_call(
        functools.partial(expert_kernel, topk, slots),
        out_shape=jax.ShapeDtypeStruct((half, packed), bf16),
        in_specs=[in_vmem] * 3,
        out_specs=in_vmem,
        compiler_params=pltpu.CompilerParams(vmem_limit_bytes=16 * 2**20),
        cost_estimate=pl.CostEstimate(
            flops=12 * half * w_down.size,
            bytes_accessed=2 * (both.nbytes + arrived.nbytes),
            transcendentals=2 * half * hidden,
        ),
        name="expert_pieces",
    )(arrived, *stay_in(pltpu.VMEM, both, both2))
    pieces = jnp.swapaxes(pieces.reshape(own, peers, packed), 0, 1)
    returned = exchange(pieces, ("row", "inner"))
    return pl.pallas_call(
        final_kernel,
        out_shape=[
            jax.ShapeDtypeStruct((own, width), bf16),
            jax.ShapeDtypeStruct((own, topk), jnp.float32),
        ],
        in_specs=[in_vmem],
        out_specs=[in_hbm] * 2,
        scratch_shapes=[
            pltpu.VMEM((own, width), bf16),
            pltpu.VMEM((own, topk), jnp.float32),
            pltpu.SemaphoreType.DMA((3,)),
        ],
        compiler_params=pltpu.CompilerParams(vmem_limit_bytes=16 * 2**20),
        name="sum_pieces",
    )(returned)


def staged(out_grad, routing_weight, expert_ids, slot_index, w_gate, w_up, w_down, pre_act):
    group_count = lax.axis_size("group")
    inner_count = lax.axis_size("inner")
    own, width = out_grad.shape
    topk = expert_ids.shape[1]
    split_count, experts_here = sizes(group_count, inner_count)
    local_expert = lax.axis_index("inner") // split_count
    block = inner_count * own
    slots = pre_act.shape[1]
    capacity = slots // group_count
    high = -(-(capacity + 1) // 8) * 8

    payload = pack(out_grad, expert_ids, slot_index, routing_weight)
    sent = jnp.broadcast_to(payload[None], (inner_count,) + payload.shape)
    arrived = exchange(sent, "inner").reshape(block, payload.shape[1])
    rows = arrived[:, :width]
    small = arrived[:, width : width + 3 * topk].astype(jnp.float32)
    ids = small[:, :topk].astype(jnp.int32)
    slot = small[:, topk : 2 * topk].astype(jnp.int32)
    weight = small[:, 2 * topk :]
    selected = ids % experts_here == local_expert
    column = ids // experts_here * high + slot
    one_hot = jnp.logical_and(
        column[:, :, None] == jnp.arange(group_count * high, dtype=jnp.int32), selected[:, :, None]
    ).astype(jnp.float32)
    placement = jnp.sum(one_hot, axis=1).astype(jnp.bfloat16)
    send_weight = jnp.sum(one_hot * weight[:, :, None], axis=(0, 1)).reshape(group_count, 1, high)
    send_rows = lax.dot_general(
        placement, rows, (((0,), (0,)), ((), ())), preferred_element_type=jnp.float32
    ).reshape(group_count, high, width)
    last = jnp.arange(high) == high - 1
    weight_row = jnp.pad(send_weight, ((0, 0), (0, 0), (0, width - high)))
    send = jnp.where(last[None, :, None], weight_row, send_rows).astype(jnp.bfloat16)
    buffer = exchange(send, "group")

    buffer_weight = buffer[:, high - 1, :capacity].astype(jnp.float32).reshape(slots, 1)
    buffer_rows = buffer[:, :capacity].reshape(slots, width)
    back_proj = across(buffer_rows, w_down)
    grad_gate, grad_up, gate_piece = gradients(
        back_proj, buffer_weight, pre_act[0].astype(jnp.float32), pre_act[1].astype(jnp.float32)
    )
    pieces = (across(grad_gate, w_gate) + across(grad_up, w_up)).reshape(group_count, capacity, width)
    gate_row = jnp.pad(
        gate_piece.reshape(group_count, 1, capacity), ((0, 0), (0, 0), (0, width - capacity))
    )
    pieces = jnp.pad(pieces, ((0, 0), (0, high - capacity), (0, 0)))
    back = exchange(jnp.where(last[None, :, None], gate_row, pieces).astype(jnp.bfloat16), "group")

    owned = jnp.dot(
        placement, back.reshape(group_count * high, width), preferred_element_type=jnp.float32
    ).astype(jnp.bfloat16)
    gates = back[:, high - 1, :high].reshape(group_count * high).astype(jnp.float32)
    gate_rows = jnp.sum(one_hot * gates, axis=2)
    final = exchange(pack(owned, gate_rows).reshape(inner_count, own, -1), "inner")
    total = jnp.sum(final.astype(jnp.float32), axis=0)
    return total[:, :width].astype(jnp.bfloat16), total[:, width : width + topk]


def solution(mesh):
    if mesh.size <= 64:
        group_count, inner_count = mesh.devices.shape
        devices = mesh.devices.reshape(group_count // CORES, CORES, inner_count)
        mesh, axes, on_device = Mesh(devices, ("row", "core", "inner")), ("row", "core", "inner"), flat
    else:
        axes, on_device = ("group", "inner"), staged
    token, hidden = P(axes, None), P(None, axes)
    return jax.shard_map(
        on_device,
        mesh=mesh,
        in_specs=(token, token, token, token, hidden, hidden, token, P(None, None, axes)),
        out_specs=(token, token),
        check_vma=False,
    )
```

```python
import functools

import jax
import jax.numpy as jnp
from jax import lax
from jax.experimental import pallas as pl
from jax.experimental.pallas import tpu as pltpu
from jax.sharding import Mesh, PartitionSpec as P

LANES = 128
CORES = 2
SAVED_ROWS = 32


def exchange(array, axis):
    return lax.all_to_all(array, axis, split_axis=0, concat_axis=0, tiled=True)


def pack(rows, *small):
    width = sum(s.shape[1] for s in small)
    fill = jnp.zeros((rows.shape[0], -width % LANES), rows.dtype)
    return jnp.concatenate([rows, *(s.astype(rows.dtype) for s in small), fill], axis=1)


def gradients(back_proj, weight, pre_gate, pre_up):
    gate_sig = jax.nn.sigmoid(pre_gate)
    swish_gate = pre_gate * gate_sig
    gate_piece = jnp.sum(swish_gate * pre_up * back_proj, axis=1, keepdims=True)
    scaled = weight * back_proj
    grad_up = (scaled * swish_gate).astype(jnp.bfloat16)
    grad_gate = (scaled * pre_up * gate_sig * (1.0 + pre_gate * (1.0 - gate_sig))).astype(
        jnp.bfloat16
    )
    return grad_gate, grad_up, gate_piece


def across(a, b):
    return lax.dot_general(a, b, (((1,), (1,)), ((), ())), preferred_element_type=jnp.float32)


def sizes(group_count, inner_count):
    split_count = min(8, inner_count // 4)
    return split_count, inner_count // split_count


def pack_kernel(
    out_grad, ids, slots, weights, w_gate, w_up, w_down, pre_act,
    sent, both, rows, words, reals, saved, small, sems,
):
    width, topk = w_gate.shape[0], ids.shape[1]
    first_down = 2 * width + 2 * SAVED_ROWS
    copies = [
        pltpu.make_async_copy(source, target, sems.at[at])
        for at, (source, target) in enumerate(
            (
                (ids, words.at[0]),
                (slots, words.at[1]),
                (weights, reals),
                (out_grad, rows),
                (pre_act, saved),
                (w_gate, both.at[:width]),
                (w_up, both.at[width : 2 * width]),
                *(
                    (w_down.at[:, at : at + LANES], both.at[first_down + at : first_down + at + LANES])
                    for at in range(0, width, LANES)
                ),
            )
        )
    ]
    for copy in copies:
        copy.start()
    small[...] = jnp.zeros_like(small)
    both[2 * width : first_down] = jnp.zeros((2 * SAVED_ROWS, LANES), both.dtype)
    for copy in copies[:5]:
        copy.wait()
    for at, part in enumerate((words[0], words[1], reals[...])):
        small[:, at * topk : (at + 1) * topk] = part.astype(jnp.float32)
    tail = small[...].astype(sent.dtype)
    own_rows = rows[...]
    for peer in range(sent.shape[0]):
        sent[peer, :, :width] = own_rows
        sent[peer, :, width:] = tail
    for at in range(2):
        first = 2 * width + at * SAVED_ROWS
        both[first : first + saved.shape[1]] = saved[at]
    for copy in copies[5:]:
        copy.wait()


def expert_kernel(topk, slots, arrived, both1, both2, out):
    half, width = arrived.shape[0], arrived.shape[1] - LANES
    row_count = lax.axis_size("row")
    peers = row_count * lax.axis_size("inner")
    capacity = slots // (row_count * CORES)
    split_count, experts_here = sizes(row_count * CORES, lax.axis_size("inner"))
    core = lax.axis_index("core")
    group_row = lax.axis_index("row") * CORES
    local_expert = lax.axis_index("inner") // split_count
    small = arrived[:, width:].astype(jnp.float32)
    lane = lax.broadcasted_iota(jnp.int32, small.shape, 1)
    peer = lax.broadcasted_iota(jnp.int32, (half, slots), 0) % peers
    source = peer // (peers // row_count)
    first = (source * CORES + core) * capacity
    column = lax.broadcasted_iota(jnp.int32, (half, slots), 1)

    def routed(group_core):
        expert = (group_row + group_core) * experts_here + local_expert
        mine = jnp.where(
            jnp.logical_and(small == expert.astype(jnp.float32), lane < topk), 1.0, 0.0
        )
        slot = jnp.sum(pltpu.roll(mine, topk, 1) * small, axis=1, keepdims=True)
        weight = jnp.sum(pltpu.roll(mine, 2 * topk, 1) * small, axis=1, keepdims=True)
        chosen = jnp.sum(mine, axis=1, keepdims=True)
        hit = jnp.logical_and(first + slot.astype(jnp.int32) == column, chosen > 0.5)
        return mine, weight, jnp.where(hit, 1.0, 0.0).astype(jnp.bfloat16)

    def backward(routing, back_proj, both):
        mine, weight, one_hot = routing
        pre_gate, pre_up = [
            jnp.dot(
                one_hot,
                both[2 * width + at * SAVED_ROWS : 2 * width + at * SAVED_ROWS + slots],
                preferred_element_type=jnp.float32,
            )
            for at in range(2)
        ]
        grad_gate, grad_up, gate_piece = gradients(back_proj, weight, pre_gate, pre_up)
        return grad_gate, grad_up, mine * gate_piece

    def back(both):
        first = 2 * width + 2 * SAVED_ROWS
        blocks = [both[first + at : first + at + LANES] for at in range(0, width, LANES)]
        return across(rows, jnp.concatenate(blocks, axis=1))

    rows = arrived[:, :width]
    own, other = routed(core), routed(1 - core)
    grad_gate1, grad_up1, gates1 = backward(own, back(both1), both1)
    grad_gate2, grad_up2, gates2 = backward(other, back(both2), both2)
    grads = jnp.concatenate([grad_gate1, grad_up1, grad_gate2, grad_up2], axis=1)
    step = width // 4
    for at in range(0, width, step):
        weights = [b[first + at : first + at + step] for b in (both1, both2) for first in (0, width)]
        pieces = across(grads, jnp.concatenate(weights, axis=1))
        out[:, at : at + step] = pieces.astype(out.dtype)
    out[:, width:] = (gates1 + gates2).astype(out.dtype)


def final_kernel(pieces, grad_rows, grad_gate, rows, gates, sems):
    width, topk = rows.shape[1], gates.shape[1]

    def summed(cols):
        total = pieces[0, :, cols].astype(jnp.float32)
        for peer in range(1, pieces.shape[0]):
            total = total + pieces[peer, :, cols].astype(jnp.float32)
        return total

    copies = [
        pltpu.make_async_copy(gates, grad_gate, sems.at[0]),
        pltpu.make_async_copy(rows, grad_rows, sems.at[1]),
    ]
    gates[...] = summed(slice(width, width + LANES))[:, :topk]
    copies[0].start()
    rows[...] = summed(slice(0, width)).astype(rows.dtype)
    copies[1].start()
    for copy in copies:
        copy.wait()


def stay_in(space, *arrays):
    return [pltpu.with_memory_space_constraint(a, space) for a in arrays]


def swap_cores(array):
    return lax.ppermute(array, "core", [(0, 1), (1, 0)])


def flat(out_grad, routing_weight, expert_ids, slot_index, w_gate, w_up, w_down, pre_act):
    row_count = lax.axis_size("row")
    inner_count = lax.axis_size("inner")
    own, width = out_grad.shape
    topk = expert_ids.shape[1]
    peers = row_count * inner_count
    half = peers * own
    slots, hidden = pre_act.shape[1:]
    packed = width + LANES
    in_vmem = pl.BlockSpec(memory_space=pltpu.VMEM)
    in_hbm = pl.BlockSpec(memory_space=pltpu.HBM)
    bf16 = out_grad.dtype

    sent, both = pl.pallas_call(
        pack_kernel,
        out_shape=[
            jax.ShapeDtypeStruct((peers, own, packed), bf16),
            pltpu.VMEM((3 * width + 2 * SAVED_ROWS, hidden), bf16),
        ],
        in_specs=[in_hbm] * 8,
        out_specs=[in_vmem] * 2,
        scratch_shapes=[
            pltpu.VMEM((own, width), bf16),
            pltpu.VMEM((2, own, topk), expert_ids.dtype),
            pltpu.VMEM((own, topk), bf16),
            pltpu.VMEM(pre_act.shape, bf16),
            pltpu.VMEM((own, LANES), jnp.float32),
            pltpu.SemaphoreType.DMA((7 + width // LANES,)),
        ],
        compiler_params=pltpu.CompilerParams(vmem_limit_bytes=16 * 2**20),
        name="pack_rows",
    )(
        *stay_in(
            pltpu.HBM,
            *(out_grad, expert_ids, slot_index, routing_weight),
            *(w_gate, w_up, w_down, pre_act),
        )
    )
    both2 = swap_cores(both)
    arrived = exchange(sent, ("row", "inner"))
    arrived = jnp.swapaxes(arrived, 0, 1).reshape(half, packed)
    pieces = pl.pallas_call(
        functools.partial(expert_kernel, topk, slots),
        out_shape=jax.ShapeDtypeStruct((half, packed), bf16),
        in_specs=[in_vmem] * 3,
        out_specs=in_vmem,
        compiler_params=pltpu.CompilerParams(vmem_limit_bytes=16 * 2**20),
        cost_estimate=pl.CostEstimate(
            flops=12 * half * w_down.size,
            bytes_accessed=2 * (both.nbytes + arrived.nbytes),
            transcendentals=2 * half * hidden,
        ),
        name="expert_pieces",
    )(arrived, *stay_in(pltpu.VMEM, both, both2))
    pieces = jnp.swapaxes(pieces.reshape(own, peers, packed), 0, 1)
    returned = exchange(pieces, ("row", "inner"))
    return pl.pallas_call(
        final_kernel,
        out_shape=[
            jax.ShapeDtypeStruct((own, width), bf16),
            jax.ShapeDtypeStruct((own, topk), jnp.float32),
        ],
        in_specs=[in_vmem],
        out_specs=[in_hbm] * 2,
        scratch_shapes=[
            pltpu.VMEM((own, width), bf16),
            pltpu.VMEM((own, topk), jnp.float32),
            pltpu.SemaphoreType.DMA((2,)),
        ],
        compiler_params=pltpu.CompilerParams(vmem_limit_bytes=16 * 2**20),
        name="sum_pieces",
    )(returned)


def staged(out_grad, routing_weight, expert_ids, slot_index, w_gate, w_up, w_down, pre_act):
    group_count = lax.axis_size("group")
    inner_count = lax.axis_size("inner")
    own, width = out_grad.shape
    topk = expert_ids.shape[1]
    split_count, experts_here = sizes(group_count, inner_count)
    local_expert = lax.axis_index("inner") // split_count
    block = inner_count * own
    slots = pre_act.shape[1]
    capacity = slots // group_count
    high = -(-(capacity + 1) // 8) * 8

    payload = pack(out_grad, expert_ids, slot_index, routing_weight)
    sent = jnp.broadcast_to(payload[None], (inner_count,) + payload.shape)
    arrived = exchange(sent, "inner").reshape(block, payload.shape[1])
    rows = arrived[:, :width]
    small = arrived[:, width : width + 3 * topk].astype(jnp.float32)
    ids = small[:, :topk].astype(jnp.int32)
    slot = small[:, topk : 2 * topk].astype(jnp.int32)
    weight = small[:, 2 * topk :]
    selected = ids % experts_here == local_expert
    column = ids // experts_here * high + slot
    one_hot = jnp.logical_and(
        column[:, :, None] == jnp.arange(group_count * high, dtype=jnp.int32), selected[:, :, None]
    ).astype(jnp.float32)
    placement = jnp.sum(one_hot, axis=1).astype(jnp.bfloat16)
    send_weight = jnp.sum(one_hot * weight[:, :, None], axis=(0, 1)).reshape(group_count, 1, high)
    send_rows = lax.dot_general(
        placement, rows, (((0,), (0,)), ((), ())), preferred_element_type=jnp.float32
    ).reshape(group_count, high, width)
    last = jnp.arange(high) == high - 1
    weight_row = jnp.pad(send_weight, ((0, 0), (0, 0), (0, width - high)))
    send = jnp.where(last[None, :, None], weight_row, send_rows).astype(jnp.bfloat16)
    buffer = exchange(send, "group")

    buffer_weight = buffer[:, high - 1, :capacity].astype(jnp.float32).reshape(slots, 1)
    buffer_rows = buffer[:, :capacity].reshape(slots, width)
    back_proj = across(buffer_rows, w_down)
    grad_gate, grad_up, gate_piece = gradients(
        back_proj, buffer_weight, pre_act[0].astype(jnp.float32), pre_act[1].astype(jnp.float32)
    )
    pieces = (across(grad_gate, w_gate) + across(grad_up, w_up)).reshape(group_count, capacity, width)
    gate_row = jnp.pad(
        gate_piece.reshape(group_count, 1, capacity), ((0, 0), (0, 0), (0, width - capacity))
    )
    pieces = jnp.pad(pieces, ((0, 0), (0, high - capacity), (0, 0)))
    back = exchange(jnp.where(last[None, :, None], gate_row, pieces).astype(jnp.bfloat16), "group")

    owned = jnp.dot(
        placement, back.reshape(group_count * high, width), preferred_element_type=jnp.float32
    ).astype(jnp.bfloat16)
    gates = back[:, high - 1, :high].reshape(group_count * high).astype(jnp.float32)
    gate_rows = jnp.sum(one_hot * gates, axis=2)
    final = exchange(pack(owned, gate_rows).reshape(inner_count, own, -1), "inner")
    total = jnp.sum(final.astype(jnp.float32), axis=0)
    return total[:, :width].astype(jnp.bfloat16), total[:, width : width + topk]


def solution(mesh):
    if mesh.size <= 64:
        group_count, inner_count = mesh.devices.shape
        devices = mesh.devices.reshape(group_count // CORES, CORES, inner_count)
        mesh, axes, on_device = Mesh(devices, ("row", "core", "inner")), ("row", "core", "inner"), flat
    else:
        axes, on_device = ("group", "inner"), staged
    token, hidden = P(axes, None), P(None, axes)
    return jax.shard_map(
        on_device,
        mesh=mesh,
        in_specs=(token, token, token, token, hidden, hidden, token, P(None, None, axes)),
        out_specs=(token, token),
        check_vma=False,
    )
```
